32 devices in a mesh: img: 16 (over z, y, x), seq: 2 (over core).
Axes of the slice: x: 2, y: 2, z: 4, core: 2. Of those that a mesh axis runs over, the one named last changes fastest.
Arguments:
- inputs: bfloat16 [32, 320, 1024], P('img', 'seq'), may hold values from -6 to 6
- cotangent: bfloat16 [32, 320, 1024], P('img', 'seq'), may hold values from -6 to 6
- kept_counts: int32 [32], P('img'), may hold values from 200 to 256, as said below
- norm1_gain: bfloat16 [1024], P(('img', 'seq')), may hold values from 0.099609375 to 1.8984375
- norm1_bias: bfloat16 [1024], P(('img', 'seq')), may hold values from -4 to 4
- qkv_weight: bfloat16 [1024, 3072], P(('img', 'seq')), may hold values from -0.25 to 0.25
- qv_bias: bfloat16 [2048], P(('img', 'seq')), may hold values from -6 to 6
- proj_weight: bfloat16 [1024, 1024], P(('img', 'seq')), may hold values from -0.5 to 0.5
- proj_bias: bfloat16 [1024], P(('img', 'seq')), may hold values from -6 to 6
- norm2_gain: bfloat16 [1024], P(('img', 'seq')), may hold values from 0.099609375 to 1.8984375
- norm2_bias: bfloat16 [1024], P(('img', 'seq')), may hold values from -4 to 4
- fc1_weight: bfloat16 [1024, 4096], P(('img', 'seq')), may hold values from -0.1875 to 0.1875
- fc1_bias: bfloat16 [4096], P(('img', 'seq')), may hold values from -6 to 6
- fc2_weight: bfloat16 [4096, 1024], P(('img', 'seq')), may hold values from -0.1875 to 0.1875
- fc2_bias: bfloat16 [1024], P(('img', 'seq')), may hold values from -6 to 6
Outputs:
- outputs: bfloat16 [32, 320, 1024], P('img', 'seq')
- input_grad: float32 [32, 320, 1024], P('img', 'seq')
- norm1_gain_grad: float32 [1024], P(('img', 'seq'))
- norm1_bias_grad: float32 [1024], P(('img', 'seq'))
- qkv_weight_grad: float32 [1024, 3072], P(('img', 'seq'))
- qv_bias_grad: float32 [2048], P(('img', 'seq'))
- proj_weight_grad: float32 [1024, 1024], P(('img', 'seq'))
- proj_bias_grad: float32 [1024], P(('img', 'seq'))
- norm2_gain_grad: float32 [1024], P(('img', 'seq'))
- norm2_bias_grad: float32 [1024], P(('img', 'seq'))
- fc1_weight_grad: float32 [1024, 4096], P(('img', 'seq'))
- fc1_bias_grad: float32 [4096], P(('img', 'seq'))
- fc2_weight_grad: float32 [4096, 1024], P(('img', 'seq'))
- fc2_bias_grad: float32 [1024], P(('img', 'seq'))
The draws below stay inside these ranges and needn't reach their ends.
Inputs may be any that keep to these rules, and one draw needn't show every extreme that they name: `kept_counts`: kept tokens of each image; some image has exactly 256 and some exactly 200.
All inputs are finite; a program needn't handle non-finite values.
Results may differ from the reference program's by a relative error of at most 0.015.
Values may be sent and summed in bfloat16 or wider, within the bound.
No kernel may reach another device: no remote copies, remote signals or barrier semaphores. Data moves between devices by JAX's collectives and lax.ppermute only.
A program may use at most 256 MiB of HBM per device.

```python
import jax
import jax.numpy as jnp
from jax import lax

D = 1024
FF = 4096
HEADS = 16
HEAD_DIM = 64
SLOTS = 320
BUFFER = 64
KEEP_MIN = 200
KEEP_MAX = 256
IMAGES = 32


def draw_kept_counts(key, part):
    key = jax.random.fold_in(key, 7)
    first_key, second_key = jax.random.split(key)
    counts = jax.random.randint(first_key, (IMAGES,), KEEP_MIN, KEEP_MAX + 1).astype(jnp.int32)
    places = jax.random.permutation(second_key, IMAGES)
    counts = counts.at[places[0]].set(KEEP_MAX)
    counts = counts.at[places[1]].set(KEEP_MIN)
    return counts


def block_levels(rng, extent, cuts, least, top_value):
    factor_of = 1.0
    for position, blocks in cuts:
        draws = jax.random.uniform(jax.random.fold_in(jax.random.fold_in(rng, 6), position), (blocks,), jnp.float32, least / len(cuts), top_value / len(cuts))
        factor_of = factor_of * jnp.repeat(jnp.exp(draws), extent[position] // blocks).reshape((-1,) + (1,) * (len(extent) - 1 - position))
    return factor_of


def scatter_about(stream_key, extent, width, limit, cuts=(), kind=jnp.bfloat16):
    values = jax.random.normal(stream_key, extent, jnp.float32) * width
    if len(cuts) > 0:
        values = block_levels(stream_key, extent, cuts, -0.22, 0.18) * values
    return jnp.clip(values, min=-limit, max=limit).astype(kind)


def setup_inputs(seed: int = 0) -> dict:
    key_list = jax.random.split(jax.random.key(seed), 16)
    return {
        "inputs": scatter_about(key_list[0], (IMAGES, SLOTS, D), 1.0, 6.0, ((0, 16), (1, 2))),
        "cotangent": scatter_about(key_list[1], (IMAGES, SLOTS, D), 1.0, 6.0, ((0, 16), (1, 2))),
        "kept_counts": draw_kept_counts(jax.random.fold_in(key_list[15], 71), 0),
        "norm1_gain": jnp.clip(1.0 + 0.18 * jax.random.normal(key_list[3], (D,), jnp.float32), 0.099609375, 1.8984375).astype(jnp.bfloat16),
        "norm1_bias": scatter_about(key_list[4], (D,), 0.3, 4.0, ((0, 32),)),
        "qkv_weight": scatter_about(key_list[5], (D, 3 * D), (D // 2) ** -0.5, 0.25, ((0, 32),)),
        "qv_bias": scatter_about(key_list[6], (2 * D,), 0.5, 6.0, ((0, 32),)),
        "proj_weight": scatter_about(key_list[7], (D, D), (D // 8) ** -0.5, 0.5, ((0, 32),)),
        "proj_bias": scatter_about(key_list[8], (D,), 0.5, 6.0, ((0, 32),)),
        "norm2_gain": jnp.clip(1.0 + 0.18 * jax.random.normal(key_list[9], (D,), jnp.float32), 0.099609375, 1.8984375).astype(jnp.bfloat16),
        "norm2_bias": scatter_about(key_list[10], (D,), 0.3, 4.0, ((0, 32),)),
        "fc1_weight": scatter_about(key_list[11], (D, FF), D ** -0.5, 0.1875, ((0, 32),)),
        "fc1_bias": scatter_about(key_list[12], (FF,), 0.5, 6.0, ((0, 32),)),
        "fc2_weight": scatter_about(key_list[13], (FF, D), (FF // 4) ** -0.5, 0.1875, ((0, 32),)),
        "fc2_bias": scatter_about(key_list[14], (D,), 0.5, 6.0, ((0, 32),)),
    }


@jax.custom_vjp
def low(v):
    return lax.optimization_barrier(v.astype(jnp.bfloat16)).astype(jnp.float32)

@jax.custom_vjp
def low_back(v):
    return v

def low_keep(v):
    return (low(v), None)

def low_pass(kept, grad):
    return (grad,)

def back_keep(v):
    return (v, None)

def back_low(kept, grad):
    return (low(grad),)
low.defvjp(low_keep, low_pass)
low_back.defvjp(back_keep, back_low)
HIGH = lax.Precision.HIGHEST

def layer_norm(values, gain, shift):
    centre = values - lax.optimization_barrier(jnp.mean(values, axis=-1, keepdims=True))
    spread = lax.optimization_barrier(jnp.mean(centre * centre, axis=-1, keepdims=True))
    return centre * lax.rsqrt(spread + 1e-06) * gain + shift

def image_forward(image, count, params):
    gain_one, shift_one, w_qkv, b_qv, w_proj, b_proj, gain_two, shift_two, w_fc1, b_fc1, w_fc2, b_fc2 = params
    slot_ids = jnp.arange(SLOTS, dtype=jnp.int32)
    living = slot_ids < BUFFER + count
    first = low(layer_norm(image, gain_one, shift_one))
    mixed = jnp.dot(first, w_qkv, precision=HIGH)
    queries = low_back(low(mixed[:, :D] + b_qv[:D]))
    keys = low_back(low(mixed[:, D:2 * D]))
    values = low_back(low(mixed[:, 2 * D:] + b_qv[D:]))
    scale = HEAD_DIM ** (-0.5)
    raw = jnp.einsum('qhd,khd->hqk', queries.reshape(SLOTS, HEADS, HEAD_DIM), keys.reshape(SLOTS, HEADS, HEAD_DIM), precision=HIGH) * scale
    scores = low_back(jnp.where(living[None, None, :], raw, -1e+30))
    top = lax.optimization_barrier(jnp.max(scores, axis=-1, keepdims=True))
    expo = jnp.exp(scores - top)
    probs = low(expo / lax.optimization_barrier(jnp.sum(expo, axis=-1, keepdims=True)))
    attended = jnp.einsum('hqk,khd->qhd', probs, values.reshape(SLOTS, HEADS, HEAD_DIM), precision=HIGH).reshape(SLOTS, D)
    attended = low_back(low(attended))
    branch = low_back(jnp.dot(attended, w_proj, precision=HIGH) + b_proj)
    middle = image + branch
    second = low(layer_norm(middle, gain_two, shift_two))
    hidden_pre = low_back(jnp.dot(second, w_fc1, precision=HIGH) + b_fc1)
    activated = low(jax.nn.gelu(hidden_pre, approximate=False))
    result = middle + jnp.dot(activated, w_fc2, precision=HIGH) + b_fc2
    return jnp.where(living[:, None], result, 0.0)

def reference(inputs, cotangent, kept_counts, norm1_gain, norm1_bias, qkv_weight, qv_bias, proj_weight, proj_bias, norm2_gain, norm2_bias, fc1_weight, fc1_bias, fc2_weight, fc2_bias):
    params = tuple((item.astype(jnp.float32) for item in (norm1_gain, norm1_bias, qkv_weight, qv_bias, proj_weight, proj_bias, norm2_gain, norm2_bias, fc1_weight, fc1_bias, fc2_weight, fc2_bias)))
    group = 8 if IMAGES % 8 == 0 else 2
    count_groups = kept_counts.reshape(IMAGES // group, group)

    def forward(images, weights):

        def run_group(carry, pieces):
            block, counts = pieces
            outs = jax.vmap(lambda image, count: image_forward(image, count, weights))(block, counts)
            return (carry, outs)
        blocks = images.reshape(IMAGES // group, group, SLOTS, D)
        _, outs = lax.scan(jax.checkpoint(run_group), jnp.zeros((), jnp.float32), (blocks, count_groups))
        return outs.reshape(IMAGES, SLOTS, D)
    result, back = jax.vjp(forward, inputs.astype(jnp.float32), params)
    d_in, grads = back(cotangent.astype(jnp.float32))
    return (result.astype(jnp.bfloat16), d_in, grads[0], grads[1], grads[2], grads[3], grads[4], grads[5], grads[6], grads[7], grads[8], grads[9], grads[10], grads[11])
```

```python
import jax
import jax.numpy as jnp
import numpy as np
from jax import lax
from jax.experimental import pallas as pl
from jax.experimental.pallas import tpu as pltpu
from jax.sharding import PartitionSpec as P

HEAD_DIM = 64
BUFFER = 64
PAIR = 2
f32 = jnp.float32
b16 = jnp.bfloat16
HIGH = lax.Precision.HIGHEST


def dot(left, right):
    return jnp.dot(left, right, preferred_element_type=f32)


def dot_tn(left, right):
    return lax.dot_general(left, right, (((0,), (0,)), ((), ())), preferred_element_type=f32)


def dot_nt(left, right):
    return lax.dot_general(left, right, (((1,), (1,)), ((), ())), preferred_element_type=f32)


def norm_parts(values):
    centre = values - jnp.mean(values, axis=-1, keepdims=True)
    scale = lax.rsqrt(jnp.mean(centre * centre, axis=-1, keepdims=True) + 1e-06)
    return centre * scale, scale


def norm_back(grad, normed, scale, gain):
    e = grad * gain
    return scale * (
        e
        - jnp.mean(e, axis=-1, keepdims=True)
        - normed * jnp.mean(e * normed, axis=-1, keepdims=True)
    )


def core_swap(value):
    return lax.ppermute(value, "seq", [(0, 1), (1, 0)])


def bit_swap(value, bits):
    n = lax.axis_size("img")
    pairs = [
        (2 * j + c, 2 * (j ^ (1 << bits[c])) + c) for j in range(n) for c in range(2)
    ]
    return lax.ppermute(value, ("img", "seq"), pairs)


def after(value, *others):
    return lax.optimization_barrier((value, *others))[0]


class Gather:
    def __init__(self, block, orders):
        self.held = block[None]
        self.steps = list(zip(*orders))

    def step(self, *others):
        held = after(self.held, *others) if others else self.held
        got = bit_swap(held, self.steps.pop(0))
        self.held = jnp.concatenate([held, got], axis=0)
        return got


def scatter(send, keep, orders):
    steps = list(zip(*orders))[::-1]
    for k, bits in enumerate(steps):
        got = bit_swap(send, bits)
        total = keep.astype(f32) + got.astype(f32)
        if k + 1 == len(steps):
            return total[0]
        cut = total.shape[0] // 2
        send, keep = total[cut:].astype(send.dtype), total[:cut]


def spread(position, order):
    return sum((((position >> k) & 1) << bit) for k, bit in enumerate(order))


def onehot(left, right):
    return (left[:, None] == right[None, :]).astype(b16)


class Places:
    def __init__(self, n, width, units, full, most):
        rows, half, few = width // (2 * n), width // 2, n // 2
        place, chips = np.arange(width), np.arange(few)
        col = np.arange(few * units)
        names = ("qkv", "fc1", "proj", "heads", "units", "chips", "owners")
        found = {name: [] for name in names}
        for me in range(n):
            for core in range(2):
                chip = me ^ spread(place // (2 * rows), full[core])
                found["qkv"].append((2 * chip + (core ^ (place // rows % 2))) * rows + place % rows)
                chip = me ^ spread(place // (4 * rows), most[core])
                chip = chip ^ ((place // (2 * rows) % 2) << PAIR)
                found["fc1"].append((2 * chip + (core ^ (place // rows % 2))) * rows + place % rows)
                source = core ^ (place // half)
                chip = me ^ np.where(
                    source == 0,
                    spread(place // rows % n, full[0]),
                    spread(place // rows % n, full[1]),
                )
                found["proj"].append((2 * chip + source) * rows + place % rows)
                found["heads"].append(source * half + place % half)
                short = lambda chip: (chip >> (PAIR + 1) << PAIR) + chip % (1 << PAIR)
                owner = me ^ spread(chips, most[core])
                found["units"].append(short(owner)[col // units] * units + col % units)
                side = (me >> PAIR) & 1
                low = 1 << PAIR
                found["owners"].append(chips // low * 2 * low + side * low + chips % low)
                found["chips"].append(me ^ spread(np.arange(n), full[core]))
        for name in names:
            setattr(self, name, np.stack(found[name]).astype(np.int32))


def live_slots(meta_ref, image, local, axis):
    shape = (2 * local, 1) if axis == 0 else (1, 2 * local)
    place = lax.broadcasted_iota(jnp.int32, shape, axis)
    core = meta_ref[0]
    own = place < local
    slot = jnp.where(own, place + core * local, place - core * local)
    return slot < BUFFER + meta_ref[1 + image]


def attend_kernel(meta_ref, q_ref, k_ref, v_ref, o_ref):
    local = q_ref.shape[2]
    slots = 2 * local
    live = live_slots(meta_ref, pl.program_id(0), local, 1)
    q, k, v = (r[...].reshape(slots, 2 * HEAD_DIM) for r in (q_ref, k_ref, v_ref))
    outs = []
    for e in range(2):
        part = slice(e * HEAD_DIM, (e + 1) * HEAD_DIM)
        raw = dot_nt(q[:, part], k[:, part]) * (HEAD_DIM**-0.5)
        raw = jnp.where(live, raw, -1e30)
        expo = jnp.exp(raw - jnp.max(raw, axis=-1, keepdims=True))
        probs = expo * (1.0 / jnp.sum(expo, axis=-1, keepdims=True))
        outs.append(dot(probs.astype(b16), v[:, part]))
    o_ref[...] = jnp.concatenate(outs, axis=1).astype(b16).reshape(o_ref.shape)


def attend_back_kernel(meta_ref, q_ref, k_ref, v_ref, g_ref, o_ref):
    local = q_ref.shape[2]
    slots = 2 * local
    blocks = o_ref.shape[3] // (3 * 2 * HEAD_DIM)
    live = live_slots(meta_ref, pl.program_id(0), local, 0)
    q, k, v, g = (r[...].reshape(slots, 2 * HEAD_DIM) for r in (q_ref, k_ref, v_ref, g_ref))
    scale = HEAD_DIM**-0.5
    parts = ([], [], [])
    for e in range(2):
        part = slice(e * HEAD_DIM, (e + 1) * HEAD_DIM)
        qe, ke, ve, ge = q[:, part], k[:, part], v[:, part], g[:, part]
        raw = jnp.where(live, dot_nt(ke, qe) * scale, -1e30)
        expo = jnp.exp(raw - jnp.max(raw, axis=0, keepdims=True))
        probs = expo * (1.0 / jnp.sum(expo, axis=0, keepdims=True))
        d_probs = dot_nt(ve, ge)
        inner = jnp.sum(probs * d_probs, axis=0, keepdims=True)
        d_scores = (probs * (d_probs - inner)).astype(b16)
        parts[0].append(dot_tn(d_scores, ke) * scale)
        parts[1].append(dot(d_scores, qe) * scale)
        parts[2].append(dot(probs.astype(b16), ge))
    for which in range(3):
        at = pl.multiple_of((which * blocks + pl.program_id(1)) * 2 * HEAD_DIM, 2 * HEAD_DIM)
        value = jnp.concatenate(parts[which], axis=1).astype(b16)
        o_ref[:, :, :, pl.ds(at, 2 * HEAD_DIM)] = value.reshape(2, 1, local, 2 * HEAD_DIM)


def attention(mixed, meta):
    _, images, local, wide = mixed.shape
    block = (2, 1, local, 2 * HEAD_DIM)
    blocks = wide // (3 * 2 * HEAD_DIM)
    spec = lambda first: pl.BlockSpec(block, lambda i, h, m, f=first: (0, i, 0, f + h))
    flops = 2 * images * blocks * 2 * 2 * (2 * local) ** 2 * HEAD_DIM
    return pl.pallas_call(
        attend_kernel,
        out_shape=jax.ShapeDtypeStruct((2, images, local, wide // 3), b16),
        grid_spec=pltpu.PrefetchScalarGridSpec(
            num_scalar_prefetch=1,
            grid=(images, blocks),
            in_specs=[spec(0), spec(blocks), spec(2 * blocks)],
            out_specs=spec(0),
        ),
        cost_estimate=pl.CostEstimate(
            flops=4 * flops, bytes_accessed=mixed.size * 3, transcendentals=0
        ),
    )(meta, mixed, mixed, mixed)


def attention_back(mixed, grad, meta):
    _, images, local, wide = mixed.shape
    block = (2, 1, local, 2 * HEAD_DIM)
    blocks = wide // (3 * 2 * HEAD_DIM)
    spec = lambda first: pl.BlockSpec(block, lambda i, h, m, f=first: (0, i, 0, f + h))
    flops = 2 * images * blocks * 2 * 5 * (2 * local) ** 2 * HEAD_DIM
    return pl.pallas_call(
        attend_back_kernel,
        out_shape=jax.ShapeDtypeStruct(mixed.shape, b16),
        grid_spec=pltpu.PrefetchScalarGridSpec(
            num_scalar_prefetch=1,
            grid=(images, blocks),
            in_specs=[spec(0), spec(blocks), spec(2 * blocks), spec(0)],
            out_specs=pl.BlockSpec((2, 1, local, wide), lambda i, h, m: (0, i, 0, 0)),
        ),
        cost_estimate=pl.CostEstimate(
            flops=4 * flops, bytes_accessed=mixed.size * 5, transcendentals=0
        ),
    )(meta, mixed, mixed, mixed, grad)


def body(
    inputs,
    cotangent,
    kept_counts,
    norm1_gain,
    norm1_bias,
    qkv_weight,
    qv_bias,
    proj_weight,
    proj_bias,
    norm2_gain,
    norm2_bias,
    fc1_weight,
    fc1_bias,
    fc2_weight,
    fc2_bias,
):
    images, local, width = inputs.shape
    n = lax.axis_size("img")
    me = lax.axis_index("img")
    core = lax.axis_index("seq")
    levels = n.bit_length() - 1
    half = width // 2
    rows = width // (2 * n)
    units = fc2_weight.shape[0]
    few = n // 2
    hidden = units * few
    tok = images * local
    low = 1 << PAIR
    side = (me >> PAIR) & 1

    full = tuple(tuple(range(levels - 1, 1, -1)) + last for last in ((0, 1), (1, 0)))
    most = tuple(
        (first,) + tuple(b for b in range(levels - 1, 1, -1) if b != PAIR) + (1 - first,)
        for first in (0, 1)
    )

    table = Places(n, width, units, full, most)
    dev = 2 * me + core
    pick = lambda rows_of: lax.dynamic_index_in_dim(jnp.asarray(rows_of), dev, 0, False)
    abs_rows = lax.iota(jnp.int32, width)
    qkv_perm = onehot(abs_rows, pick(table.qkv))
    fc1_perm = onehot(abs_rows, pick(table.fc1))
    proj_perm = onehot(pick(table.heads), pick(table.proj))
    col_perm = onehot(lax.iota(jnp.int32, hidden), pick(table.units))
    chip_perm = onehot(lax.iota(jnp.int32, n), pick(table.chips))
    unit_perm = onehot(pick(table.owners), lax.iota(jnp.int32, n))

    mine_of = lambda a, axis: lax.dynamic_index_in_dim(a, core, axis, False)
    theirs_of = lambda a, axis: lax.dynamic_index_in_dim(a, 1 - core, axis, False)
    smalls = (norm1_gain, norm1_bias, qv_bias, proj_bias, norm2_gain, norm2_bias, fc1_bias, fc2_bias)
    ends = [0]
    for item in smalls:
        ends.append(ends[-1] + item.shape[0])
    pair = (PAIR, PAIR)
    qkv_cut = qkv_weight.reshape(rows, 3, 2, half)
    qkv_got = core_swap(theirs_of(qkv_cut, 2))
    qkv_block = jnp.concatenate([mine_of(qkv_cut, 2), qkv_got], axis=0)
    qkv = Gather(qkv_block.reshape(2 * rows, 3 * half), full)
    x_own = inputs.reshape(tok, width)
    x_all = jnp.concatenate([x_own, core_swap(x_own)], axis=0).astype(f32)
    qkv_1 = qkv.step()

    fc1_cut = fc1_weight.reshape(rows, few // low, 2, low, 2, units)
    fc1_got = core_swap(after(theirs_of(fc1_cut, 4), qkv_got))
    fc1_block = jnp.stack([mine_of(fc1_cut, 4), fc1_got])
    side_of = lambda which: lax.dynamic_index_in_dim(fc1_block, which, 3, False)
    fc1_block = jnp.stack([side_of(side), bit_swap(side_of(1 - side), pair)])
    fc1 = Gather(fc1_block.reshape(4 * rows, hidden), most)
    fc2 = Gather(after(fc2_weight, qkv_got), most)
    fc2.step()

    small_own = jnp.concatenate([after(a, qkv_got) for a in smalls])
    small_other = core_swap(small_own)
    small = jnp.where(
        core == 0, jnp.stack([small_own, small_other]), jnp.stack([small_other, small_own])
    )
    small = Gather(small, full)
    small.step(qkv_1)
    qkv_2 = qkv.step()
    fc1.step()
    for _ in full[0][1:]:
        small_done = small.step()
    small = small.held.reshape(n, -1)
    small = dot(chip_perm, small).reshape(n, 2, -1)
    gain_one, shift_one, b_qv, b_proj, gain_two, shift_two, b_fc1, b_fc2 = (
        small[:, :, a:b].reshape(-1) for a, b in zip(ends, ends[1:])
    )
    bias_fc1 = jnp.dot(
        unit_perm.astype(f32), mine_of(b_fc1.reshape(n, 2, units), 1), precision=HIGH
    ).reshape(-1)
    while len(qkv.steps) > 2:
        qkv_2 = qkv.step()
    qkv_3 = qkv.step()
    proj = Gather(after(proj_weight, qkv_2), full)
    while len(proj.steps) > 2:
        proj_2 = proj.step()
    while len(fc2.steps) > 1:
        fc2_2 = fc2.step(proj_2)
    qkv_4 = qkv.step()
    w_qkv = qkv.held.reshape(width, 3 * half)

    slot = jnp.tile(core * local + lax.iota(jnp.int32, local), images)
    row_live = (slot < BUFFER + jnp.repeat(kept_counts, local, total_repeat_length=tok))[:, None]

    def to_four(own):
        two = jnp.concatenate([own, bit_swap(own, pair)], axis=0)
        return jnp.concatenate([two, core_swap(two)], axis=0)

    def from_four(part):
        two = part[: 2 * tok] + core_swap(part[2 * tok :].astype(b16)).astype(f32)
        return two[:tok] + bit_swap(two[tok:].astype(b16), pair).astype(f32)

    up_low = jnp.where(row_live, cotangent.reshape(tok, width), 0).astype(b16)
    up_low = after(up_low, qkv_2)
    up_all = to_four(up_low)
    upstream = up_low.astype(f32)
    while len(fc1.steps) > 1:
        fc1_2 = fc1.step(fc2_2)
    proj.step(qkv_4)
    proj.step()
    w_proj = proj.held.reshape(half, width)
    w_proj = jnp.concatenate([w_proj, core_swap(w_proj)], axis=0)
    w_proj = dot(proj_perm, w_proj).astype(b16)
    fc2_3 = fc2.step(qkv_4)
    w_fc2 = fc2.held.reshape(hidden, width)
    w_fc2 = dot(col_perm, w_fc2).astype(b16)
    fc1.step(fc2_3)
    w_fc1 = fc1.held.reshape(width, hidden)
    w_fc1 = dot(fc1_perm, w_fc1).astype(b16)

    meta = jnp.concatenate([core[None].astype(jnp.int32), kept_counts])
    normed_all, scale_all = norm_parts(x_all)
    first = (normed_all * gain_one + shift_one).astype(b16)
    normed_one, scale_one = normed_all[:tok], scale_all[:tok]
    first = dot(first, qkv_perm).astype(b16)
    qv_cut = mine_of(b_qv.reshape(2, 2, half), 1)
    bias_qkv = jnp.concatenate([qv_cut[0], jnp.zeros((half,), f32), qv_cut[1]])
    mixed = (dot(first, w_qkv) + bias_qkv).astype(b16).reshape(2, images, local, 3 * half)
    attended = attention(mixed, meta).reshape(2, tok, half)
    attended = jnp.concatenate([attended[0], core_swap(attended[1])], axis=1)

    middle = x_own.astype(f32) + dot(attended, w_proj) + b_proj
    normed_two, scale_two = norm_parts(middle)
    second = to_four((normed_two * gain_two + shift_two).astype(b16))
    pre = dot(second, w_fc1) + bias_fc1
    phi = 0.5 * (1.0 + lax.erf(pre * (0.5**0.5)))
    activated = (pre * phi).astype(b16)
    slope = (phi + pre * jnp.exp(-0.5 * pre * pre) * 0.3989422804014327).astype(b16)

    parts = lambda a: a.reshape(-1, rows, a.shape[-1])
    cut = hidden // 2
    activated_rel = dot(activated, col_perm).astype(b16)
    grad_fc2 = scatter(
        dot_tn(activated_rel[:, cut:], up_all).astype(b16).reshape(-1, units, width),
        dot_tn(activated_rel[:, :cut], up_all).reshape(-1, units, width),
        most,
    )
    d_pre = (slope.astype(f32) * dot_nt(up_all, w_fc2)).astype(b16)
    second_rel = dot(second, fc1_perm).astype(b16)
    grad_fc1 = scatter(
        dot_tn(second_rel[:, half:], d_pre).astype(b16).reshape(-1, 4 * rows, hidden),
        dot_tn(second_rel[:, :half], d_pre).reshape(-1, 4 * rows, hidden),
        most,
    )
    outputs = middle + from_four(dot(activated, w_fc2)) + b_fc2
    outputs = jnp.where(row_live, outputs, 0.0).astype(b16).reshape(inputs.shape)

    d_second = from_four(dot_nt(d_pre, w_fc1))
    d_middle = upstream + norm_back(d_second, normed_two, scale_two, gain_two)
    d_branch = d_middle.astype(b16)
    d_attended = dot_nt(d_branch, w_proj).astype(b16)
    d_attended = jnp.stack([d_attended[:, :half], core_swap(d_attended[:, half:])])
    d_mixed = attention_back(mixed, d_attended.reshape(2, images, local, half), meta)
    d_mixed = d_mixed.reshape(2 * tok, 3 * half)

    attended_rel = dot(attended, proj_perm).astype(b16)
    attended_rel = jnp.concatenate([attended_rel[:, :half], core_swap(attended_rel[:, half:])], axis=0)
    branch_all = jnp.concatenate([d_branch, core_swap(d_branch)], axis=0)
    grad_proj = scatter(
        parts(dot_tn(attended_rel[:, half // 2 :], branch_all).astype(b16)),
        parts(dot_tn(attended_rel[:, : half // 2], branch_all)),
        full,
    )
    grad_qkv = scatter(
        dot_tn(first[:, half:], d_mixed).astype(b16).reshape(-1, 2 * rows, 3 * half),
        dot_tn(first[:, :half], d_mixed).reshape(-1, 2 * rows, 3 * half),
        full,
    )
    d_first = dot_nt(dot_nt(d_mixed, w_qkv).astype(b16), qkv_perm).astype(b16)
    d_first = d_first[:tok].astype(f32) + core_swap(d_first[tok:]).astype(f32)
    input_grad = d_middle + norm_back(d_first, normed_one, scale_one, gain_one)
    input_grad = input_grad.reshape(inputs.shape)

    placed = lambda a, axis: jnp.stack(
        [jnp.where(core == 0, a, 0.0), jnp.where(core == 1, a, 0.0)], axis=axis
    )
    total = lambda a: jnp.sum(a.astype(f32), axis=0)
    d_mixed_sum = total(d_mixed).reshape(3, half)
    d_pre_sum = jnp.dot(
        unit_perm.astype(f32).T, total(d_pre).reshape(few, units), precision=HIGH
    )
    small_grads = (
        total(d_first * normed_one),
        total(d_first),
        placed(d_mixed_sum[::2], 1),
        total(d_branch),
        total(d_second * normed_two),
        total(d_second),
        placed(d_pre_sum, 1),
        total(upstream),
    )
    small_grads = jnp.concatenate([g.reshape(n, 2, -1) for g in small_grads], axis=2)
    small_grads = mine_of(small_grads, 1) + core_swap(theirs_of(small_grads, 1))
    small_grads = jnp.dot(chip_perm.astype(f32).T, small_grads, precision=HIGH)
    small_grads = small_grads[:, None]
    small_grads = scatter(small_grads[few:], small_grads[:few], full)[0]
    small_grads = [small_grads[a:b] for a, b in zip(ends, ends[1:])]

    qkv_other = core_swap(grad_qkv[rows:])
    both = lambda own, other, which, axis: jnp.where(
        which == 0, jnp.stack([own, other], axis=axis), jnp.stack([other, own], axis=axis)
    )
    cut3 = lambda a: a.reshape(rows, 3, half)
    grad_qkv = both(cut3(grad_qkv[:rows]), cut3(qkv_other), core, 2).reshape(qkv_weight.shape)

    pair_other = bit_swap(grad_fc1[2 * rows :], pair)
    cut4 = lambda a: a.reshape(2 * rows, few // low, low, units)
    grad_fc1 = both(cut4(grad_fc1[: 2 * rows]), cut4(pair_other), side, 2)
    core_other = core_swap(grad_fc1[rows:])
    grad_fc1 = both(grad_fc1[:rows], core_other, core, 4).reshape(fc1_weight.shape)
    return (
        outputs,
        input_grad,
        small_grads[0],
        small_grads[1],
        grad_qkv,
        small_grads[2],
        grad_proj,
        small_grads[3],
        small_grads[4],
        small_grads[5],
        grad_fc1,
        small_grads[6],
        grad_fc2,
        small_grads[7],
    )


def solution(mesh):
    row = P(("img", "seq"))
    mat = P(("img", "seq"), None)
    act = P("img", "seq", None)
    return jax.shard_map(
        body,
        mesh=mesh,
        in_specs=(act, act, P("img"), row, row, mat, row, mat, row, row, row, mat, row, mat, row),
        out_specs=(act, act, row, row, mat, row, mat, row, row, row, mat, row, mat, row),
        check_vma=False,
    )
```

```python
import functools

import jax
import jax.numpy as jnp
import numpy as np
from jax import lax
from jax.experimental import pallas as pl
from jax.experimental.pallas import tpu as pltpu
from jax.sharding import PartitionSpec as P

HEAD_DIM = 64
BUFFER = 64
PAIR = 2
f32 = jnp.float32
b16 = jnp.bfloat16
HIGH = lax.Precision.HIGHEST


def dot(left, right):
    return jnp.dot(left, right, preferred_element_type=f32)


def dot_tn(left, right):
    return lax.dot_general(left, right, (((0,), (0,)), ((), ())), preferred_element_type=f32)


def dot_nt(left, right):
    return lax.dot_general(left, right, (((1,), (1,)), ((), ())), preferred_element_type=f32)


def norm_parts(values):
    centre = values - jnp.mean(values, axis=-1, keepdims=True)
    scale = lax.rsqrt(jnp.mean(centre * centre, axis=-1, keepdims=True) + 1e-06)
    return centre * scale, scale


def norm_back(grad, normed, scale, gain):
    e = grad * gain
    return scale * (
        e
        - jnp.mean(e, axis=-1, keepdims=True)
        - normed * jnp.mean(e * normed, axis=-1, keepdims=True)
    )


def core_swap(value):
    return lax.ppermute(value, "seq", [(0, 1), (1, 0)])


def bit_swap(value, bits):
    n = lax.axis_size("img")
    pairs = [
        (2 * j + c, 2 * (j ^ (1 << bits[c])) + c) for j in range(n) for c in range(2)
    ]
    return lax.ppermute(value, ("img", "seq"), pairs)


def after(value, *others):
    return lax.optimization_barrier((value, *others))[0]


class Gather:
    def __init__(self, block, orders):
        self.held = None if block is None else block[None]
        self.steps = list(zip(*orders))

    def step(self, *others):
        self.sent = after(self.held, *others) if others else self.held
        self.got = bit_swap(self.sent, self.steps.pop(0))
        self.held = jnp.concatenate([self.sent, self.got], axis=0)
        return self.got


class Scatter:
    def __init__(self, send, keep, orders):
        self.send, self.keep = send, keep
        self.steps = list(zip(*orders))[::-1]

    def step(self, *others):
        send = after(self.send, *others) if others else self.send
        self.got = bit_swap(send, self.steps.pop(0))
        total = self.keep + self.got.astype(f32)
        cut = total.shape[0] // 2
        if cut:
            self.send = total[cut:].astype(send.dtype)
        self.keep = total[: max(cut, 1)]


def spread(position, order):
    return sum((((position >> k) & 1) << bit) for k, bit in enumerate(order))


def onehot(left, right):
    return (left[:, None] == right[None, :]).astype(b16)


class Places:
    def __init__(self, n, width, units, full, most):
        rows, half, few = width // (2 * n), width // 2, n // 2
        place, chips = np.arange(width), np.arange(few)
        col = np.arange(few * units)
        names = ("qkv", "fc1", "proj", "heads", "units", "chips", "owners")
        found = {name: [] for name in names}
        for me in range(n):
            for core in range(2):
                chip = me ^ spread(place // (2 * rows), full[core])
                found["qkv"].append((2 * chip + (core ^ (place // rows % 2))) * rows + place % rows)
                chip = me ^ spread(place // (4 * rows), most[core])
                chip = chip ^ ((place // (2 * rows) % 2) << PAIR)
                found["fc1"].append((2 * chip + (core ^ (place // rows % 2))) * rows + place % rows)
                source = core ^ (place // half)
                chip = me ^ np.where(
                    source == 0,
                    spread(place // rows % n, full[0]),
                    spread(place // rows % n, full[1]),
                )
                found["proj"].append((2 * chip + source) * rows + place % rows)
                found["heads"].append(source * half + place % half)
                short = lambda chip: (chip >> (PAIR + 1) << PAIR) + chip % (1 << PAIR)
                owner = me ^ spread(chips, most[core])
                found["units"].append(short(owner)[col // units] * units + col % units)
                side = (me >> PAIR) & 1
                low = 1 << PAIR
                found["owners"].append(chips // low * 2 * low + side * low + chips % low)
                found["chips"].append(me ^ spread(np.arange(n), full[core]))
        for name in names:
            setattr(self, name, np.stack(found[name]).astype(np.int32))


def live_slots(meta_ref, local, axis):
    shape = (2 * local, 1) if axis == 0 else (1, 2 * local)
    place = lax.broadcasted_iota(jnp.int32, shape, axis)
    core = meta_ref[0]
    slot = jnp.where(place < local, place + core * local, place - core * local)
    return slot < BUFFER + meta_ref[1]


def attend_kernel(meta_ref, q_ref, k_ref, v_ref, o_ref):
    live = live_slots(meta_ref, q_ref.shape[0] // 2, 1)
    outs = []
    for e in range(2):
        part = slice(e * HEAD_DIM, (e + 1) * HEAD_DIM)
        raw = dot_nt(q_ref[:, part], k_ref[:, part]) * (HEAD_DIM**-0.5)
        raw = jnp.where(live, raw, -1e30)
        expo = jnp.exp(raw - jnp.max(raw, axis=-1, keepdims=True))
        probs = expo * (1.0 / jnp.sum(expo, axis=-1, keepdims=True))
        outs.append(dot(probs.astype(b16), v_ref[:, part]))
    o_ref[...] = jnp.concatenate(outs, axis=1).astype(b16)


def attend_back_kernel(meta_ref, q_ref, k_ref, v_ref, g_ref, o_ref):
    pairs = o_ref.shape[1] // (3 * 2 * HEAD_DIM)
    live = live_slots(meta_ref, q_ref.shape[0] // 2, 0)
    scale = HEAD_DIM**-0.5
    parts = ([], [], [])
    for e in range(2):
        part = slice(e * HEAD_DIM, (e + 1) * HEAD_DIM)
        qe, ke, ve, ge = (r[:, part] for r in (q_ref, k_ref, v_ref, g_ref))
        raw = jnp.where(live, dot_nt(ke, qe) * scale, -1e30)
        expo = jnp.exp(raw - jnp.max(raw, axis=0, keepdims=True))
        probs = expo * (1.0 / jnp.sum(expo, axis=0, keepdims=True))
        d_probs = dot_nt(ve, ge)
        inner = jnp.sum(probs * d_probs, axis=0, keepdims=True)
        d_scores = (probs * (d_probs - inner)).astype(b16)
        parts[0].append(dot_tn(d_scores, ke) * scale)
        parts[1].append(dot(d_scores, qe) * scale)
        parts[2].append(dot(probs.astype(b16), ge))
    for which in range(3):
        at = pl.multiple_of((which * pairs + pl.program_id(0)) * 2 * HEAD_DIM, 2 * HEAD_DIM)
        o_ref[:, pl.ds(at, 2 * HEAD_DIM)] = jnp.concatenate(parts[which], axis=1).astype(b16)


def attention(mixed, meta, grad=None):
    slots, wide = mixed.shape
    pairs = wide // (3 * 2 * HEAD_DIM)
    block = (slots, 2 * HEAD_DIM)
    spec = lambda first: pl.BlockSpec(block, lambda h, m, f=first: (0, f + h))
    specs = [spec(0), spec(pairs), spec(2 * pairs)]
    dots = 2 * pairs * 2 * slots * slots * HEAD_DIM
    if grad is None:
        kernel, extra, out_wide, out_spec, count = attend_kernel, (), wide // 3, spec(0), 2
    else:
        kernel, extra, out_wide, count = attend_back_kernel, (grad,), wide, 5
        specs.append(spec(0))
        out_spec = pl.BlockSpec((slots, wide), lambda h, m: (0, 0))
    return pl.pallas_call(
        kernel,
        out_shape=jax.ShapeDtypeStruct((slots, out_wide), b16),
        grid_spec=pltpu.PrefetchScalarGridSpec(
            num_scalar_prefetch=1, grid=(pairs,), in_specs=specs, out_specs=out_spec
        ),
        cost_estimate=pl.CostEstimate(
            flops=4 * count * dots, bytes_accessed=4 * mixed.size, transcendentals=0
        ),
    )(meta, mixed, mixed, mixed, *extra)


def plain_body(
    inputs,
    cotangent,
    kept_counts,
    norm1_gain,
    norm1_bias,
    qkv_weight,
    qv_bias,
    proj_weight,
    proj_bias,
    norm2_gain,
    norm2_bias,
    fc1_weight,
    fc1_bias,
    fc2_weight,
    fc2_bias,
):
    images, local, width = inputs.shape
    n = lax.axis_size("img")
    me = lax.axis_index("img")
    core = lax.axis_index("seq")
    levels = n.bit_length() - 1
    half = width // 2
    rows = width // (2 * n)
    units = fc2_weight.shape[0]
    few = n // 2
    hidden = units * few
    low = 1 << PAIR
    side = (me >> PAIR) & 1

    full = tuple(tuple(range(levels - 1, 1, -1)) + last for last in ((0, 1), (1, 0)))
    most = tuple(
        (first,) + tuple(b for b in range(levels - 1, 1, -1) if b != PAIR) + (1 - first,)
        for first in (0, 1)
    )

    table = Places(n, width, units, full, most)
    dev = 2 * me + core
    pick = lambda rows_of: lax.dynamic_index_in_dim(jnp.asarray(rows_of), dev, 0, False)

    mine_of = lambda a, axis: lax.dynamic_index_in_dim(a, core, axis, False)
    theirs_of = lambda a, axis: lax.dynamic_index_in_dim(a, 1 - core, axis, False)
    smalls = (norm1_gain, norm1_bias, qv_bias, proj_bias, norm2_gain, norm2_bias, fc1_bias, fc2_bias)
    ends = [0]
    for item in smalls:
        ends.append(ends[-1] + item.shape[0])
    pair = (PAIR, PAIR)
    qkv_cut = qkv_weight.reshape(rows, 3, 2, half)
    qkv_got = core_swap(theirs_of(qkv_cut, 2))
    qkv_block = jnp.concatenate([mine_of(qkv_cut, 2), qkv_got], axis=0)
    qkv = Gather(qkv_block.reshape(2 * rows, 3 * half), full)
    x_other = core_swap(inputs)
    q_got = [qkv.step()]

    small_own = jnp.concatenate(smalls)
    small_other = core_swap(small_own)
    small = jnp.where(
        core == 0, jnp.stack([small_own, small_other]), jnp.stack([small_other, small_own])
    )
    small = Gather(small, full)
    small.step(qkv_got)

    fc1_cut = after(fc1_weight, qkv_got).reshape(rows, few // low, 2, low, 2, units)
    fc1_got = core_swap(theirs_of(fc1_cut, 4))
    fc1_block = jnp.stack([mine_of(fc1_cut, 4), fc1_got])
    side_of = lambda which: lax.dynamic_index_in_dim(fc1_block, which, 3, False)
    fc1_block = jnp.stack([side_of(side), bit_swap(side_of(1 - side), pair)])
    fc1 = Gather(fc1_block.reshape(4 * rows, hidden), most)
    fc2 = Gather(fc2_weight, most)

    q_got.append(qkv.step())
    small.step(q_got[0])
    fc2_got = fc2.step(q_got[0])
    while len(qkv.steps) > 2:
        q_got.append(qkv.step())
        small.step(q_got[-2])
    qkv.step()
    q_got.append(qkv.got)
    small.step(q_got[-2])
    proj = Gather(proj_weight, full)
    proj_got = proj.step(q_got[-2])
    fc1_first = fc1.step(fc2_got)
    qkv.step()
    q_got.append(qkv.got)
    small.step(q_got[-2])
    while len(proj.steps) > 2:
        proj_got = proj.step(q_got[-2])
    slot = core * local + lax.iota(jnp.int32, local)
    row_live = [(slot < BUFFER + kept_counts[i])[:, None] for i in range(images)]

    def to_four(own, *others):
        two = jnp.concatenate([own, bit_swap(after(own, *others), pair)], axis=0)
        return jnp.concatenate([two, core_swap(two)], axis=0)

    cotangent = after(cotangent, q_got[-3])
    up_low = [jnp.where(live, c, 0).astype(b16) for live, c in zip(row_live, cotangent)]
    up_all = [to_four(u) for u in up_low]

    dev = after(dev, q_got[0])
    abs_rows = lax.iota(jnp.int32, width)
    qkv_perm = onehot(abs_rows, pick(table.qkv))
    fc1_perm = onehot(abs_rows, pick(table.fc1))
    proj_perm = onehot(pick(table.heads), pick(table.proj))
    col_perm = onehot(lax.iota(jnp.int32, hidden), pick(table.units))
    chip_perm = onehot(lax.iota(jnp.int32, n), pick(table.chips))
    unit_perm = onehot(pick(table.owners), lax.iota(jnp.int32, n))
    x_all = jnp.stack([inputs, x_other], axis=1).reshape(images * 2 * local, width)
    normed_all, _ = norm_parts(x_all.astype(f32))
    small = dot(chip_perm, small.held.reshape(n, -1)).reshape(n, 2, -1)
    gain_one, shift_one, b_qv, b_proj, gain_two, shift_two, b_fc1, b_fc2 = (
        small[:, :, a:b].reshape(-1) for a, b in zip(ends, ends[1:])
    )
    bias_fc1 = jnp.dot(
        unit_perm.astype(f32), mine_of(b_fc1.reshape(n, 2, units), 1), precision=HIGH
    ).reshape(-1)
    qv_cut = mine_of(b_qv.reshape(2, 2, half), 1)
    bias_qkv = jnp.concatenate([qv_cut[0], jnp.zeros((half,), f32), qv_cut[1]])
    first = (normed_all * gain_one + shift_one).astype(b16)
    first = dot(first, qkv_perm).astype(b16)

    w_qkv = qkv.held.reshape(width, 3 * half)
    mixed = (dot(first, w_qkv) + bias_qkv).astype(b16).reshape(images, 2 * local, 3 * half)
    metas = [jnp.stack([core.astype(jnp.int32), kept_counts[i]]) for i in range(images)]
    proj.step(q_got[-1])
    proj.step()
    w_proj = proj.held.reshape(half, width)
    w_proj = jnp.concatenate([w_proj, core_swap(w_proj)], axis=0)
    w_proj = dot(proj_perm, w_proj).astype(b16)
    fc2_got = fc2.step(q_got[-1])
    fc1_got = fc1.step(fc2_got)
    while fc2.steps:
        fc2.step()
    w_fc2 = dot(col_perm, fc2.held.reshape(hidden, width)).astype(b16)
    while fc1.steps:
        fc1.step()
    w_fc1 = dot(fc1_perm, fc1.held.reshape(width, hidden)).astype(b16)

    attended, middle, second, normed_two, scale_two = [], [], [], [], []
    for i in range(images):
        heads = attention(mixed[i], metas[i])
        heads = jnp.concatenate([heads[:local], core_swap(heads[local:])], axis=1)
        attended.append(heads)
        middle.append(inputs[i].astype(f32) + dot(heads, w_proj) + b_proj)
        normed, scale = norm_parts(middle[i])
        normed_two.append(normed)
        scale_two.append(scale)
        second.append(to_four((normed * gain_two + shift_two).astype(b16)))

    activated, slope = [], []
    for i in range(images):
        pre = dot(second[i], w_fc1) + bias_fc1
        phi = 0.5 * (1.0 + lax.erf(pre * (0.5**0.5)))
        activated.append((pre * phi).astype(b16))
        slope.append((phi + pre * jnp.exp(-0.5 * pre * pre) * 0.3989422804014327).astype(b16))

    def core_sum(part):
        return part[: 2 * local] + core_swap(part[2 * local :].astype(b16)).astype(f32)

    def pair_sum(two):
        return two[:local] + bit_swap(two[local:].astype(b16), pair).astype(f32)

    d_pre, d_two = [], []
    for i in range(images):
        d_pre.append((slope[i].astype(f32) * dot_nt(up_all[i], w_fc2)).astype(b16))
        d_two.append(core_sum(dot_nt(d_pre[i], w_fc1)))
    out_two = [core_sum(dot(activated[i], w_fc2)) for i in range(images)]
    d_second = [pair_sum(d) for d in d_two]

    cat = lambda parts: jnp.concatenate(parts, axis=0)
    cut = hidden // 2
    up_cat = cat(up_all)
    activated = after(cat(activated), *d_two)
    activated_rel = dot(activated, col_perm).astype(b16)
    grad_fc2 = Scatter(
        dot_tn(activated_rel[:, cut:], up_cat).astype(b16).reshape(-1, units, width),
        dot_tn(activated_rel[:, :cut], up_cat).reshape(-1, units, width),
        most,
    )
    second_rel = dot(cat(second), fc1_perm).astype(b16)
    d_pre_cat = cat(d_pre)
    grad_fc1 = Scatter(
        dot_tn(second_rel[:, half:], d_pre_cat).astype(b16).reshape(-1, 4 * rows, hidden),
        dot_tn(second_rel[:, :half], d_pre_cat).reshape(-1, 4 * rows, hidden),
        most,
    )
    grad_fc2.step()
    grad_fc1.step(grad_fc2.got)
    while grad_fc2.steps:
        grad_fc2.step()
    while grad_fc1.steps:
        grad_fc1.step()

    outputs = [
        jnp.where(row_live[i], middle[i] + pair_sum(after(out_two[i], *d_second)) + b_fc2, 0.0)
        for i in range(images)
    ]
    outputs = jnp.stack(outputs).astype(b16)

    d_middle, d_branch, d_mixed = [], [], []
    for i in range(images):
        back = norm_back(d_second[i], normed_two[i], scale_two[i], gain_two)
        d_middle.append(up_low[i].astype(f32) + back)
        d_branch.append(d_middle[i].astype(b16))
        d_att = dot_nt(d_branch[i], w_proj).astype(b16)
        d_att = jnp.concatenate([d_att[:, :half], core_swap(d_att[:, half:])], axis=0)
        d_mixed.append(attention(mixed[i], metas[i], d_att))

    attended_rel = dot(cat(attended), proj_perm).astype(b16)
    attended_rel = jnp.concatenate(
        [attended_rel[:, :half], core_swap(attended_rel[:, half:])], axis=0
    )
    branch = cat(d_branch)
    branch_all = jnp.concatenate([branch, core_swap(branch)], axis=0)
    parts = lambda a: a.reshape(-1, rows, a.shape[-1])
    proj_send = dot_tn(attended_rel[:, half // 2 :], branch_all).astype(b16)
    proj_keep = dot_tn(attended_rel[:, : half // 2], branch_all)
    grad_proj = Scatter(parts(proj_send), parts(proj_keep), full)
    while grad_proj.steps:
        grad_proj.step()

    d_mixed = cat(d_mixed)
    qkv_send = dot_tn(first[:, half:], d_mixed).astype(b16)
    d_first = dot_nt(dot_nt(after(d_mixed, qkv_send), w_qkv).astype(b16), qkv_perm).astype(b16)
    d_first = d_first.reshape(images, 2, local, width)
    d_first = d_first[:, 0].astype(f32) + core_swap(d_first[:, 1]).astype(f32)
    qkv_keep = dot_tn(first[:, :half], after(d_mixed, d_first))
    cut3 = lambda a: a.reshape(-1, 2 * rows, 3 * half)
    grad_qkv = Scatter(cut3(qkv_send), cut3(qkv_keep), full)
    normed_one, scale_one = norm_parts(inputs.astype(f32))
    input_grad = jnp.stack(d_middle) + norm_back(d_first, normed_one, scale_one, gain_one)

    placed = lambda a, axis: jnp.stack(
        [jnp.where(core == 0, a, 0.0), jnp.where(core == 1, a, 0.0)], axis=axis
    )
    total = lambda a: jnp.sum(a.astype(f32).reshape(-1, a.shape[-1]), axis=0)
    d_mixed_sum = total(d_mixed).reshape(3, half)
    d_pre_sum = jnp.dot(
        unit_perm.astype(f32).T, total(d_pre_cat).reshape(few, units), precision=HIGH
    )
    d_second = jnp.stack(d_second)
    small_grads = (
        total(d_first * normed_one),
        total(d_first),
        placed(d_mixed_sum[::2], 1),
        total(branch),
        total(d_second * jnp.stack(normed_two)),
        total(d_second),
        placed(d_pre_sum, 1),
        total(jnp.stack(up_low)),
    )
    small_grads = jnp.concatenate([g.reshape(n, 2, -1) for g in small_grads], axis=2)
    small_grads = mine_of(small_grads, 1) + core_swap(theirs_of(small_grads, 1))
    small_grads = jnp.dot(chip_perm.astype(f32).T, small_grads, precision=HIGH)
    small_grads = small_grads[:, None]
    small_grads = Scatter(small_grads[few:], small_grads[:few], full)
    small_grads.step()
    grad_qkv.step()
    while grad_qkv.steps:
        small_grads.step(grad_qkv.got)
        grad_qkv.step()
    small_grads = small_grads.keep[0, 0]
    small_grads = [small_grads[a:b] for a, b in zip(ends, ends[1:])]
    grad_fc1, grad_fc2, grad_proj, grad_qkv = (
        g.keep[0] for g in (grad_fc1, grad_fc2, grad_proj, grad_qkv)
    )

    qkv_other = core_swap(grad_qkv[rows:])
    both = lambda own, other, which, axis: jnp.where(
        which == 0, jnp.stack([own, other], axis=axis), jnp.stack([other, own], axis=axis)
    )
    cut3 = lambda a: a.reshape(rows, 3, half)
    grad_qkv = both(cut3(grad_qkv[:rows]), cut3(qkv_other), core, 2).reshape(qkv_weight.shape)

    pair_other = bit_swap(grad_fc1[2 * rows :], pair)
    cut4 = lambda a: a.reshape(2 * rows, few // low, low, units)
    grad_fc1 = both(cut4(grad_fc1[: 2 * rows]), cut4(pair_other), side, 2)
    core_other = core_swap(grad_fc1[rows:])
    grad_fc1 = both(grad_fc1[:rows], core_other, core, 4).reshape(fc1_weight.shape)
    return (
        outputs,
        input_grad,
        small_grads[0],
        small_grads[1],
        grad_qkv,
        small_grads[2],
        grad_proj,
        small_grads[3],
        small_grads[4],
        small_grads[5],
        grad_fc1,
        small_grads[6],
        grad_fc2,
        small_grads[7],
    )


def pack_units_kernel(where_ref, w_ref, mine_ref, theirs_ref):
    wide = mine_ref.shape[2]
    units = 128
    low = 1 << PAIR
    for ref, core in ((mine_ref, where_ref[0]), (theirs_ref, 1 - where_ref[0])):
        for p in range(2):
            side = where_ref[1] ^ p
            for b in range(wide // units):
                chip = (b // low) * 2 * low + side * low + b % low
                at = pl.multiple_of((2 * chip + core) * units, units)
                ref[p, :, b * units : (b + 1) * units] = w_ref[:, pl.ds(at, units)]


def pack_units(weight, units, core, side):
    rows, hidden = weight.shape
    if units == 128:
        out = jax.ShapeDtypeStruct((2, rows, hidden // 4), weight.dtype)
        return pl.pallas_call(
            pack_units_kernel,
            out_shape=(out, out),
            in_specs=[pl.BlockSpec(memory_space=pltpu.SMEM), pl.BlockSpec(memory_space=pltpu.VMEM)],
            out_specs=(pl.BlockSpec(memory_space=pltpu.VMEM),) * 2,
        )(jnp.stack([core, side]), weight)
    low = 1 << PAIR
    cut = weight.reshape(rows, -1, 2, low, 2, units)

    def part(c, p):
        block = lax.dynamic_index_in_dim(cut, c, 4, False)
        return lax.dynamic_index_in_dim(block, p, 2, False).reshape(rows, hidden // 4)

    return tuple(jnp.stack([part(c, side), part(c, 1 - side)]) for c in (core, 1 - core))


LANES = 128
MEASURED_US = {
    "k_pack_heads": 1.6, "k_heads": 7, "k_attend": 6, "k_proj_weight": 3, "k_project": 3.4,
    "k_unpack_units": 4.5, "k_feed": 20, "k_feed_out": 6, "k_pair_send": 5, "k_grad_feed": 15,
    "k_middle_back": 4.4, "k_attend_back": 8.3, "k_grad_proj": 5.5, "k_grad_heads": 8.7,
    "k_first_back": 6, "k_input_back": 4.3, "k_small": 1.8, "k_output": 2.5, "k_columns": 2, "k_rows": 1.8,
}
FLOPS_PER_US = 0.5e9
VMEM_LIMIT = 56 * 1024 * 1024
SMALL_ROWS = 8
GAIN1, BIAS1, QV, PROJ_B, GAIN2, BIAS2, FC1_B, FC2_B = range(8)


def spread_of(position, orders, core):
    a, b = (spread(position, order) for order in orders)
    return a if a == b else jnp.where(core == 0, a, b)


def position_of(bits, orders, core):
    a, b = (
        sum((((bits >> bit) & 1) << k) for k, bit in enumerate(order)) for order in orders
    )
    return jnp.where(core == 0, a, b)


def call(kernel, out, args, grid=None, in_specs=None, out_specs=None, scratch=(), deps=(), place=None):
    whole = pl.BlockSpec(memory_space=pltpu.VMEM)
    outs = out if isinstance(out, tuple) else (out,)
    specs = [pl.BlockSpec(memory_space=pltpu.SMEM)] + list(in_specs or [whole] * len(args))
    out_specs = out_specs if out_specs is not None else tuple(whole for _ in outs)
    extra = {} if grid is None else {"grid": grid}
    name = getattr(kernel, "func", kernel).__name__
    flops = int(MEASURED_US[name] * FLOPS_PER_US)
    if deps:
        specs += [pl.BlockSpec(memory_space=pl.ANY)] * len(deps)
        inner, count = kernel, 1 + len(args)

        def kernel(*refs):
            return inner(*refs[:count], *refs[count + len(deps) :])

    result = pl.pallas_call(
        kernel,
        out_shape=outs,
        in_specs=specs,
        out_specs=tuple(out_specs),
        scratch_shapes=list(scratch),
        compiler_params=pltpu.CompilerParams(vmem_limit_bytes=VMEM_LIMIT),
        cost_estimate=pl.CostEstimate(flops=flops, bytes_accessed=1000, transcendentals=0),
        **extra,
    )(place, *args, *deps)
    return result if isinstance(out, tuple) else result[0]


class Order:
    def __init__(self, place):
        self.place, self.last = place, ()

    def call(self, *args, wait=(), **named):
        result = call(*args, deps=tuple(wait) + self.last, place=self.place, **named)
        found = result if isinstance(result, tuple) else (result,)
        self.last = (min(found, key=lambda a: a.size),)
        return result

    def now(self, *values):
        values = lax.optimization_barrier((*values, *self.last))
        self.last = tuple(values[len(values) - len(self.last) :])
        values = values[: len(values) - len(self.last)]
        return values if len(values) > 1 else values[0]


def tie(*values):
    return lax.optimization_barrier(values)


def shape(dims, dtype=f32):
    return jax.ShapeDtypeStruct(tuple(dims), dtype)


def aligned(index, step):
    return pl.multiple_of(index * step, step)


def k_pack_heads(place, w, small, theirs, mine):
    three = w.shape[1]
    half = three // 6
    me_core = lax.axis_index("seq")
    for ref, core in ((mine, me_core), (theirs, 1 - me_core)):
        for which in range(3):
            at = pl.multiple_of((which * 2 + core) * half, half)
            ref[:, which * half : (which + 1) * half] = w[:, pl.ds(at, half)]
        ref[:, 3 * half :] = jnp.zeros((w.shape[0], LANES), b16)
        ref[:SMALL_ROWS, 3 * half :] = small[...]


def k_heads(orders, place, sent, got, x_own, x_other, w_qkv, vectors, first, mixed, small):
    me, core, side = place[0], place[1], place[2]
    blocks, two_rows, lanes = sent.shape
    n = 2 * blocks
    rows = two_rows // 2
    three = w_qkv.shape[1]
    half = three // 3
    for p in range(n):
        block = sent if p < blocks else got
        at = p % blocks
        chip = me ^ spread_of(p, orders, core)
        for c in range(2):
            dev = 2 * chip + (core ^ c)
            part = slice(c * rows, (c + 1) * rows)
            w_qkv[pl.ds(aligned(dev, rows), rows), :] = block[at, part, :three]
            small[dev] = block[at, c * rows : c * rows + SMALL_ROWS, three:].astype(f32)

    def lane_block(first_dev, vector, size):
        total = small[first_dev, vector : vector + 1, :]
        for i in range(1, LANES // size):
            total += pltpu.roll(small[first_dev + i, vector : vector + 1, :], i * size, 1)
        return total

    width = w_qkv.shape[0]
    per = width // (2 * n)
    for row, vector in enumerate((GAIN1, BIAS1, PROJ_B, GAIN2, BIAS2, FC2_B)):
        for q in range(width // LANES):
            vectors[row : row + 1, q * LANES : (q + 1) * LANES] = lane_block(
                q * (LANES // per), vector, per
            )
    for which in range(2):
        for q in range(half // LANES):
            dev = (which * 2 + core) * (half // (2 * per)) + q * (LANES // (2 * per))
            at = which * half + q * LANES
            vectors[6:7, at : at + LANES] = lane_block(dev, QV, 2 * per)
    low = 1 << PAIR
    for b in range(n // 2):
        chip = (b // low) * 2 * low + side * low + b % low
        vectors[7:8, b * LANES : (b + 1) * LANES] = small[2 * chip + core, FC1_B : FC1_B + 1, :]

    images, local, _ = x_own.shape
    for i in range(images):
        for c, ref in enumerate((x_own, x_other)):
            normed, _ = norm_parts(ref[i].astype(f32))
            at = (2 * i + c) * local
            first[at : at + local, :] = (
                normed * vectors[0:1, :] + vectors[1:2, :]
            ).astype(b16)
    for which in range(3):
        part = slice(which * half, (which + 1) * half)
        total = dot(first[...], w_qkv[:, part])
        if which != 1:
            total += vectors[6:7, (which // 2) * half : (which // 2 + 1) * half]
        mixed[:, part] = total.astype(b16)


def k_proj_weight(orders, place, sent, got, sent_far, got_far, w_proj):
    me, core = place[0], place[1]
    blocks, rows, _ = sent.shape
    for c, refs in enumerate(((sent, got), (sent_far, got_far))):
        for p in range(2 * blocks):
            chip = me ^ spread_of(p, orders, core ^ c)
            at = aligned(2 * chip + (core ^ c), rows)
            w_proj[pl.ds(at, rows), :] = refs[p // blocks][p % blocks]


def k_pair_send(place, pair, got, send):
    send[...] = (pair[...] + got[pair.shape[0] :, :].astype(f32)).astype(b16)


def k_output(image, place, middle, own, got, pair_got, vectors, out):
    local = own.shape[0]
    slot = place[1] * local + lax.broadcasted_iota(jnp.int32, (local, 1), 0)
    total = middle[...] + vectors[5:6, :] + own[...]
    total += got[:local, :].astype(f32) + pair_got[...].astype(f32)
    out[...] = jnp.where(slot < BUFFER + place[3 + image], total, 0.0).astype(b16)


def k_unpack_units(orders, place, sent, got, w_fc1, w_fc2):
    me, core = place[0], place[1]
    blocks = sent.shape[0]
    units = LANES
    rows = (sent.shape[1] - units) // 4
    low = 1 << PAIR
    for p in range(2 * blocks):
        block = sent if p < blocks else got
        at = p % blocks
        chip = me ^ spread_of(p, orders, core)
        for c2 in range(2):
            for c in range(2):
                dev = 2 * (chip ^ (c2 << PAIR)) + (core ^ c)
                k = 2 * c2 + c
                w_fc1[pl.ds(aligned(dev, rows), rows), :] = block[at, k * rows : (k + 1) * rows, :]
        short = ((chip >> (PAIR + 1)) << PAIR) + (chip & (low - 1))
        w_fc2[pl.ds(aligned(short, units), units), :] = block[at, 4 * rows :, :]


def live_of(place, image, local, axis):
    dims = (2 * local, 1) if axis == 0 else (1, 2 * local)
    at = lax.broadcasted_iota(jnp.int32, dims, axis)
    core = place[1]
    slot = jnp.where(at < local, at + core * local, at - core * local)
    return slot < BUFFER + place[3 + image]


def k_attend(image, place, q, k, v, own, other):
    local = own.shape[0]
    live = live_of(place, image, local, 1)
    outs = []
    for e in range(2):
        part = slice(e * HEAD_DIM, (e + 1) * HEAD_DIM)
        raw = dot_nt(q[:, part], k[:, part]) * (HEAD_DIM**-0.5)
        raw = jnp.where(live, raw, -1e30)
        expo = jnp.exp(raw - jnp.max(raw, axis=-1, keepdims=True))
        probs = expo * (1.0 / jnp.sum(expo, axis=-1, keepdims=True))
        outs.append(dot(probs.astype(b16), v[:, part]))
    both = jnp.concatenate(outs, axis=1).astype(b16)
    own[...] = both[:local]
    other[...] = both[local:]


def k_attend_back(image, place, q, k, v, g_own, g_other, d_mixed, sums):
    local = g_own.shape[0]
    pairs = pl.num_programs(0)
    live = live_of(place, image, local, 0)
    scale = HEAD_DIM**-0.5
    g = jnp.concatenate([g_own[...], g_other[...]], axis=0)
    parts = ([], [], [])
    for e in range(2):
        part = slice(e * HEAD_DIM, (e + 1) * HEAD_DIM)
        qe, ke, ve, ge = q[:, part], k[:, part], v[:, part], g[:, part]
        raw = jnp.where(live, dot_nt(ke, qe) * scale, -1e30)
        expo = jnp.exp(raw - jnp.max(raw, axis=0, keepdims=True))
        probs = expo * (1.0 / jnp.sum(expo, axis=0, keepdims=True))
        d_probs = dot_nt(ve, ge)
        inner = jnp.sum(probs * d_probs, axis=0, keepdims=True)
        d_scores = (probs * (d_probs - inner)).astype(b16)
        parts[0].append(dot_tn(d_scores, ke) * scale)
        parts[1].append(dot(d_scores, qe) * scale)
        parts[2].append(dot(probs.astype(b16), ge))
    for which in range(3):
        at = pl.multiple_of((which * pairs + pl.program_id(0)) * LANES, LANES)
        value = jnp.concatenate(parts[which], axis=1).astype(b16)
        d_mixed[:, pl.ds(at, LANES)] = value
        total = jnp.sum(value.astype(f32), axis=0, keepdims=True)
        sums[:, pl.ds(at, LANES)] = jnp.broadcast_to(total, (8, LANES))


def k_project(place, att_own, att_got, w, x, vectors, middle, second):
    core = place[1]
    half = att_own.shape[1]
    own = w[pl.ds(aligned(core, half), half), :]
    other = w[pl.ds(aligned(1 - core, half), half), :]
    total = dot(att_own[...], own) + dot(att_got[...], other)
    mid = x[0].astype(f32) + total + vectors[2:3, :]
    middle[...] = mid
    normed, _ = norm_parts(mid)
    second[...] = (normed * vectors[3:4, :] + vectors[4:5, :]).astype(b16)


def k_feed(image, place, s0, s1, s2, s3, u0, u1, u2, u3, w1, w2, vectors,
           act, d_pre, ds_own, ds_pair, ds_other, sums, sec, up):
    local = s0.shape[0]
    tile = 256
    for k, (s, u) in enumerate(((s0, u0), (s1, u1), (s2, u2), (s3, u3))):
        sec[k * local : (k + 1) * local, :] = s[...]
        up[k * local : (k + 1) * local, :] = u[image]
    for at in range(0, w1.shape[1], tile):
        part = slice(at, at + tile)
        pre = dot(sec[...], w1[:, part]) + vectors[7:8, part]
        phi = 0.5 * (1.0 + lax.erf(pre * (0.5**0.5)))
        act[:, part] = (pre * phi).astype(b16)
        slope = phi + pre * jnp.exp(-0.5 * pre * pre) * 0.3989422804014327
        grad = (slope * dot_nt(up[...], w2[part, :])).astype(b16)
        d_pre[:, part] = grad
        total = jnp.sum(grad.astype(f32), axis=0, keepdims=True)
        sums[:, part] = jnp.broadcast_to(total, (8, tile))
    ds_other[...] = dot_nt(d_pre[2 * local :, :], w1[...]).astype(b16)
    ds_pair[...] = dot_nt(d_pre[local : 2 * local, :], w1[...])
    ds_own[...] = dot_nt(d_pre[:local, :], w1[...])


def k_feed_out(place, act, w2, own, pair, other):
    local = own.shape[0]
    other[...] = dot(act[2 * local :, :], w2[...]).astype(b16)
    pair[...] = dot(act[local : 2 * local, :], w2[...])
    own[...] = dot(act[:local, :], w2[...])


def k_middle_back(place, ds_own, ds_got, pair_got, middle, up, w, vectors,
                  d_middle, d_branch, att_own, att_other, sums):
    core = place[1]
    local = ds_own.shape[0]
    half = att_own.shape[1]
    d_second = ds_own[...] + ds_got[:local, :].astype(f32) + pair_got[...].astype(f32)
    normed, scale = norm_parts(middle[...])
    upstream = up[0].astype(f32)
    d_mid = upstream + norm_back(d_second, normed, scale, vectors[3:4, :])
    d_middle[...] = d_mid
    branch = d_mid.astype(b16)
    d_branch[...] = branch
    att_own[...] = dot_nt(branch, w[pl.ds(aligned(core, half), half), :]).astype(b16)
    att_other[...] = dot_nt(branch, w[pl.ds(aligned(1 - core, half), half), :]).astype(b16)
    total = lambda a: jnp.sum(a, axis=0, keepdims=True)
    sums[0:1, :] = total(d_second * normed)
    sums[1:2, :] = total(d_second)
    sums[2:3, :] = total(branch.astype(f32))
    sums[3:4, :] = total(upstream)
    sums[4:, :] = jnp.zeros((4, sums.shape[1]), f32)


def put(send, keep, place_at, rows_at, value, half_count, per):
    @pl.when(place_at >= half_count)
    def _():
        at = pl.multiple_of((place_at - half_count) * per + rows_at, value.shape[0])
        send[pl.ds(at, value.shape[0]), :] = value.astype(b16)

    @pl.when(place_at < half_count)
    def _():
        at = pl.multiple_of(place_at * per + rows_at, value.shape[0])
        keep[pl.ds(at, value.shape[0]), :] = value


def k_grad_heads(orders, n, place, left, r0, r1, send, keep):
    me, core = place[0], place[1]
    step = pl.program_id(0)
    cut = left.shape[0] // 2
    tile = left.shape[1]
    rows = 2 * send.shape[0] // (2 * n)
    total = dot_tn(left[:cut, :], r0[...]) + dot_tn(left[cut:, :], r1[...])
    for i in range(tile // (2 * rows)):
        chip = step * (tile // (2 * rows)) + i
        at = position_of(me ^ chip, orders, core)
        for c in range(2):
            value = total[(2 * i + c) * rows : (2 * i + c + 1) * rows, :]
            put(send, keep, at, (core ^ c) * rows, value, n // 2, 2 * rows)


def k_grad_feed(orders, n, place, a0, a1, u0, u1, s0, s1, d0, d1, send, keep):
    me, core, side = place[0], place[1], place[2]
    low = 1 << PAIR
    tile = 256
    per = 2 * send.shape[0] // (n // 2)
    rows = (per - LANES) // 4
    for step in range(a0.shape[1] // tile):
        part = slice(step * tile, (step + 1) * tile)
        total = dot_tn(a0[:, part], u0[...]) + dot_tn(a1[:, part], u1[...])
        for i in range(tile // LANES):
            b = step * (tile // LANES) + i
            chip = (b // low) * 2 * low + side * low + b % low
            at = position_of(me ^ chip, orders, core)
            put(send, keep, at, 0, total[i * LANES : (i + 1) * LANES, :], n // 4, per)
    for step in range(s0.shape[1] // tile):
        part = slice(step * tile, (step + 1) * tile)
        total = dot_tn(s0[:, part], d0[...]) + dot_tn(s1[:, part], d1[...])
        for i in range(tile // rows):
            dev = step * (tile // rows) + i
            bits = me ^ (dev // 2)
            at = position_of(bits, orders, core)
            inner = LANES + (((bits >> PAIR) & 1) * 2 + (core ^ (i % 2))) * rows
            put(send, keep, at, inner, total[i * rows : (i + 1) * rows, :], n // 4, per)


def k_grad_proj(orders, place, *refs):
    lefts, rights, (send, keep) = (refs[:4], refs[4:8]), refs[8:12], refs[12:]
    me, core = place[0], place[1]
    rows = 32
    right = jnp.concatenate([a[...] for a in rights], axis=0)
    count = lefts[0][0].shape[1] // (2 * rows)
    for which in range(2):
        left = jnp.concatenate([a[...] for a in lefts[which]], axis=0)
        total = dot_tn(left, right)
        for i in range(count):
            chip = (core ^ which) * count + i
            at = position_of(me ^ chip, orders, core)
            value = jnp.where(
                core == 0,
                total[2 * i * rows : (2 * i + 1) * rows, :],
                total[(2 * i + 1) * rows : (2 * i + 2) * rows, :],
            )
            put(send, keep, at, 0, value, count, rows)


def k_first_back(place, d0, d1, w, own, other):
    local = own.shape[1]
    for i, d in enumerate((d0, d1)):
        total = dot_nt(d[...], w[...])
        own[i] = total[:local]
        other[i] = total[local:].astype(b16)


def k_input_back(place, x, own, got, m0, m1, vectors, grad, sums):
    total = lambda a: jnp.sum(a, axis=0, keepdims=True)
    gains = biases = 0.0
    for i, mid in enumerate((m0, m1)):
        normed, scale = norm_parts(x[i].astype(f32))
        d_first = own[i] + got[i].astype(f32)
        grad[i] = mid[...] + norm_back(d_first, normed, scale, vectors[0:1, :])
        gains += total(d_first * normed)
        biases += total(d_first)
    sums[0:1, :] = gains
    sums[1:2, :] = biases
    sums[2:, :] = jnp.zeros((6, sums.shape[1]), f32)


def k_small(orders, n, place, one, mid0, mid1, pre0, pre1, mix0, mix1, mine, theirs, small):
    me, core, side = place[0], place[1], place[2]
    width = one.shape[1]
    per = width // (2 * n)
    half = width // 2
    mids = mid0[...] + mid1[...]
    pres = pre0[...] + pre1[...]
    mixes = mix0[...] + mix1[...]
    small[...] = jnp.zeros(small.shape, f32)
    rows = (
        (GAIN1, one[0:1, :]),
        (BIAS1, one[1:2, :]),
        (GAIN2, mids[0:1, :]),
        (BIAS2, mids[1:2, :]),
        (PROJ_B, mids[2:3, :]),
        (FC2_B, mids[3:4, :]),
    )
    lane = lambda row, q: row[:, q * LANES : (q + 1) * LANES]
    for vector, row in rows:
        for dev in range(2 * n):
            q, i = divmod(dev * per, LANES)
            part = lane(row, q)
            small[dev, vector : vector + 1, :] = part if i == 0 else pltpu.roll(part, LANES - i, 1)
    for which in range(2):
        row = mixes[0:1, 2 * which * half : (2 * which + 1) * half]
        for dev in range(half // (2 * per)):
            q, i = divmod(dev * 2 * per, LANES)
            part = lane(row, q)
            part = part if i == 0 else pltpu.roll(part, LANES - i, 1)
            small[(2 * which + core) * (half // (2 * per)) + dev, QV : QV + 1, :] = part
    low = 1 << PAIR
    for b in range(n // 2):
        chip = (b // low) * 2 * low + side * low + b % low
        small[2 * chip + core, FC1_B : FC1_B + 1, :] = lane(pres[0:1, :], b)
    for p in range(n):
        mine[p] = small[2 * (me ^ spread_of(p, orders, core)) + core]
        theirs[p] = small[2 * (me ^ spread_of(p, orders, 1 - core)) + 1 - core]


def k_rows(place, own, got, out):
    core = place[1]
    half = out.shape[1] // 6
    for which in range(3):
        part = slice(which * half, (which + 1) * half)
        at = pl.multiple_of((2 * which + core) * half, half)
        out[:, pl.ds(at, half)] = own[: out.shape[0], part]
        at = pl.multiple_of((2 * which + 1 - core) * half, half)
        out[:, pl.ds(at, half)] = got[:, part]


def k_columns(place, own, own_pair, got, got_pair, out):
    core, side = place[1], place[2]
    low = 1 << PAIR
    rows = out.shape[0]
    for ref, c, s in (
        (own, core, side),
        (own_pair, core, 1 - side),
        (got, 1 - core, side),
        (got_pair, 1 - core, 1 - side),
    ):
        for b in range(ref.shape[1] // LANES):
            chip = (b // low) * 2 * low + s * low + b % low
            at = pl.multiple_of((2 * chip + c) * LANES, LANES)
            out[:, pl.ds(at, LANES)] = ref[:rows, b * LANES : (b + 1) * LANES]


class Sums:
    def __init__(self, run, send, keep, orders):
        self.run, self.send, self.keep, self.got = run, send, keep, None
        self.steps = list(zip(*orders))[::-1]
        self.step()

    def settle(self):
        got = self.run.now(self.got)
        cut = got.shape[0] // 2
        if cut:
            self.send = (self.keep[cut:] + got[cut:].astype(f32)).astype(self.send.dtype)
            self.keep = self.keep[:cut] + got[:cut].astype(f32)
        else:
            self.keep = self.keep + got.astype(f32)
        self.got = None

    def step(self):
        if self.got is not None:
            self.settle()
        self.got = bit_swap(self.send, self.steps.pop(0))

    def sum(self):
        while self.steps:
            self.step()
        self.settle()
        return self.keep[0]


def fast_body(
    inputs,
    cotangent,
    kept_counts,
    norm1_gain,
    norm1_bias,
    qkv_weight,
    qv_bias,
    proj_weight,
    proj_bias,
    norm2_gain,
    norm2_bias,
    fc1_weight,
    fc1_bias,
    fc2_weight,
    fc2_bias,
):
    images, local, width = inputs.shape
    n = lax.axis_size("img")
    me = lax.axis_index("img")
    core = lax.axis_index("seq")
    levels = n.bit_length() - 1
    half = width // 2
    rows = width // (2 * n)
    units = fc2_weight.shape[0]
    few = n // 2
    hidden = units * few
    side = (me >> PAIR) & 1
    pair = (PAIR, PAIR)
    full = tuple(tuple(range(levels - 1, 1, -1)) + last for last in ((0, 1), (1, 0)))
    most = tuple(tuple(b for b in order if b != PAIR) for order in full)
    last = tuple(order[-2:] + order[:-2] for order in full)
    place = jnp.concatenate([jnp.stack([me, core, side]).astype(jnp.int32), kept_counts])
    run = Order(place)
    on = run.call
    bind = functools.partial
    block = lambda dims, index: pl.BlockSpec(dims, index)
    whole = pl.BlockSpec(memory_space=pltpu.VMEM)

    smalls = (norm1_gain, norm1_bias, qv_bias, proj_bias, norm2_gain, norm2_bias, fc1_bias, fc2_bias)
    small = sum(
        jnp.pad(a[None], ((i, 7 - i), (0, LANES - a.shape[0]))) for i, a in enumerate(smalls)
    )
    packed = shape((rows, 3 * half + LANES), b16)
    theirs, mine = call(k_pack_heads, (packed, packed), (qkv_weight, small), place=kept_counts)
    fc1_mine, fc1_theirs = pack_units(fc1_weight, units, core, side)
    heads = Gather(jnp.concatenate([mine, core_swap(theirs)], axis=0), full)
    fc1_got = core_swap(fc1_theirs)
    x_other = core_swap(inputs)
    slot = core * local + lax.iota(jnp.int32, local)
    row_live = slot[None, :] < BUFFER + kept_counts[:, None]
    up = jnp.where(row_live[:, :, None], cotangent, 0).astype(b16)
    up_other = core_swap(up)
    fc1_send = jnp.concatenate([fc1_mine[1], fc1_got[1]], axis=0)
    proj = Gather(proj_weight, last)

    heads.step()
    heads.held, proj.held, fc1_send, x_other, up_other = tie(
        heads.held, proj.held, fc1_send, x_other, up_other
    )
    heads.step()
    proj.step()
    fc2 = Gather(fc2_weight, most)
    heads.held, proj.held, fc1_send, fc2.held = tie(heads.held, proj.held, fc1_send, fc2.held)
    while len(heads.steps) > 1:
        heads.step()
    proj.step()
    fc1_pair = bit_swap(fc1_send, pair)
    fc2.step()
    fc1 = Gather(jnp.concatenate([fc1_mine[0], fc1_got[0], fc1_pair], axis=0), most)
    heads.held, proj.held, fc1.held, fc2.held = tie(heads.held, proj.held, fc1.held, fc2.held)
    heads.step()
    proj.step()
    fc1.step()
    feed = Gather(None, most)
    feed.steps = fc1.steps
    feed.held = jnp.concatenate([fc1.held, fc2.held], axis=1)
    feed.held, up, heads.got, proj.held = tie(feed.held, up, heads.got, proj.held)
    feed.step()
    proj.step()
    up_pair = bit_swap(up, pair)

    tokens = images * 2 * local
    w_qkv, vectors, first, mixed = on(
        bind(k_heads, full),
        (
            shape((width, 3 * half), b16),
            shape((8, width)),
            shape((tokens, width), b16),
            shape((tokens, 3 * half), b16),
        ),
        (heads.sent, heads.got, inputs, x_other),
        scratch=[pltpu.VMEM((2 * n, SMALL_ROWS, LANES), f32)],
    )
    pairs = half // LANES
    slots = 2 * local
    head_specs = lambda i: [
        block((slots, LANES), lambda h, i=i, f=f: (i, f + h)) for f in (0, pairs, 2 * pairs)
    ]
    lane_spec = block((local, LANES), lambda h: (0, h))
    att_own, att_got, att_other = [], [], []
    for i in range(images):
        own, other = on(
            bind(k_attend, i),
            (shape((local, half), b16),) * 2,
            (mixed, mixed, mixed),
            grid=(pairs,),
            in_specs=head_specs(i),
            out_specs=[lane_spec, lane_spec],
        )
        att_own.append(own)
        att_other.append(other)
        att_got.append(core_swap(other))
        if i == 0:
            proj.got, feed.got = run.now(proj.got, feed.got)
            proj_far = core_swap(proj.sent), core_swap(proj.got)
            feed.held = jnp.concatenate([feed.sent, feed.got], axis=0)
            feed.step()
    w_proj = on(
        bind(k_proj_weight, last),
        shape((width, width), b16),
        (proj.sent, proj.got, *proj_far),
    )
    middle, second = [], []
    for i in range(images):
        mid, sec = on(
            k_project,
            (shape((local, width)), shape((local, width), b16)),
            (att_own[i], att_got[i], w_proj, inputs, vectors),
            grid=(1,),
            in_specs=[whole, whole, whole, block((1, local, width), lambda t, i=i: (i, 0, 0)), whole],
        )
        middle.append(mid)
        second.append((sec, bit_swap(sec, pair), core_swap(sec)))
        if i == 0:
            up_pair = run.now(up_pair)
            up_other_pair = core_swap(up_pair)
    ups = (up, up_pair, up_other, up_other_pair)
    w_fc1, w_fc2 = on(
        bind(k_unpack_units, most),
        (shape((width, hidden), b16), shape((hidden, width), b16)),
        (feed.sent, feed.got),
    )

    tile = 256
    tiles = hidden // tile
    part = shape((local, width))
    other_part = shape((2 * local, width), b16)
    fixed = lambda dims: block(dims, lambda t: (0,) * len(dims))
    feeds, outs, ds_got, ds_sends, out_got = [], [], [], [], []
    send_shape = shape((local, width), b16)
    for i in range(images):
        sec, sec_pair, sec_other = second[i]
        if i == 0:
            sec_pair = run.now(sec_pair)
        second[i] = (sec, sec_pair, sec_other, core_swap(sec_pair))
        feeds.append(
            on(
                bind(k_feed, i),
                (
                    shape((4 * local, hidden), b16),
                    shape((4 * local, hidden), b16),
                    part, part, other_part,
                    shape((8, hidden)),
                    shape((4 * local, width), b16),
                    shape((4 * local, width), b16),
                ),
                second[i] + ups + (w_fc1, w_fc2, vectors),
            )
        )
        ds_got.append(core_swap(feeds[i][4]))
        outs.append(on(k_feed_out, (part, part, other_part), (feeds[i][0], w_fc2)))
        out_got.append(core_swap(outs[i][2]))
        if i == 0:
            sec, sec_pair, sec_other = second[1]
            second[1] = (sec, run.now(sec_pair), sec_other)
        ds_sends.append(on(k_pair_send, send_shape, (feeds[i][3], ds_got[i])))
    pair_got = [bit_swap(s, pair) for s in ds_sends]

    acts = [f[0] for f in feeds]
    d_pres = [f[1] for f in feeds]

    halves = lambda count, cols: (shape((count, cols), b16), shape((count, cols)))
    cut = lambda a, per: a.reshape(-1, per, a.shape[-1])
    feed_send, feed_keep = on(
        bind(k_grad_feed, most, n),
        halves(few // 2 * (4 * rows + units), width),
        (*acts, *[f[7] for f in feeds], *[f[6] for f in feeds], *d_pres),
    )
    grad_feed = Sums(run, cut(feed_send, 4 * rows + units), cut(feed_keep, 4 * rows + units), most)

    d_middle, d_branch, mid_sums, d_mixed, mix_sums, att_grads = [], [], [], [], [], []
    for i in range(images):
        d_mid, branch, own, other, sums = on(
            k_middle_back,
            (part, shape((local, width), b16)) + (shape((local, half), b16),) * 2 + (shape((8, width)),),
            (feeds[i][2], ds_got[i], pair_got[i], middle[i], up, w_proj, vectors),
            grid=(1,),
            in_specs=[whole] * 4 + [block((1, local, width), lambda t, i=i: (i, 0, 0)), whole, whole],
        )
        d_middle.append(d_mid)
        d_branch.append(branch)
        mid_sums.append(sums)
        att_grads.append((own, core_swap(other)))
    def attend_back(i, *wait):
        d, sums = on(
            bind(k_attend_back, i),
            (shape((slots, 3 * half), b16), shape((8, 3 * half))),
            (mixed, mixed, mixed) + att_grads[i],
            grid=(pairs,),
            in_specs=head_specs(i) + [lane_spec, lane_spec],
            out_specs=[fixed((slots, 3 * half)), fixed((8, 3 * half))],
            wait=wait,
        )
        d_mixed.append(d)
        mix_sums.append(sums)

    att_far = [core_swap(a) for a in att_own]
    d_branch_far = [core_swap(b) for b in d_branch]
    attend_back(0)
    grad_feed.step()
    proj_send, proj_keep = on(
        bind(k_grad_proj, full),
        halves(half // 2, width),
        (*att_own, *att_other, *att_got, *att_far, *d_branch, *d_branch_far),
    )
    grad_proj = Sums(run, cut(proj_send, rows), cut(proj_keep, rows), full)
    attend_back(1)
    grad_feed.step()
    qkv_send, qkv_keep = on(
        bind(k_grad_heads, full, n),
        halves(half, 3 * half),
        (first, *d_mixed),
        grid=(width // tile,),
        in_specs=[block((tokens, tile), lambda t: (0, t)), whole, whole],
        out_specs=[fixed((half, 3 * half))] * 2,
    )
    grad_qkv = Sums(run, cut(qkv_send, 2 * rows), cut(qkv_keep, 2 * rows), full)
    grad_proj.step()
    df_own, df_other = on(
        k_first_back,
        (shape(inputs.shape), shape(inputs.shape, b16)),
        (*d_mixed, w_qkv),
    )
    df_got = core_swap(df_other)
    out_sends = [on(k_pair_send, send_shape, (f[1], g)) for f, g in zip(outs, out_got)]
    out_pair = [bit_swap(s, pair) for s in out_sends]
    input_grad, one_sums = on(
        k_input_back,
        (shape(inputs.shape), shape((8, width))),
        (inputs, df_own, df_got, d_middle[0], d_middle[1], vectors),
    )
    small_shape = shape((n, SMALL_ROWS, LANES))
    grad_proj.step()
    small_mine, small_theirs = on(
        bind(k_small, full, n),
        (small_shape, small_shape),
        (one_sums, *mid_sums, feeds[0][5], feeds[1][5], *mix_sums),
        scratch=[pltpu.VMEM((2 * n, SMALL_ROWS, LANES), f32)],
    )
    small_got = core_swap(small_theirs)
    grad_proj.step()
    grad_feed = grad_feed.sum()
    grad_fc2, fc1_own = grad_feed[:units], grad_feed[units:]
    fc1_from = bit_swap(fc1_own[2 * rows :], pair)
    fc1_core = core_swap(fc1_own[rows : 2 * rows])
    small_sum = small_mine + run.now(small_got)
    small_sums = Sums(run, small_sum[few:], small_sum[:few], full)
    grad_qkv.step()
    small_sums.step()
    outputs = [
        on(bind(k_output, i), send_shape, (middle[i], f[0], out_got[i], out_pair[i], vectors))
        for i, f in enumerate(outs)
    ]
    outputs = jnp.stack(outputs)
    fc1_from = run.now(fc1_from)
    fc1_from_core = core_swap(fc1_from[rows:])
    grad_qkv.step()
    small_sums.step()
    fc1_rows = on(
        k_columns, shape(fc1_weight.shape), (fc1_own, fc1_from, fc1_core, fc1_from_core)
    )
    while grad_qkv.steps:
        grad_qkv.step()
        small_sums.step()
    small_sums.settle()

    final = small_sums.keep[0]
    vector_grads = [final[v, : a.shape[0]] for v, a in enumerate(smalls)]
    grad_proj = grad_proj.sum()
    qkv_own = grad_qkv.sum()
    qkv_rows = on(
        k_rows, shape((rows, 6 * half)), (qkv_own, core_swap(qkv_own[rows:]))
    )
    return (
        outputs,
        input_grad,
        vector_grads[GAIN1],
        vector_grads[BIAS1],
        qkv_rows,
        vector_grads[QV],
        grad_proj,
        vector_grads[PROJ_B],
        vector_grads[GAIN2],
        vector_grads[BIAS2],
        fc1_rows,
        vector_grads[FC1_B],
        grad_fc2,
        vector_grads[FC2_B],
    )


def body(*args):
    whole_tiles = args[3].shape[0] % 32 == 0 and args[12].shape[0] == LANES
    return (fast_body if whole_tiles else plain_body)(*args)


def solution(mesh):
    row = P(("img", "seq"))
    mat = P(("img", "seq"), None)
    act = P("img", "seq", None)
    return jax.shard_map(
        body,
        mesh=mesh,
        in_specs=(act, act, P("img"), row, row, mat, row, mat, row, row, row, mat, row, mat, row),
        out_specs=(act, act, row, row, mat, row, mat, row, row, row, mat, row, mat, row),
        check_vma=False,
    )
```

```python
import functools

import jax
import jax.numpy as jnp
import numpy as np
from jax import lax
from jax.experimental import pallas as pl
from jax.experimental.pallas import tpu as pltpu
from jax.sharding import PartitionSpec as P

HEAD_DIM = 64
BUFFER = 64
PAIR = 2
f32 = jnp.float32
b16 = jnp.bfloat16
HIGH = lax.Precision.HIGHEST


def dot(left, right):
    return jnp.dot(left, right, preferred_element_type=f32)


def dot_tn(left, right):
    return lax.dot_general(left, right, (((0,), (0,)), ((), ())), preferred_element_type=f32)


def dot_nt(left, right):
    return lax.dot_general(left, right, (((1,), (1,)), ((), ())), preferred_element_type=f32)


def norm_parts(values):
    centre = values - jnp.mean(values, axis=-1, keepdims=True)
    scale = lax.rsqrt(jnp.mean(centre * centre, axis=-1, keepdims=True) + 1e-06)
    return centre * scale, scale


def norm_back(grad, normed, scale, gain):
    e = grad * gain
    return scale * (
        e
        - jnp.mean(e, axis=-1, keepdims=True)
        - normed * jnp.mean(e * normed, axis=-1, keepdims=True)
    )


def core_swap(value):
    return lax.ppermute(value, "seq", [(0, 1), (1, 0)])


def bit_swap(value, bits):
    n = lax.axis_size("img")
    pairs = [
        (2 * j + c, 2 * (j ^ (1 << bits[c])) + c) for j in range(n) for c in range(2)
    ]
    return lax.ppermute(value, ("img", "seq"), pairs)


def after(value, *others):
    return lax.optimization_barrier((value, *others))[0]


class Gather:
    def __init__(self, block, orders):
        self.held = None if block is None else block[None]
        self.steps = list(zip(*orders))

    def step(self, *others):
        self.sent = after(self.held, *others) if others else self.held
        self.got = bit_swap(self.sent, self.steps.pop(0))
        self.held = jnp.concatenate([self.sent, self.got], axis=0)
        return self.got


class Scatter:
    def __init__(self, send, keep, orders):
        self.send, self.keep = send, keep
        self.steps = list(zip(*orders))[::-1]

    def step(self, *others):
        send = after(self.send, *others) if others else self.send
        self.got = bit_swap(send, self.steps.pop(0))
        total = self.keep + self.got.astype(f32)
        cut = total.shape[0] // 2
        if cut:
            self.send = total[cut:].astype(send.dtype)
        self.keep = total[: max(cut, 1)]


def spread(position, order):
    return sum((((position >> k) & 1) << bit) for k, bit in enumerate(order))


def onehot(left, right):
    return (left[:, None] == right[None, :]).astype(b16)


class Places:
    def __init__(self, n, width, units, full, most):
        rows, half, few = width // (2 * n), width // 2, n // 2
        place, chips = np.arange(width), np.arange(few)
        col = np.arange(few * units)
        names = ("qkv", "fc1", "proj", "heads", "units", "chips", "owners")
        found = {name: [] for name in names}
        for me in range(n):
            for core in range(2):
                chip = me ^ spread(place // (2 * rows), full[core])
                found["qkv"].append((2 * chip + (core ^ (place // rows % 2))) * rows + place % rows)
                chip = me ^ spread(place // (4 * rows), most[core])
                chip = chip ^ ((place // (2 * rows) % 2) << PAIR)
                found["fc1"].append((2 * chip + (core ^ (place // rows % 2))) * rows + place % rows)
                source = core ^ (place // half)
                chip = me ^ np.where(
                    source == 0,
                    spread(place // rows % n, full[0]),
                    spread(place // rows % n, full[1]),
                )
                found["proj"].append((2 * chip + source) * rows + place % rows)
                found["heads"].append(source * half + place % half)
                short = lambda chip: (chip >> (PAIR + 1) << PAIR) + chip % (1 << PAIR)
                owner = me ^ spread(chips, most[core])
                found["units"].append(short(owner)[col // units] * units + col % units)
                side = (me >> PAIR) & 1
                low = 1 << PAIR
                found["owners"].append(chips // low * 2 * low + side * low + chips % low)
                found["chips"].append(me ^ spread(np.arange(n), full[core]))
        for name in names:
            setattr(self, name, np.stack(found[name]).astype(np.int32))


def live_slots(meta_ref, local, axis):
    shape = (2 * local, 1) if axis == 0 else (1, 2 * local)
    place = lax.broadcasted_iota(jnp.int32, shape, axis)
    core = meta_ref[0]
    slot = jnp.where(place < local, place + core * local, place - core * local)
    return slot < BUFFER + meta_ref[1]


def attend_kernel(meta_ref, q_ref, k_ref, v_ref, o_ref):
    live = live_slots(meta_ref, q_ref.shape[0] // 2, 1)
    outs = []
    for e in range(2):
        part = slice(e * HEAD_DIM, (e + 1) * HEAD_DIM)
        raw = dot_nt(q_ref[:, part], k_ref[:, part]) * (HEAD_DIM**-0.5)
        raw = jnp.where(live, raw, -1e30)
        expo = jnp.exp(raw - jnp.max(raw, axis=-1, keepdims=True))
        probs = expo * (1.0 / jnp.sum(expo, axis=-1, keepdims=True))
        outs.append(dot(probs.astype(b16), v_ref[:, part]))
    o_ref[...] = jnp.concatenate(outs, axis=1).astype(b16)


def attend_back_kernel(meta_ref, q_ref, k_ref, v_ref, g_ref, o_ref):
    pairs = o_ref.shape[1] // (3 * 2 * HEAD_DIM)
    live = live_slots(meta_ref, q_ref.shape[0] // 2, 0)
    scale = HEAD_DIM**-0.5
    parts = ([], [], [])
    for e in range(2):
        part = slice(e * HEAD_DIM, (e + 1) * HEAD_DIM)
        qe, ke, ve, ge = (r[:, part] for r in (q_ref, k_ref, v_ref, g_ref))
        raw = jnp.where(live, dot_nt(ke, qe) * scale, -1e30)
        expo = jnp.exp(raw - jnp.max(raw, axis=0, keepdims=True))
        probs = expo * (1.0 / jnp.sum(expo, axis=0, keepdims=True))
        d_probs = dot_nt(ve, ge)
        inner = jnp.sum(probs * d_probs, axis=0, keepdims=True)
        d_scores = (probs * (d_probs - inner)).astype(b16)
        parts[0].append(dot_tn(d_scores, ke) * scale)
        parts[1].append(dot(d_scores, qe) * scale)
        parts[2].append(dot(probs.astype(b16), ge))
    for which in range(3):
        at = pl.multiple_of((which * pairs + pl.program_id(0)) * 2 * HEAD_DIM, 2 * HEAD_DIM)
        o_ref[:, pl.ds(at, 2 * HEAD_DIM)] = jnp.concatenate(parts[which], axis=1).astype(b16)


def attention(mixed, meta, grad=None):
    slots, wide = mixed.shape
    pairs = wide // (3 * 2 * HEAD_DIM)
    block = (slots, 2 * HEAD_DIM)
    spec = lambda first: pl.BlockSpec(block, lambda h, m, f=first: (0, f + h))
    specs = [spec(0), spec(pairs), spec(2 * pairs)]
    dots = 2 * pairs * 2 * slots * slots * HEAD_DIM
    if grad is None:
        kernel, extra, out_wide, out_spec, count = attend_kernel, (), wide // 3, spec(0), 2
    else:
        kernel, extra, out_wide, count = attend_back_kernel, (grad,), wide, 5
        specs.append(spec(0))
        out_spec = pl.BlockSpec((slots, wide), lambda h, m: (0, 0))
    return pl.pallas_call(
        kernel,
        out_shape=jax.ShapeDtypeStruct((slots, out_wide), b16),
        grid_spec=pltpu.PrefetchScalarGridSpec(
            num_scalar_prefetch=1, grid=(pairs,), in_specs=specs, out_specs=out_spec
        ),
        cost_estimate=pl.CostEstimate(
            flops=4 * count * dots, bytes_accessed=4 * mixed.size, transcendentals=0
        ),
    )(meta, mixed, mixed, mixed, *extra)


def plain_body(
    inputs,
    cotangent,
    kept_counts,
    norm1_gain,
    norm1_bias,
    qkv_weight,
    qv_bias,
    proj_weight,
    proj_bias,
    norm2_gain,
    norm2_bias,
    fc1_weight,
    fc1_bias,
    fc2_weight,
    fc2_bias,
):
    images, local, width = inputs.shape
    n = lax.axis_size("img")
    me = lax.axis_index("img")
    core = lax.axis_index("seq")
    levels = n.bit_length() - 1
    half = width // 2
    rows = width // (2 * n)
    units = fc2_weight.shape[0]
    few = n // 2
    hidden = units * few
    low = 1 << PAIR
    side = (me >> PAIR) & 1

    full = tuple(tuple(range(levels - 1, 1, -1)) + last for last in ((0, 1), (1, 0)))
    most = tuple(
        (first,) + tuple(b for b in range(levels - 1, 1, -1) if b != PAIR) + (1 - first,)
        for first in (0, 1)
    )

    table = Places(n, width, units, full, most)
    dev = 2 * me + core
    pick = lambda rows_of: lax.dynamic_index_in_dim(jnp.asarray(rows_of), dev, 0, False)

    mine_of = lambda a, axis: lax.dynamic_index_in_dim(a, core, axis, False)
    theirs_of = lambda a, axis: lax.dynamic_index_in_dim(a, 1 - core, axis, False)
    smalls = (norm1_gain, norm1_bias, qv_bias, proj_bias, norm2_gain, norm2_bias, fc1_bias, fc2_bias)
    ends = [0]
    for item in smalls:
        ends.append(ends[-1] + item.shape[0])
    pair = (PAIR, PAIR)
    qkv_cut = qkv_weight.reshape(rows, 3, 2, half)
    qkv_got = core_swap(theirs_of(qkv_cut, 2))
    qkv_block = jnp.concatenate([mine_of(qkv_cut, 2), qkv_got], axis=0)
    qkv = Gather(qkv_block.reshape(2 * rows, 3 * half), full)
    x_other = core_swap(inputs)
    q_got = [qkv.step()]

    small_own = jnp.concatenate(smalls)
    small_other = core_swap(small_own)
    small = jnp.where(
        core == 0, jnp.stack([small_own, small_other]), jnp.stack([small_other, small_own])
    )
    small = Gather(small, full)
    small.step(qkv_got)

    fc1_cut = after(fc1_weight, qkv_got).reshape(rows, few // low, 2, low, 2, units)
    fc1_got = core_swap(theirs_of(fc1_cut, 4))
    fc1_block = jnp.stack([mine_of(fc1_cut, 4), fc1_got])
    side_of = lambda which: lax.dynamic_index_in_dim(fc1_block, which, 3, False)
    fc1_block = jnp.stack([side_of(side), bit_swap(side_of(1 - side), pair)])
    fc1 = Gather(fc1_block.reshape(4 * rows, hidden), most)
    fc2 = Gather(fc2_weight, most)

    q_got.append(qkv.step())
    small.step(q_got[0])
    fc2_got = fc2.step(q_got[0])
    while len(qkv.steps) > 2:
        q_got.append(qkv.step())
        small.step(q_got[-2])
    qkv.step()
    q_got.append(qkv.got)
    small.step(q_got[-2])
    proj = Gather(proj_weight, full)
    proj_got = proj.step(q_got[-2])
    fc1_first = fc1.step(fc2_got)
    qkv.step()
    q_got.append(qkv.got)
    small.step(q_got[-2])
    while len(proj.steps) > 2:
        proj_got = proj.step(q_got[-2])
    slot = core * local + lax.iota(jnp.int32, local)
    row_live = [(slot < BUFFER + kept_counts[i])[:, None] for i in range(images)]

    def to_four(own, *others):
        two = jnp.concatenate([own, bit_swap(after(own, *others), pair)], axis=0)
        return jnp.concatenate([two, core_swap(two)], axis=0)

    cotangent = after(cotangent, q_got[-3])
    up_low = [jnp.where(live, c, 0).astype(b16) for live, c in zip(row_live, cotangent)]
    up_all = [to_four(u) for u in up_low]

    dev = after(dev, q_got[0])
    abs_rows = lax.iota(jnp.int32, width)
    qkv_perm = onehot(abs_rows, pick(table.qkv))
    fc1_perm = onehot(abs_rows, pick(table.fc1))
    proj_perm = onehot(pick(table.heads), pick(table.proj))
    col_perm = onehot(lax.iota(jnp.int32, hidden), pick(table.units))
    chip_perm = onehot(lax.iota(jnp.int32, n), pick(table.chips))
    unit_perm = onehot(pick(table.owners), lax.iota(jnp.int32, n))
    x_all = jnp.stack([inputs, x_other], axis=1).reshape(images * 2 * local, width)
    normed_all, _ = norm_parts(x_all.astype(f32))
    small = dot(chip_perm, small.held.reshape(n, -1)).reshape(n, 2, -1)
    gain_one, shift_one, b_qv, b_proj, gain_two, shift_two, b_fc1, b_fc2 = (
        small[:, :, a:b].reshape(-1) for a, b in zip(ends, ends[1:])
    )
    bias_fc1 = jnp.dot(
        unit_perm.astype(f32), mine_of(b_fc1.reshape(n, 2, units), 1), precision=HIGH
    ).reshape(-1)
    qv_cut = mine_of(b_qv.reshape(2, 2, half), 1)
    bias_qkv = jnp.concatenate([qv_cut[0], jnp.zeros((half,), f32), qv_cut[1]])
    first = (normed_all * gain_one + shift_one).astype(b16)
    first = dot(first, qkv_perm).astype(b16)

    w_qkv = qkv.held.reshape(width, 3 * half)
    mixed = (dot(first, w_qkv) + bias_qkv).astype(b16).reshape(images, 2 * local, 3 * half)
    metas = [jnp.stack([core.astype(jnp.int32), kept_counts[i]]) for i in range(images)]
    proj.step(q_got[-1])
    proj.step()
    w_proj = proj.held.reshape(half, width)
    w_proj = jnp.concatenate([w_proj, core_swap(w_proj)], axis=0)
    w_proj = dot(proj_perm, w_proj).astype(b16)
    fc2_got = fc2.step(q_got[-1])
    fc1_got = fc1.step(fc2_got)
    while fc2.steps:
        fc2.step()
    w_fc2 = dot(col_perm, fc2.held.reshape(hidden, width)).astype(b16)
    while fc1.steps:
        fc1.step()
    w_fc1 = dot(fc1_perm, fc1.held.reshape(width, hidden)).astype(b16)

    attended, middle, second, normed_two, scale_two = [], [], [], [], []
    for i in range(images):
        heads = attention(mixed[i], metas[i])
        heads = jnp.concatenate([heads[:local], core_swap(heads[local:])], axis=1)
        attended.append(heads)
        middle.append(inputs[i].astype(f32) + dot(heads, w_proj) + b_proj)
        normed, scale = norm_parts(middle[i])
        normed_two.append(normed)
        scale_two.append(scale)
        second.append(to_four((normed * gain_two + shift_two).astype(b16)))

    activated, slope = [], []
    for i in range(images):
        pre = dot(second[i], w_fc1) + bias_fc1
        phi = 0.5 * (1.0 + lax.erf(pre * (0.5**0.5)))
        activated.append((pre * phi).astype(b16))
        slope.append((phi + pre * jnp.exp(-0.5 * pre * pre) * 0.3989422804014327).astype(b16))

    def core_sum(part):
        return part[: 2 * local] + core_swap(part[2 * local :].astype(b16)).astype(f32)

    def pair_sum(two):
        return two[:local] + bit_swap(two[local:].astype(b16), pair).astype(f32)

    d_pre, d_two = [], []
    for i in range(images):
        d_pre.append((slope[i].astype(f32) * dot_nt(up_all[i], w_fc2)).astype(b16))
        d_two.append(core_sum(dot_nt(d_pre[i], w_fc1)))
    out_two = [core_sum(dot(activated[i], w_fc2)) for i in range(images)]
    d_second = [pair_sum(d) for d in d_two]

    cat = lambda parts: jnp.concatenate(parts, axis=0)
    cut = hidden // 2
    up_cat = cat(up_all)
    activated = after(cat(activated), *d_two)
    activated_rel = dot(activated, col_perm).astype(b16)
    grad_fc2 = Scatter(
        dot_tn(activated_rel[:, cut:], up_cat).astype(b16).reshape(-1, units, width),
        dot_tn(activated_rel[:, :cut], up_cat).reshape(-1, units, width),
        most,
    )
    second_rel = dot(cat(second), fc1_perm).astype(b16)
    d_pre_cat = cat(d_pre)
    grad_fc1 = Scatter(
        dot_tn(second_rel[:, half:], d_pre_cat).astype(b16).reshape(-1, 4 * rows, hidden),
        dot_tn(second_rel[:, :half], d_pre_cat).reshape(-1, 4 * rows, hidden),
        most,
    )
    grad_fc2.step()
    grad_fc1.step(grad_fc2.got)
    while grad_fc2.steps:
        grad_fc2.step()
    while grad_fc1.steps:
        grad_fc1.step()

    outputs = [
        jnp.where(row_live[i], middle[i] + pair_sum(after(out_two[i], *d_second)) + b_fc2, 0.0)
        for i in range(images)
    ]
    outputs = jnp.stack(outputs).astype(b16)

    d_middle, d_branch, d_mixed = [], [], []
    for i in range(images):
        back = norm_back(d_second[i], normed_two[i], scale_two[i], gain_two)
        d_middle.append(up_low[i].astype(f32) + back)
        d_branch.append(d_middle[i].astype(b16))
        d_att = dot_nt(d_branch[i], w_proj).astype(b16)
        d_att = jnp.concatenate([d_att[:, :half], core_swap(d_att[:, half:])], axis=0)
        d_mixed.append(attention(mixed[i], metas[i], d_att))

    attended_rel = dot(cat(attended), proj_perm).astype(b16)
    attended_rel = jnp.concatenate(
        [attended_rel[:, :half], core_swap(attended_rel[:, half:])], axis=0
    )
    branch = cat(d_branch)
    branch_all = jnp.concatenate([branch, core_swap(branch)], axis=0)
    parts = lambda a: a.reshape(-1, rows, a.shape[-1])
    proj_send = dot_tn(attended_rel[:, half // 2 :], branch_all).astype(b16)
    proj_keep = dot_tn(attended_rel[:, : half // 2], branch_all)
    grad_proj = Scatter(parts(proj_send), parts(proj_keep), full)
    while grad_proj.steps:
        grad_proj.step()

    d_mixed = cat(d_mixed)
    qkv_send = dot_tn(first[:, half:], d_mixed).astype(b16)
    d_first = dot_nt(dot_nt(after(d_mixed, qkv_send), w_qkv).astype(b16), qkv_perm).astype(b16)
    d_first = d_first.reshape(images, 2, local, width)
    d_first = d_first[:, 0].astype(f32) + core_swap(d_first[:, 1]).astype(f32)
    qkv_keep = dot_tn(first[:, :half], after(d_mixed, d_first))
    cut3 = lambda a: a.reshape(-1, 2 * rows, 3 * half)
    grad_qkv = Scatter(cut3(qkv_send), cut3(qkv_keep), full)
    normed_one, scale_one = norm_parts(inputs.astype(f32))
    input_grad = jnp.stack(d_middle) + norm_back(d_first, normed_one, scale_one, gain_one)

    placed = lambda a, axis: jnp.stack(
        [jnp.where(core == 0, a, 0.0), jnp.where(core == 1, a, 0.0)], axis=axis
    )
    total = lambda a: jnp.sum(a.astype(f32).reshape(-1, a.shape[-1]), axis=0)
    d_mixed_sum = total(d_mixed).reshape(3, half)
    d_pre_sum = jnp.dot(
        unit_perm.astype(f32).T, total(d_pre_cat).reshape(few, units), precision=HIGH
    )
    d_second = jnp.stack(d_second)
    small_grads = (
        total(d_first * normed_one),
        total(d_first),
        placed(d_mixed_sum[::2], 1),
        total(branch),
        total(d_second * jnp.stack(normed_two)),
        total(d_second),
        placed(d_pre_sum, 1),
        total(jnp.stack(up_low)),
    )
    small_grads = jnp.concatenate([g.reshape(n, 2, -1) for g in small_grads], axis=2)
    small_grads = mine_of(small_grads, 1) + core_swap(theirs_of(small_grads, 1))
    small_grads = jnp.dot(chip_perm.astype(f32).T, small_grads, precision=HIGH)
    small_grads = small_grads[:, None]
    small_grads = Scatter(small_grads[few:], small_grads[:few], full)
    small_grads.step()
    grad_qkv.step()
    while grad_qkv.steps:
        small_grads.step(grad_qkv.got)
        grad_qkv.step()
    small_grads = small_grads.keep[0, 0]
    small_grads = [small_grads[a:b] for a, b in zip(ends, ends[1:])]
    grad_fc1, grad_fc2, grad_proj, grad_qkv = (
        g.keep[0] for g in (grad_fc1, grad_fc2, grad_proj, grad_qkv)
    )

    qkv_other = core_swap(grad_qkv[rows:])
    both = lambda own, other, which, axis: jnp.where(
        which == 0, jnp.stack([own, other], axis=axis), jnp.stack([other, own], axis=axis)
    )
    cut3 = lambda a: a.reshape(rows, 3, half)
    grad_qkv = both(cut3(grad_qkv[:rows]), cut3(qkv_other), core, 2).reshape(qkv_weight.shape)

    pair_other = bit_swap(grad_fc1[2 * rows :], pair)
    cut4 = lambda a: a.reshape(2 * rows, few // low, low, units)
    grad_fc1 = both(cut4(grad_fc1[: 2 * rows]), cut4(pair_other), side, 2)
    core_other = core_swap(grad_fc1[rows:])
    grad_fc1 = both(grad_fc1[:rows], core_other, core, 4).reshape(fc1_weight.shape)
    return (
        outputs,
        input_grad,
        small_grads[0],
        small_grads[1],
        grad_qkv,
        small_grads[2],
        grad_proj,
        small_grads[3],
        small_grads[4],
        small_grads[5],
        grad_fc1,
        small_grads[6],
        grad_fc2,
        small_grads[7],
    )


def pack_units_kernel(where_ref, w_ref, mine_ref, theirs_ref):
    wide = mine_ref.shape[2]
    units = 128
    low = 1 << PAIR
    for ref, core in ((mine_ref, where_ref[0]), (theirs_ref, 1 - where_ref[0])):
        for p in range(2):
            side = where_ref[1] ^ p
            for b in range(wide // units):
                chip = (b // low) * 2 * low + side * low + b % low
                at = pl.multiple_of((2 * chip + core) * units, units)
                ref[p, :, b * units : (b + 1) * units] = w_ref[:, pl.ds(at, units)]


def pack_units(weight, units, core, side):
    rows, hidden = weight.shape
    if units == 128:
        out = jax.ShapeDtypeStruct((2, rows, hidden // 4), weight.dtype)
        return pl.pallas_call(
            pack_units_kernel,
            out_shape=(out, out),
            in_specs=[pl.BlockSpec(memory_space=pltpu.SMEM), pl.BlockSpec(memory_space=pltpu.VMEM)],
            out_specs=(pl.BlockSpec(memory_space=pltpu.VMEM),) * 2,
        )(jnp.stack([core, side]), weight)
    low = 1 << PAIR
    cut = weight.reshape(rows, -1, 2, low, 2, units)

    def part(c, p):
        block = lax.dynamic_index_in_dim(cut, c, 4, False)
        return lax.dynamic_index_in_dim(block, p, 2, False).reshape(rows, hidden // 4)

    return tuple(jnp.stack([part(c, side), part(c, 1 - side)]) for c in (core, 1 - core))


LANES = 128
MEASURED_US = {
    "k_pack_heads": 1.6, "k_heads": 7, "k_attend": 6, "k_project": 0.1,
    "k_unpack_units": 4.5, "k_feed": 10, "k_feed_out": 3, "k_pair_send": 0.2, "k_grad_feed": 15,
    "k_middle_back": 30, "k_attend_back": 8, "k_grad_proj": 0.2, "k_grad_heads": 8.7,
    "k_first_back": 6, "k_input_back": 4.3, "k_small": 2, "k_output": 4, "k_columns": 2, "k_rows": 1.8,
}
FLOPS_PER_US = 3e9
VMEM_LIMIT = 56 * 1024 * 1024
SMALL_ROWS = 8
GAIN1, BIAS1, QV, PROJ_B, GAIN2, BIAS2, FC1_B, FC2_B = range(8)


def spread_of(position, orders, core):
    a, b = (spread(position, order) for order in orders)
    return a if a == b else jnp.where(core == 0, a, b)


def position_of(bits, orders, core):
    a, b = (
        sum((((bits >> bit) & 1) << k) for k, bit in enumerate(order)) for order in orders
    )
    return jnp.where(core == 0, a, b)


def call(kernel, out, args, grid=None, in_specs=None, out_specs=None, scratch=(), deps=(), kept=0, us=None, place=None):
    whole = pl.BlockSpec(memory_space=pltpu.VMEM)
    outs = out if isinstance(out, tuple) else (out,)
    specs = [pl.BlockSpec(memory_space=pltpu.SMEM)] + list(in_specs or [whole] * len(args))
    out_specs = out_specs if out_specs is not None else tuple(whole for _ in outs)
    extra = {} if grid is None else {"grid": grid}
    name = getattr(kernel, "func", kernel).__name__
    flops = int((us or MEASURED_US[name]) * FLOPS_PER_US)
    if deps:
        specs += [pl.BlockSpec(memory_space=pl.ANY)] * len(deps)
        inner, count = kernel, 1 + len(args)

        def kernel(*refs):
            return inner(*refs[:count], *refs[count + len(deps) :])

        extra["input_output_aliases"] = {count + k: k for k in range(kept)}
    result = pl.pallas_call(
        kernel,
        out_shape=outs,
        in_specs=specs,
        out_specs=tuple(out_specs),
        scratch_shapes=list(scratch),
        compiler_params=pltpu.CompilerParams(vmem_limit_bytes=VMEM_LIMIT),
        cost_estimate=pl.CostEstimate(flops=flops, bytes_accessed=1000, transcendentals=0),
        **extra,
    )(place, *args, *deps)
    return result if isinstance(out, tuple) else result[0]


class Order:
    def __init__(self, place):
        self.place, self.last = place, ()

    def call(self, *args, wait=(), **named):
        result = call(*args, deps=tuple(wait) + self.last, place=self.place, **named)
        found = result if isinstance(result, tuple) else (result,)
        self.last = (min(found, key=lambda a: a.size),)
        return result

    def now(self, *values):
        values = lax.optimization_barrier((*values, *self.last))
        self.last = tuple(values[len(values) - len(self.last) :])
        values = values[: len(values) - len(self.last)]
        return values if len(values) > 1 else values[0]


def tie(*values):
    return lax.optimization_barrier(values)


def shape(dims, dtype=f32):
    return jax.ShapeDtypeStruct(tuple(dims), dtype)


def aligned(index, step):
    return pl.multiple_of(index * step, step)


def k_pack_heads(place, w, small, theirs, mine):
    three = w.shape[1]
    half = three // 6
    me_core = lax.axis_index("seq")
    for ref, core in ((mine, me_core), (theirs, 1 - me_core)):
        for which in range(3):
            at = pl.multiple_of((which * 2 + core) * half, half)
            ref[:, which * half : (which + 1) * half] = w[:, pl.ds(at, half)]
        ref[:, 3 * half :] = jnp.zeros((w.shape[0], LANES), b16)
        ref[:SMALL_ROWS, 3 * half :] = small[...]


def k_heads(orders, place, sent, got, x_own, x_other, w_qkv, vectors, first, mixed, small):
    me, core, side = place[0], place[1], place[2]
    blocks, two_rows, lanes = sent.shape
    n = 2 * blocks
    rows = two_rows // 2
    three = w_qkv.shape[1]
    half = three // 3
    for p in range(n):
        block = sent if p < blocks else got
        at = p % blocks
        chip = me ^ spread_of(p, orders, core)
        for c in range(2):
            dev = 2 * chip + (core ^ c)
            part = slice(c * rows, (c + 1) * rows)
            w_qkv[pl.ds(aligned(dev, rows), rows), :] = block[at, part, :three]
            small[dev] = block[at, c * rows : c * rows + SMALL_ROWS, three:].astype(f32)

    def lane_block(first_dev, vector, size):
        total = small[first_dev, vector : vector + 1, :]
        for i in range(1, LANES // size):
            total += pltpu.roll(small[first_dev + i, vector : vector + 1, :], i * size, 1)
        return total

    width = w_qkv.shape[0]
    per = width // (2 * n)
    for row, vector in enumerate((GAIN1, BIAS1, PROJ_B, GAIN2, BIAS2, FC2_B)):
        for q in range(width // LANES):
            vectors[row : row + 1, q * LANES : (q + 1) * LANES] = lane_block(
                q * (LANES // per), vector, per
            )
    for which in range(2):
        for q in range(half // LANES):
            dev = (which * 2 + core) * (half // (2 * per)) + q * (LANES // (2 * per))
            at = which * half + q * LANES
            vectors[6:7, at : at + LANES] = lane_block(dev, QV, 2 * per)
    low = 1 << PAIR
    for b in range(n // 2):
        chip = (b // low) * 2 * low + side * low + b % low
        vectors[7:8, b * LANES : (b + 1) * LANES] = small[2 * chip + core, FC1_B : FC1_B + 1, :]

    images, local, _ = x_own.shape
    for i in range(images):
        for c, ref in enumerate((x_own, x_other)):
            normed, _ = norm_parts(ref[i].astype(f32))
            at = (2 * i + c) * local
            first[at : at + local, :] = (
                normed * vectors[0:1, :] + vectors[1:2, :]
            ).astype(b16)
    for which in range(3):
        part = slice(which * half, (which + 1) * half)
        total = dot(first[...], w_qkv[:, part])
        if which != 1:
            total += vectors[6:7, (which // 2) * half : (which // 2 + 1) * half]
        mixed[:, part] = total.astype(b16)


def k_pair_send(place, own0, got0, own1, got1, send0, send1):
    for own, got, send in ((own0, got0, send0), (own1, got1, send1)):
        send[...] = (own[...] + got[...].astype(f32)).astype(b16)


def k_output(place, middle, own, got, pair_got, vectors, out):
    images, local, _ = out.shape
    slot = place[1] * local + lax.broadcasted_iota(jnp.int32, (local, 1), 0)
    for i in range(images):
        part = slice(i * local, (i + 1) * local)
        total = middle[part, :] + vectors[5:6, :] + own[part, :]
        total += got[part, :].astype(f32) + pair_got[part, :].astype(f32)
        out[i] = jnp.where(slot < BUFFER + place[3 + i], total, 0.0).astype(b16)


def k_unpack_units(orders, place, sent, got, w_fc1, w_fc2):
    me, core = place[0], place[1]
    blocks = sent.shape[0]
    units = LANES
    rows = (sent.shape[1] - units) // 4
    low = 1 << PAIR
    for p in range(2 * blocks):
        block = sent if p < blocks else got
        at = p % blocks
        chip = me ^ spread_of(p, orders, core)
        for c2 in range(2):
            for c in range(2):
                dev = 2 * (chip ^ (c2 << PAIR)) + (core ^ c)
                k = 2 * c2 + c
                w_fc1[pl.ds(aligned(dev, rows), rows), :] = block[at, k * rows : (k + 1) * rows, :]
        short = ((chip >> (PAIR + 1)) << PAIR) + (chip & (low - 1))
        w_fc2[pl.ds(aligned(short, units), units), :] = block[at, 4 * rows :, :]


def live_of(place, image, local, axis):
    dims = (2 * local, 1) if axis == 0 else (1, 2 * local)
    at = lax.broadcasted_iota(jnp.int32, dims, axis)
    core = place[1]
    slot = jnp.where(at < local, at + core * local, at - core * local)
    return slot < BUFFER + place[3 + image]


def k_attend(image, place, q, k, v, own, other):
    local = own.shape[0]
    live = live_of(place, image, local, 1)
    outs = []
    for e in range(2):
        part = slice(e * HEAD_DIM, (e + 1) * HEAD_DIM)
        raw = dot_nt(q[:, part], k[:, part]) * (HEAD_DIM**-0.5)
        raw = jnp.where(live, raw, -1e30)
        expo = jnp.exp(raw - jnp.max(raw, axis=-1, keepdims=True))
        probs = expo * (1.0 / jnp.sum(expo, axis=-1, keepdims=True))
        outs.append(dot(probs.astype(b16), v[:, part]))
    both = jnp.concatenate(outs, axis=1).astype(b16)
    own[...] = both[:local]
    other[...] = both[local:]


def k_attend_back(image, place, q, k, v, g_own, g_other, d_mixed, sums):
    local = g_own.shape[0]
    pairs = pl.num_programs(0)
    live = live_of(place, image, local, 0)
    scale = HEAD_DIM**-0.5
    g = jnp.concatenate([g_own[...], g_other[...]], axis=0)
    parts = ([], [], [])
    for e in range(2):
        part = slice(e * HEAD_DIM, (e + 1) * HEAD_DIM)
        qe, ke, ve, ge = q[:, part], k[:, part], v[:, part], g[:, part]
        raw = jnp.where(live, dot_nt(ke, qe) * scale, -1e30)
        expo = jnp.exp(raw - jnp.max(raw, axis=0, keepdims=True))
        probs = expo * (1.0 / jnp.sum(expo, axis=0, keepdims=True))
        d_probs = dot_nt(ve, ge)
        inner = jnp.sum(probs * d_probs, axis=0, keepdims=True)
        d_scores = (probs * (d_probs - inner)).astype(b16)
        parts[0].append(dot_tn(d_scores, ke) * scale)
        parts[1].append(dot(d_scores, qe) * scale)
        parts[2].append(dot(probs.astype(b16), ge))
    for which in range(3):
        at = pl.multiple_of((which * pairs + pl.program_id(0)) * LANES, LANES)
        value = jnp.concatenate(parts[which], axis=1).astype(b16)
        d_mixed[:, pl.ds(at, LANES)] = value
        total = jnp.sum(value.astype(f32), axis=0, keepdims=True)
        sums[:, pl.ds(at, LANES)] = jnp.broadcast_to(total, (8, LANES))


def k_project(orders, place, sent, got, sent_far, got_far, own0, own1, got0, got1, x, vectors,
              w, middle, second):
    me, core = place[0], place[1]
    blocks, rows, _ = sent.shape
    for c, refs in enumerate(((sent, got), (sent_far, got_far))):
        for p in range(2 * blocks):
            chip = me ^ spread_of(p, orders, core ^ c)
            at = aligned(2 * chip + (core ^ c), rows)
            w[pl.ds(at, rows), :] = refs[p // blocks][p % blocks]
    half = own0.shape[1]
    images, local, _ = x.shape
    both = lambda a, b: jnp.concatenate([a[...], b[...]], axis=0)
    total = dot(both(own0, own1), w[pl.ds(aligned(core, half), half), :])
    total += dot(both(got0, got1), w[pl.ds(aligned(1 - core, half), half), :])
    for i in range(images):
        part = slice(i * local, (i + 1) * local)
        mid = x[i].astype(f32) + total[part] + vectors[2:3, :]
        middle[part, :] = mid
        normed, _ = norm_parts(mid)
        second[part, :] = (normed * vectors[3:4, :] + vectors[4:5, :]).astype(b16)


def k_feed(place, s0, s1, u0, u1, w1, w2, vectors, act, d_pre, ds_own, ds_other, sums, sec, up):
    images, local, _ = u0.shape
    tokens = images * local
    tile = 256
    for k, (s, u) in enumerate(((s0, u0), (s1, u1))):
        sec[k * tokens : (k + 1) * tokens, :] = s[...]
        for i in range(images):
            at = k * tokens + i * local
            up[at : at + local, :] = u[i]
    for at in range(0, w1.shape[1], tile):
        part = slice(at, at + tile)
        pre = dot(sec[...], w1[:, part]) + vectors[7:8, part]
        phi = 0.5 * (1.0 + lax.erf(pre * (0.5**0.5)))
        act[:, part] = (pre * phi).astype(b16)
        slope = phi + pre * jnp.exp(-0.5 * pre * pre) * 0.3989422804014327
        grad = (slope * dot_nt(up[...], w2[part, :])).astype(b16)
        d_pre[:, part] = grad
        total = jnp.sum(grad.astype(f32), axis=0, keepdims=True)
        sums[:, part] = jnp.broadcast_to(total, (8, tile))
    ds_other[...] = dot_nt(d_pre[tokens:, :], w1[...]).astype(b16)
    ds_own[...] = dot_nt(d_pre[:tokens, :], w1[...])


def k_feed_out(place, act, w2, own, other):
    tokens = own.shape[0]
    other[...] = dot(act[tokens:, :], w2[...]).astype(b16)
    own[...] = dot(act[:tokens, :], w2[...])


def k_middle_back(place, ds_own, ds_got, pair_got, middle, up, w, vectors,
                  d_middle, d_branch, att_own, att_other, sums):
    core = place[1]
    images, local, _ = up.shape
    half = att_own.shape[1]
    total = lambda a: jnp.sum(a, axis=0, keepdims=True)
    rows = [0.0] * 4
    for i in range(images):
        part = slice(i * local, (i + 1) * local)
        d_second = ds_own[part, :] + ds_got[part, :].astype(f32) + pair_got[part, :].astype(f32)
        normed, scale = norm_parts(middle[part, :])
        upstream = up[i].astype(f32)
        d_mid = upstream + norm_back(d_second, normed, scale, vectors[3:4, :])
        d_middle[part, :] = d_mid
        branch = d_mid.astype(b16)
        d_branch[part, :] = branch
        rows[0] += total(d_second * normed)
        rows[1] += total(d_second)
        rows[2] += total(branch.astype(f32))
        rows[3] += total(upstream)
    branch = d_branch[...]
    att_other[...] = dot_nt(branch, w[pl.ds(aligned(1 - core, half), half), :]).astype(b16)
    att_own[...] = dot_nt(branch, w[pl.ds(aligned(core, half), half), :]).astype(b16)
    for r in range(4):
        sums[r : r + 1, :] = rows[r]
    sums[4:, :] = jnp.zeros((4, sums.shape[1]), f32)


def put(held, row, value):
    held[pl.ds(pl.multiple_of(row, value.shape[0]), value.shape[0]), :] = value.astype(b16)


def split(held, send, keep):
    cut = send.shape[0]
    send[...] = held[cut:, :]
    keep[...] = held[:cut, :]


def k_grad_heads(orders, n, place, left, right, send, keep, held):
    me, core = place[0], place[1]
    tile = 256
    rows = held.shape[0] // (2 * n)
    for step in range(left.shape[1] // tile):
        total = dot_tn(left[:, step * tile : (step + 1) * tile], right[...])
        for i in range(tile // rows):
            dev = step * (tile // rows) + i
            at = position_of(me ^ (dev // 2), orders, core)
            value = total[i * rows : (i + 1) * rows, :]
            put(held, at * 2 * rows + (core ^ (dev % 2)) * rows, value)
    split(held, send, keep)


def k_grad_feed(orders, n, place, a0, a1, u0, u1, s0, s1, d0, d1, send, keep, held):
    me, core, side = place[0], place[1], place[2]
    low = 1 << PAIR
    tile = 256
    per = 2 * send.shape[0] // (n // 2)
    rows = (per - LANES) // 4
    for step in range(a0.shape[1] // tile):
        part = slice(step * tile, (step + 1) * tile)
        total = dot_tn(a0[:, part], u0[...]) + dot_tn(a1[:, part], u1[...])
        for i in range(tile // LANES):
            b = step * (tile // LANES) + i
            chip = (b // low) * 2 * low + side * low + b % low
            at = position_of(me ^ chip, orders, core)
            put(held, at * per, total[i * LANES : (i + 1) * LANES, :])
    for step in range(s0.shape[1] // tile):
        part = slice(step * tile, (step + 1) * tile)
        total = dot_tn(s0[:, part], d0[...]) + dot_tn(s1[:, part], d1[...])
        for i in range(tile // rows):
            dev = step * (tile // rows) + i
            bits = me ^ (dev // 2)
            at = position_of(bits, orders, core)
            inner = LANES + (((bits >> PAIR) & 1) * 2 + (core ^ (i % 2))) * rows
            put(held, at * per + inner, total[i * rows : (i + 1) * rows, :])
    split(held, send, keep)


def k_grad_proj(orders, place, *refs):
    lefts, rights, (send, keep, held) = (refs[:4], refs[4:8]), refs[8:10], refs[10:]
    me, core = place[0], place[1]
    rows = 32
    right = jnp.concatenate([a[...] for a in rights], axis=0)
    count = lefts[0][0].shape[1] // (2 * rows)
    for which in range(2):
        left = jnp.concatenate([a[...] for a in lefts[which]], axis=0)
        total = dot_tn(left, right)
        for i in range(count):
            chip = (core ^ which) * count + i
            at = position_of(me ^ chip, orders, core)
            value = jnp.where(
                core == 0,
                total[2 * i * rows : (2 * i + 1) * rows, :],
                total[(2 * i + 1) * rows : (2 * i + 2) * rows, :],
            )
            put(held, at * rows, value)
    split(held, send, keep)


def k_first_back(place, d, w, own, other):
    images, local, width = own.shape
    tile = 256
    for step in range(width // tile):
        part = slice(step * tile, (step + 1) * tile)
        total = dot_nt(d[...], w[part, :])
        for i in range(images):
            at = 2 * i * local
            own[i, :, part] = total[at : at + local]
            other[i, :, part] = total[at + local : at + 2 * local].astype(b16)


def k_input_back(place, x, own, got, mid, vectors, grad, sums):
    total = lambda a: jnp.sum(a, axis=0, keepdims=True)
    images, local, _ = x.shape
    gains = biases = 0.0
    for i in range(images):
        normed, scale = norm_parts(x[i].astype(f32))
        d_first = own[i] + got[i].astype(f32)
        back = norm_back(d_first, normed, scale, vectors[0:1, :])
        grad[i] = mid[i * local : (i + 1) * local, :] + back
        gains += total(d_first * normed)
        biases += total(d_first)
    sums[0:1, :] = gains
    sums[1:2, :] = biases
    sums[2:, :] = jnp.zeros((6, sums.shape[1]), f32)


def k_small(orders, n, place, one, mids, pre0, pre1, mix, mine, theirs, small):
    me, core, side = place[0], place[1], place[2]
    width = one.shape[1]
    per = width // (2 * n)
    half = width // 2
    pres = pre0[...] + pre1[...]
    mixes = mix[:8, :] + mix[8:, :]
    small[...] = jnp.zeros(small.shape, f32)
    rows = (
        (GAIN1, one[0:1, :]),
        (BIAS1, one[1:2, :]),
        (GAIN2, mids[0:1, :]),
        (BIAS2, mids[1:2, :]),
        (PROJ_B, mids[2:3, :]),
        (FC2_B, mids[3:4, :]),
    )
    lane = lambda row, q: row[:, q * LANES : (q + 1) * LANES]
    for vector, row in rows:
        for dev in range(2 * n):
            q, i = divmod(dev * per, LANES)
            part = lane(row, q)
            small[dev, vector : vector + 1, :] = part if i == 0 else pltpu.roll(part, LANES - i, 1)
    for which in range(2):
        row = mixes[0:1, 2 * which * half : (2 * which + 1) * half]
        for dev in range(half // (2 * per)):
            q, i = divmod(dev * 2 * per, LANES)
            part = lane(row, q)
            part = part if i == 0 else pltpu.roll(part, LANES - i, 1)
            small[(2 * which + core) * (half // (2 * per)) + dev, QV : QV + 1, :] = part
    low = 1 << PAIR
    for b in range(n // 2):
        chip = (b // low) * 2 * low + side * low + b % low
        small[2 * chip + core, FC1_B : FC1_B + 1, :] = lane(pres[0:1, :], b)
    for p in range(n):
        mine[p] = small[2 * (me ^ spread_of(p, orders, core)) + core]
        theirs[p] = small[2 * (me ^ spread_of(p, orders, 1 - core)) + 1 - core]


def k_rows(place, own, got, out):
    core = place[1]
    half = out.shape[1] // 6
    for which in range(3):
        part = slice(which * half, (which + 1) * half)
        at = pl.multiple_of((2 * which + core) * half, half)
        out[:, pl.ds(at, half)] = own[: out.shape[0], part]
        at = pl.multiple_of((2 * which + 1 - core) * half, half)
        out[:, pl.ds(at, half)] = got[:, part]


def k_columns(place, own, own_pair, got, got_pair, out):
    core, side = place[1], place[2]
    low = 1 << PAIR
    rows = out.shape[0]
    for ref, c, s in (
        (own, core, side),
        (own_pair, core, 1 - side),
        (got, 1 - core, side),
        (got_pair, 1 - core, 1 - side),
    ):
        for b in range(ref.shape[1] // LANES):
            chip = (b // low) * 2 * low + s * low + b % low
            at = pl.multiple_of((2 * chip + c) * LANES, LANES)
            out[:, pl.ds(at, LANES)] = ref[:rows, b * LANES : (b + 1) * LANES]


class Sums:
    def __init__(self, run, send, keep, orders):
        self.run, self.send, self.keep, self.got = run, send, keep, None
        self.steps = list(zip(*orders))[::-1]
        self.step()

    def settle(self):
        got = self.run.now(self.got)
        cut = got.shape[0] // 2
        if cut:
            total = self.keep[cut:].astype(f32) + got[cut:].astype(f32)
            self.send = total.astype(self.send.dtype)
            self.keep = self.keep[:cut].astype(f32) + got[:cut].astype(f32)
        else:
            self.keep = self.keep.astype(f32) + got.astype(f32)
        self.got = None

    def step(self):
        if self.got is not None:
            self.settle()
        self.got = bit_swap(self.send, self.steps.pop(0))

    def sum(self):
        while self.steps:
            self.step()
        self.settle()
        return self.keep[0]


def fast_body(
    inputs,
    cotangent,
    kept_counts,
    norm1_gain,
    norm1_bias,
    qkv_weight,
    qv_bias,
    proj_weight,
    proj_bias,
    norm2_gain,
    norm2_bias,
    fc1_weight,
    fc1_bias,
    fc2_weight,
    fc2_bias,
):
    images, local, width = inputs.shape
    n = lax.axis_size("img")
    me = lax.axis_index("img")
    core = lax.axis_index("seq")
    levels = n.bit_length() - 1
    half = width // 2
    rows = width // (2 * n)
    units = fc2_weight.shape[0]
    few = n // 2
    hidden = units * few
    side = (me >> PAIR) & 1
    pair = (PAIR, PAIR)
    full = tuple(tuple(range(levels - 1, 1, -1)) + last for last in ((0, 1), (1, 0)))
    most = tuple(tuple(b for b in order if b != PAIR) for order in full)
    last = tuple(order[-2:] + order[:-2] for order in full)
    place = jnp.concatenate([jnp.stack([me, core, side]).astype(jnp.int32), kept_counts])
    run = Order(place)
    on = run.call
    bind = functools.partial
    block = lambda dims, index: pl.BlockSpec(dims, index)
    whole = pl.BlockSpec(memory_space=pltpu.VMEM)

    smalls = (norm1_gain, norm1_bias, qv_bias, proj_bias, norm2_gain, norm2_bias, fc1_bias, fc2_bias)
    small = sum(
        jnp.pad(a[None], ((i, 7 - i), (0, LANES - a.shape[0]))) for i, a in enumerate(smalls)
    )
    packed = shape((rows, 3 * half + LANES), b16)
    theirs, mine = call(k_pack_heads, (packed, packed), (qkv_weight, small), place=kept_counts)
    fc1_mine, fc1_theirs = pack_units(fc1_weight, units, core, side)
    heads = Gather(jnp.concatenate([mine, core_swap(theirs)], axis=0), full)
    fc1_got = core_swap(fc1_theirs)
    x_other = core_swap(inputs)
    slot = core * local + lax.iota(jnp.int32, local)
    row_live = slot[None, :] < BUFFER + kept_counts[:, None]
    up = jnp.where(row_live[:, :, None], cotangent, 0).astype(b16)
    up_other = core_swap(up)
    fc1_send = jnp.concatenate([fc1_mine[1], fc1_got[1]], axis=0)
    proj = Gather(proj_weight, last)

    heads.step()
    fc1_pair = bit_swap(fc1_send, pair)
    heads.held, proj.held, fc1_pair, x_other, up_other = tie(
        heads.held, proj.held, fc1_pair, x_other, up_other
    )
    heads.step()
    proj.step()
    feed = Gather(jnp.concatenate([fc1_mine[0], fc1_got[0], fc1_pair, fc2_weight], axis=0), most)
    heads.held, proj.held, feed.held = tie(heads.held, proj.held, feed.held)
    while len(heads.steps) > 1:
        heads.step()
    proj.step()
    heads.held, proj.held, feed.held = tie(heads.held, proj.held, feed.held)
    heads.step()
    feed.step()
    heads.got, feed.held, proj.held = tie(heads.got, feed.held, proj.held)
    feed.step()
    proj.step()

    tokens = images * 2 * local
    w_qkv, vectors, first, mixed = on(
        bind(k_heads, full),
        (
            shape((width, 3 * half), b16),
            shape((8, width)),
            shape((tokens, width), b16),
            shape((tokens, 3 * half), b16),
        ),
        (heads.sent, heads.got, inputs, x_other),
        scratch=[pltpu.VMEM((2 * n, SMALL_ROWS, LANES), f32)],
    )
    pairs = half // LANES
    slots = 2 * local
    head_specs = lambda i: [
        block((slots, LANES), lambda h, i=i, f=f: (i, f + h)) for f in (0, pairs, 2 * pairs)
    ]
    lane_spec = block((local, LANES), lambda h: (0, h))
    tok = images * local
    flat = lambda cols, dtype=f32: shape((tok, cols), dtype)
    att_own, att_other, att_got = [], [], []
    for i in range(images):
        own, other = on(
            bind(k_attend, i),
            (shape((local, half), b16),) * 2,
            (mixed, mixed, mixed),
            grid=(pairs,),
            in_specs=head_specs(i),
            out_specs=[lane_spec, lane_spec],
        )
        att_own.append(own)
        att_other.append(other)
        att_got.append(core_swap(other))
        if i == 0:
            proj.got, feed.got = run.now(proj.got, feed.got)
            proj.held = jnp.concatenate([proj.sent, proj.got], axis=0)
            feed.held = jnp.concatenate([feed.sent, feed.got], axis=0)
            feed.step()
            proj.step()
            proj_sent_far = core_swap(proj.sent)
    proj.got, up = run.now(proj.got, up)
    up_pair = bit_swap(up, pair)
    proj_far = proj_sent_far, core_swap(proj.got)
    w_proj, middle, second = on(
        bind(k_project, last),
        (shape((width, width), b16), flat(width), flat(width, b16)),
        (proj.sent, proj.got, *proj_far, *att_own, *att_got, inputs, vectors),
    )
    second_other = core_swap(second)
    second_pair = bit_swap(second, pair)
    w_fc1, w_fc2 = on(
        bind(k_unpack_units, most),
        (shape((width, hidden), b16), shape((hidden, width), b16)),
        (feed.sent, feed.got),
    )
    up_pair = run.now(up_pair)
    up_other_pair = core_swap(up_pair)
    tile = 256
    fixed = lambda dims: block(dims, lambda *_: (0,) * len(dims))
    wide_rows = lambda cols: shape((2 * tok, cols), b16)
    feed_shapes = (
        wide_rows(hidden), wide_rows(hidden), flat(width), flat(width, b16), shape((8, hidden)),
        wide_rows(width), wide_rows(width),
    )
    feeds = []
    feeds.append(
        on(k_feed, feed_shapes, (second, second_other, up, up_other, w_fc1, w_fc2, vectors))
    )
    second_pair = run.now(second_pair)
    second_other_pair = core_swap(second_pair)
    feeds.append(
        on(
            k_feed,
            feed_shapes,
            (second_pair, second_other_pair, up_pair, up_other_pair, w_fc1, w_fc2, vectors),
        )
    )
    ds_pair_got = core_swap(feeds[1][3])
    out_shapes = (flat(width), flat(width, b16))
    out_pair_own, out_pair_other = on(k_feed_out, out_shapes, (feeds[1][0], w_fc2))
    out_pair_got = core_swap(out_pair_other)

    acts = [f[0] for f in feeds]
    d_pres = [f[1] for f in feeds]
    ds_send, out_send = on(
        k_pair_send,
        (flat(width, b16),) * 2,
        (feeds[1][2], ds_pair_got, out_pair_own, out_pair_got),
    )
    pair_got = bit_swap(ds_send, pair)
    ds_got = core_swap(run.now(feeds[0][3]))
    halves = lambda count, cols: (shape((count, cols), b16), shape((count, cols), b16))
    held = lambda count, cols: [pltpu.VMEM((2 * count, cols), b16)]
    cut = lambda a, per: a.reshape(-1, per, a.shape[-1])
    feed_send, feed_keep = on(
        bind(k_grad_feed, most, n),
        halves(few // 2 * (4 * rows + units), width),
        (*acts, *[f[6] for f in feeds], *[f[5] for f in feeds], *d_pres),
        scratch=held(few // 2 * (4 * rows + units), width),
    )
    grad_feed = Sums(run, cut(feed_send, 4 * rows + units), cut(feed_keep, 4 * rows + units), most)

    out_pair = bit_swap(run.now(out_send), pair)
    d_middle, d_branch, d_att, d_att_other, mid_sums = on(
        k_middle_back,
        (flat(width), flat(width, b16), flat(half, b16), flat(half, b16), shape((8, width))),
        (feeds[0][2], ds_got, pair_got, middle, up, w_proj, vectors),
    )
    d_att_got = core_swap(d_att_other)
    att_far, d_branch_far = [core_swap(a) for a in att_own], core_swap(d_branch)
    d_mixed, mix_sums = (), ()
    for i in range(images):
        part = block((local, LANES), lambda h, i=i: (i, h))
        d_mixed, mix_sums = on(
            bind(k_attend_back, i),
            (shape((tokens, 3 * half), b16), shape((8 * images, 3 * half))),
            (mixed, mixed, mixed, d_att, d_att_got),
            grid=(pairs,),
            in_specs=head_specs(i) + [part, part],
            out_specs=[
                block((slots, 3 * half), lambda h, i=i: (i, 0)),
                block((8, 3 * half), lambda h, i=i: (i, 0)),
            ],
            wait=(d_mixed, mix_sums) if i > 0 else (),
            kept=2 if i > 0 else 0,
            us=8 if i > 0 else 0.2,
        )
        if i == 0:
            proj_send, proj_keep = on(
                bind(k_grad_proj, full),
                halves(half // 2, width),
                (*att_own, *att_other, *att_got, *att_far, d_branch, d_branch_far),
                scratch=held(half // 2, width),
            )
            grad_proj = Sums(run, cut(proj_send, rows), cut(proj_keep, rows), full)
            grad_feed.step()
    qkv_send, qkv_keep = on(
        bind(k_grad_heads, full, n),
        halves(half, 3 * half),
        (first, d_mixed),
        scratch=held(half, 3 * half),
    )
    grad_qkv = Sums(run, cut(qkv_send, 2 * rows), cut(qkv_keep, 2 * rows), full)
    grad_feed.step()
    grad_proj.step()
    df_own, df_other = on(
        k_first_back,
        (shape(inputs.shape), shape(inputs.shape, b16)),
        (d_mixed, w_qkv),
    )
    df_got = core_swap(df_other)
    out_own, out_other = on(k_feed_out, out_shapes, (acts[0], w_fc2))
    out_got = core_swap(run.now(out_other))
    grad_qkv.step()
    grad_proj.step()
    input_grad, one_sums = on(
        k_input_back,
        (shape(inputs.shape), shape((8, width))),
        (inputs, df_own, df_got, d_middle, vectors),
    )
    small_shape = shape((n, SMALL_ROWS, LANES))
    small_mine, small_theirs = on(
        bind(k_small, full, n),
        (small_shape, small_shape),
        (one_sums, mid_sums, feeds[0][4], feeds[1][4], mix_sums),
        scratch=[pltpu.VMEM((2 * n, SMALL_ROWS, LANES), f32)],
    )
    small_got = core_swap(small_theirs)
    grad_feed = grad_feed.sum()
    grad_fc2, fc1_own = grad_feed[:units], grad_feed[units:]
    small_sum = small_mine + run.now(small_got)
    small_sums = Sums(run, small_sum[few:], small_sum[:few], full)
    grad_qkv.step()
    small_sums.step()
    grad_qkv.step()
    grad_proj.step()
    fc1_from = bit_swap(fc1_own[2 * rows :], pair)
    fc1_core = core_swap(fc1_own[rows : 2 * rows])
    small_sums.step()
    outputs = on(k_output, shape(inputs.shape, b16), (middle, out_own, out_got, out_pair, vectors))
    small_sums.step()
    fc1_from = run.now(fc1_from)
    fc1_from_core = core_swap(fc1_from[rows:])
    grad_proj = grad_proj.sum()
    fc1_rows = on(
        k_columns, shape(fc1_weight.shape), (fc1_own, fc1_from, fc1_core, fc1_from_core)
    )
    small_sums.settle()

    final = small_sums.keep[0]
    vector_grads = [final[v, : a.shape[0]] for v, a in enumerate(smalls)]
    qkv_own = grad_qkv.sum()
    qkv_rows = on(
        k_rows, shape((rows, 6 * half)), (qkv_own, core_swap(qkv_own[rows:]))
    )
    return (
        outputs,
        input_grad,
        vector_grads[GAIN1],
        vector_grads[BIAS1],
        qkv_rows,
        vector_grads[QV],
        grad_proj,
        vector_grads[PROJ_B],
        vector_grads[GAIN2],
        vector_grads[BIAS2],
        fc1_rows,
        vector_grads[FC1_B],
        grad_fc2,
        vector_grads[FC2_B],
    )


def body(*args):
    whole_tiles = args[3].shape[0] % 32 == 0 and args[12].shape[0] == LANES
    return (fast_body if whole_tiles else plain_body)(*args)


def solution(mesh):
    row = P(("img", "seq"))
    mat = P(("img", "seq"), None)
    act = P("img", "seq", None)
    return jax.shard_map(
        body,
        mesh=mesh,
        in_specs=(act, act, P("img"), row, row, mat, row, mat, row, row, row, mat, row, mat, row),
        out_specs=(act, act, row, row, mat, row, mat, row, row, row, mat, row, mat, row),
        check_vma=False,
    )
```

```python
import functools

import jax
import jax.numpy as jnp
import numpy as np
from jax import lax
from jax.experimental import pallas as pl
from jax.experimental.pallas import tpu as pltpu
from jax.sharding import PartitionSpec as P

HEAD_DIM = 64
BUFFER = 64
PAIR = 2
f32 = jnp.float32
b16 = jnp.bfloat16
HIGH = lax.Precision.HIGHEST


def dot(left, right):
    return jnp.dot(left, right, preferred_element_type=f32)


def dot_tn(left, right):
    return lax.dot_general(left, right, (((0,), (0,)), ((), ())), preferred_element_type=f32)


def dot_nt(left, right):
    return lax.dot_general(left, right, (((1,), (1,)), ((), ())), preferred_element_type=f32)


def norm_parts(values):
    centre = values - jnp.mean(values, axis=-1, keepdims=True)
    scale = lax.rsqrt(jnp.mean(centre * centre, axis=-1, keepdims=True) + 1e-06)
    return centre * scale, scale


def norm_back(grad, normed, scale, gain):
    e = grad * gain
    return scale * (
        e
        - jnp.mean(e, axis=-1, keepdims=True)
        - normed * jnp.mean(e * normed, axis=-1, keepdims=True)
    )


def core_swap(value):
    return lax.ppermute(value, "seq", [(0, 1), (1, 0)])


def bit_swap(value, bits):
    n = lax.axis_size("img")
    pairs = [
        (2 * j + c, 2 * (j ^ (1 << bits[c])) + c) for j in range(n) for c in range(2)
    ]
    return lax.ppermute(value, ("img", "seq"), pairs)


def after(value, *others):
    return lax.optimization_barrier((value, *others))[0]


class Gather:
    def __init__(self, block, orders):
        self.held = None if block is None else block[None]
        self.steps = list(zip(*orders))

    def step(self, *others):
        self.sent = after(self.held, *others) if others else self.held
        self.got = bit_swap(self.sent, self.steps.pop(0))
        self.held = jnp.concatenate([self.sent, self.got], axis=0)
        return self.got


class Scatter:
    def __init__(self, send, keep, orders):
        self.send, self.keep = send, keep
        self.steps = list(zip(*orders))[::-1]

    def step(self, *others):
        send = after(self.send, *others) if others else self.send
        self.got = bit_swap(send, self.steps.pop(0))
        total = self.keep + self.got.astype(f32)
        cut = total.shape[0] // 2
        if cut:
            self.send = total[cut:].astype(send.dtype)
        self.keep = total[: max(cut, 1)]


def spread(position, order):
    return sum((((position >> k) & 1) << bit) for k, bit in enumerate(order))


def onehot(left, right):
    return (left[:, None] == right[None, :]).astype(b16)


class Places:
    def __init__(self, n, width, units, full, most):
        rows, half, few = width // (2 * n), width // 2, n // 2
        place, chips = np.arange(width), np.arange(few)
        col = np.arange(few * units)
        names = ("qkv", "fc1", "proj", "heads", "units", "chips", "owners")
        found = {name: [] for name in names}
        for me in range(n):
            for core in range(2):
                chip = me ^ spread(place // (2 * rows), full[core])
                found["qkv"].append((2 * chip + (core ^ (place // rows % 2))) * rows + place % rows)
                chip = me ^ spread(place // (4 * rows), most[core])
                chip = chip ^ ((place // (2 * rows) % 2) << PAIR)
                found["fc1"].append((2 * chip + (core ^ (place // rows % 2))) * rows + place % rows)
                source = core ^ (place // half)
                chip = me ^ np.where(
                    source == 0,
                    spread(place // rows % n, full[0]),
                    spread(place // rows % n, full[1]),
                )
                found["proj"].append((2 * chip + source) * rows + place % rows)
                found["heads"].append(source * half + place % half)
                short = lambda chip: (chip >> (PAIR + 1) << PAIR) + chip % (1 << PAIR)
                owner = me ^ spread(chips, most[core])
                found["units"].append(short(owner)[col // units] * units + col % units)
                side = (me >> PAIR) & 1
                low = 1 << PAIR
                found["owners"].append(chips // low * 2 * low + side * low + chips % low)
                found["chips"].append(me ^ spread(np.arange(n), full[core]))
        for name in names:
            setattr(self, name, np.stack(found[name]).astype(np.int32))


def live_slots(meta_ref, local, axis):
    shape = (2 * local, 1) if axis == 0 else (1, 2 * local)
    place = lax.broadcasted_iota(jnp.int32, shape, axis)
    core = meta_ref[0]
    slot = jnp.where(place < local, place + core * local, place - core * local)
    return slot < BUFFER + meta_ref[1]


def attend_kernel(meta_ref, q_ref, k_ref, v_ref, o_ref):
    live = live_slots(meta_ref, q_ref.shape[0] // 2, 1)
    outs = []
    for e in range(2):
        part = slice(e * HEAD_DIM, (e + 1) * HEAD_DIM)
        raw = dot_nt(q_ref[:, part], k_ref[:, part]) * (HEAD_DIM**-0.5)
        raw = jnp.where(live, raw, -1e30)
        expo = jnp.exp(raw - jnp.max(raw, axis=-1, keepdims=True))
        probs = expo * (1.0 / jnp.sum(expo, axis=-1, keepdims=True))
        outs.append(dot(probs.astype(b16), v_ref[:, part]))
    o_ref[...] = jnp.concatenate(outs, axis=1).astype(b16)


def attend_back_kernel(meta_ref, q_ref, k_ref, v_ref, g_ref, o_ref):
    pairs = o_ref.shape[1] // (3 * 2 * HEAD_DIM)
    live = live_slots(meta_ref, q_ref.shape[0] // 2, 0)
    scale = HEAD_DIM**-0.5
    parts = ([], [], [])
    for e in range(2):
        part = slice(e * HEAD_DIM, (e + 1) * HEAD_DIM)
        qe, ke, ve, ge = (r[:, part] for r in (q_ref, k_ref, v_ref, g_ref))
        raw = jnp.where(live, dot_nt(ke, qe) * scale, -1e30)
        expo = jnp.exp(raw - jnp.max(raw, axis=0, keepdims=True))
        probs = expo * (1.0 / jnp.sum(expo, axis=0, keepdims=True))
        d_probs = dot_nt(ve, ge)
        inner = jnp.sum(probs * d_probs, axis=0, keepdims=True)
        d_scores = (probs * (d_probs - inner)).astype(b16)
        parts[0].append(dot_tn(d_scores, ke) * scale)
        parts[1].append(dot(d_scores, qe) * scale)
        parts[2].append(dot(probs.astype(b16), ge))
    for which in range(3):
        at = pl.multiple_of((which * pairs + pl.program_id(0)) * 2 * HEAD_DIM, 2 * HEAD_DIM)
        o_ref[:, pl.ds(at, 2 * HEAD_DIM)] = jnp.concatenate(parts[which], axis=1).astype(b16)


def attention(mixed, meta, grad=None):
    slots, wide = mixed.shape
    pairs = wide // (3 * 2 * HEAD_DIM)
    block = (slots, 2 * HEAD_DIM)
    spec = lambda first: pl.BlockSpec(block, lambda h, m, f=first: (0, f + h))
    specs = [spec(0), spec(pairs), spec(2 * pairs)]
    dots = 2 * pairs * 2 * slots * slots * HEAD_DIM
    if grad is None:
        kernel, extra, out_wide, out_spec, count = attend_kernel, (), wide // 3, spec(0), 2
    else:
        kernel, extra, out_wide, count = attend_back_kernel, (grad,), wide, 5
        specs.append(spec(0))
        out_spec = pl.BlockSpec((slots, wide), lambda h, m: (0, 0))
    return pl.pallas_call(
        kernel,
        out_shape=jax.ShapeDtypeStruct((slots, out_wide), b16),
        grid_spec=pltpu.PrefetchScalarGridSpec(
            num_scalar_prefetch=1, grid=(pairs,), in_specs=specs, out_specs=out_spec
        ),
        cost_estimate=pl.CostEstimate(
            flops=4 * count * dots, bytes_accessed=4 * mixed.size, transcendentals=0
        ),
    )(meta, mixed, mixed, mixed, *extra)


def plain_body(
    inputs,
    cotangent,
    kept_counts,
    norm1_gain,
    norm1_bias,
    qkv_weight,
    qv_bias,
    proj_weight,
    proj_bias,
    norm2_gain,
    norm2_bias,
    fc1_weight,
    fc1_bias,
    fc2_weight,
    fc2_bias,
):
    images, local, width = inputs.shape
    n = lax.axis_size("img")
    me = lax.axis_index("img")
    core = lax.axis_index("seq")
    levels = n.bit_length() - 1
    half = width // 2
    rows = width // (2 * n)
    units = fc2_weight.shape[0]
    few = n // 2
    hidden = units * few
    low = 1 << PAIR
    side = (me >> PAIR) & 1

    full = tuple(tuple(range(levels - 1, 1, -1)) + last for last in ((0, 1), (1, 0)))
    most = tuple(
        (first,) + tuple(b for b in range(levels - 1, 1, -1) if b != PAIR) + (1 - first,)
        for first in (0, 1)
    )

    table = Places(n, width, units, full, most)
    dev = 2 * me + core
    pick = lambda rows_of: lax.dynamic_index_in_dim(jnp.asarray(rows_of), dev, 0, False)

    mine_of = lambda a, axis: lax.dynamic_index_in_dim(a, core, axis, False)
    theirs_of = lambda a, axis: lax.dynamic_index_in_dim(a, 1 - core, axis, False)
    smalls = (norm1_gain, norm1_bias, qv_bias, proj_bias, norm2_gain, norm2_bias, fc1_bias, fc2_bias)
    ends = [0]
    for item in smalls:
        ends.append(ends[-1] + item.shape[0])
    pair = (PAIR, PAIR)
    qkv_cut = qkv_weight.reshape(rows, 3, 2, half)
    qkv_got = core_swap(theirs_of(qkv_cut, 2))
    qkv_block = jnp.concatenate([mine_of(qkv_cut, 2), qkv_got], axis=0)
    qkv = Gather(qkv_block.reshape(2 * rows, 3 * half), full)
    x_other = core_swap(inputs)
    q_got = [qkv.step()]

    small_own = jnp.concatenate(smalls)
    small_other = core_swap(small_own)
    small = jnp.where(
        core == 0, jnp.stack([small_own, small_other]), jnp.stack([small_other, small_own])
    )
    small = Gather(small, full)
    small.step(qkv_got)

    fc1_cut = after(fc1_weight, qkv_got).reshape(rows, few // low, 2, low, 2, units)
    fc1_got = core_swap(theirs_of(fc1_cut, 4))
    fc1_block = jnp.stack([mine_of(fc1_cut, 4), fc1_got])
    side_of = lambda which: lax.dynamic_index_in_dim(fc1_block, which, 3, False)
    fc1_block = jnp.stack([side_of(side), bit_swap(side_of(1 - side), pair)])
    fc1 = Gather(fc1_block.reshape(4 * rows, hidden), most)
    fc2 = Gather(fc2_weight, most)

    q_got.append(qkv.step())
    small.step(q_got[0])
    fc2_got = fc2.step(q_got[0])
    while len(qkv.steps) > 2:
        q_got.append(qkv.step())
        small.step(q_got[-2])
    qkv.step()
    q_got.append(qkv.got)
    small.step(q_got[-2])
    proj = Gather(proj_weight, full)
    proj_got = proj.step(q_got[-2])
    fc1_first = fc1.step(fc2_got)
    qkv.step()
    q_got.append(qkv.got)
    small.step(q_got[-2])
    while len(proj.steps) > 2:
        proj_got = proj.step(q_got[-2])
    slot = core * local + lax.iota(jnp.int32, local)
    row_live = [(slot < BUFFER + kept_counts[i])[:, None] for i in range(images)]

    def to_four(own, *others):
        two = jnp.concatenate([own, bit_swap(after(own, *others), pair)], axis=0)
        return jnp.concatenate([two, core_swap(two)], axis=0)

    cotangent = after(cotangent, q_got[-3])
    up_low = [jnp.where(live, c, 0).astype(b16) for live, c in zip(row_live, cotangent)]
    up_all = [to_four(u) for u in up_low]

    dev = after(dev, q_got[0])
    abs_rows = lax.iota(jnp.int32, width)
    qkv_perm = onehot(abs_rows, pick(table.qkv))
    fc1_perm = onehot(abs_rows, pick(table.fc1))
    proj_perm = onehot(pick(table.heads), pick(table.proj))
    col_perm = onehot(lax.iota(jnp.int32, hidden), pick(table.units))
    chip_perm = onehot(lax.iota(jnp.int32, n), pick(table.chips))
    unit_perm = onehot(pick(table.owners), lax.iota(jnp.int32, n))
    x_all = jnp.stack([inputs, x_other], axis=1).reshape(images * 2 * local, width)
    normed_all, _ = norm_parts(x_all.astype(f32))
    small = dot(chip_perm, small.held.reshape(n, -1)).reshape(n, 2, -1)
    gain_one, shift_one, b_qv, b_proj, gain_two, shift_two, b_fc1, b_fc2 = (
        small[:, :, a:b].reshape(-1) for a, b in zip(ends, ends[1:])
    )
    bias_fc1 = jnp.dot(
        unit_perm.astype(f32), mine_of(b_fc1.reshape(n, 2, units), 1), precision=HIGH
    ).reshape(-1)
    qv_cut = mine_of(b_qv.reshape(2, 2, half), 1)
    bias_qkv = jnp.concatenate([qv_cut[0], jnp.zeros((half,), f32), qv_cut[1]])
    first = (normed_all * gain_one + shift_one).astype(b16)
    first = dot(first, qkv_perm).astype(b16)

    w_qkv = qkv.held.reshape(width, 3 * half)
    mixed = (dot(first, w_qkv) + bias_qkv).astype(b16).reshape(images, 2 * local, 3 * half)
    metas = [jnp.stack([core.astype(jnp.int32), kept_counts[i]]) for i in range(images)]
    proj.step(q_got[-1])
    proj.step()
    w_proj = proj.held.reshape(half, width)
    w_proj = jnp.concatenate([w_proj, core_swap(w_proj)], axis=0)
    w_proj = dot(proj_perm, w_proj).astype(b16)
    fc2_got = fc2.step(q_got[-1])
    fc1_got = fc1.step(fc2_got)
    while fc2.steps:
        fc2.step()
    w_fc2 = dot(col_perm, fc2.held.reshape(hidden, width)).astype(b16)
    while fc1.steps:
        fc1.step()
    w_fc1 = dot(fc1_perm, fc1.held.reshape(width, hidden)).astype(b16)

    attended, middle, second, normed_two, scale_two = [], [], [], [], []
    for i in range(images):
        heads = attention(mixed[i], metas[i])
        heads = jnp.concatenate([heads[:local], core_swap(heads[local:])], axis=1)
        attended.append(heads)
        middle.append(inputs[i].astype(f32) + dot(heads, w_proj) + b_proj)
        normed, scale = norm_parts(middle[i])
        normed_two.append(normed)
        scale_two.append(scale)
        second.append(to_four((normed * gain_two + shift_two).astype(b16)))

    activated, slope = [], []
    for i in range(images):
        pre = dot(second[i], w_fc1) + bias_fc1
        phi = 0.5 * (1.0 + lax.erf(pre * (0.5**0.5)))
        activated.append((pre * phi).astype(b16))
        slope.append((phi + pre * jnp.exp(-0.5 * pre * pre) * 0.3989422804014327).astype(b16))

    def core_sum(part):
        return part[: 2 * local] + core_swap(part[2 * local :].astype(b16)).astype(f32)

    def pair_sum(two):
        return two[:local] + bit_swap(two[local:].astype(b16), pair).astype(f32)

    d_pre, d_two = [], []
    for i in range(images):
        d_pre.append((slope[i].astype(f32) * dot_nt(up_all[i], w_fc2)).astype(b16))
        d_two.append(core_sum(dot_nt(d_pre[i], w_fc1)))
    out_two = [core_sum(dot(activated[i], w_fc2)) for i in range(images)]
    d_second = [pair_sum(d) for d in d_two]

    cat = lambda parts: jnp.concatenate(parts, axis=0)
    cut = hidden // 2
    up_cat = cat(up_all)
    activated = after(cat(activated), *d_two)
    activated_rel = dot(activated, col_perm).astype(b16)
    grad_fc2 = Scatter(
        dot_tn(activated_rel[:, cut:], up_cat).astype(b16).reshape(-1, units, width),
        dot_tn(activated_rel[:, :cut], up_cat).reshape(-1, units, width),
        most,
    )
    second_rel = dot(cat(second), fc1_perm).astype(b16)
    d_pre_cat = cat(d_pre)
    grad_fc1 = Scatter(
        dot_tn(second_rel[:, half:], d_pre_cat).astype(b16).reshape(-1, 4 * rows, hidden),
        dot_tn(second_rel[:, :half], d_pre_cat).reshape(-1, 4 * rows, hidden),
        most,
    )
    grad_fc2.step()
    grad_fc1.step(grad_fc2.got)
    while grad_fc2.steps:
        grad_fc2.step()
    while grad_fc1.steps:
        grad_fc1.step()

    outputs = [
        jnp.where(row_live[i], middle[i] + pair_sum(after(out_two[i], *d_second)) + b_fc2, 0.0)
        for i in range(images)
    ]
    outputs = jnp.stack(outputs).astype(b16)

    d_middle, d_branch, d_mixed = [], [], []
    for i in range(images):
        back = norm_back(d_second[i], normed_two[i], scale_two[i], gain_two)
        d_middle.append(up_low[i].astype(f32) + back)
        d_branch.append(d_middle[i].astype(b16))
        d_att = dot_nt(d_branch[i], w_proj).astype(b16)
        d_att = jnp.concatenate([d_att[:, :half], core_swap(d_att[:, half:])], axis=0)
        d_mixed.append(attention(mixed[i], metas[i], d_att))

    attended_rel = dot(cat(attended), proj_perm).astype(b16)
    attended_rel = jnp.concatenate(
        [attended_rel[:, :half], core_swap(attended_rel[:, half:])], axis=0
    )
    branch = cat(d_branch)
    branch_all = jnp.concatenate([branch, core_swap(branch)], axis=0)
    parts = lambda a: a.reshape(-1, rows, a.shape[-1])
    proj_send = dot_tn(attended_rel[:, half // 2 :], branch_all).astype(b16)
    proj_keep = dot_tn(attended_rel[:, : half // 2], branch_all)
    grad_proj = Scatter(parts(proj_send), parts(proj_keep), full)
    while grad_proj.steps:
        grad_proj.step()

    d_mixed = cat(d_mixed)
    qkv_send = dot_tn(first[:, half:], d_mixed).astype(b16)
    d_first = dot_nt(dot_nt(after(d_mixed, qkv_send), w_qkv).astype(b16), qkv_perm).astype(b16)
    d_first = d_first.reshape(images, 2, local, width)
    d_first = d_first[:, 0].astype(f32) + core_swap(d_first[:, 1]).astype(f32)
    qkv_keep = dot_tn(first[:, :half], after(d_mixed, d_first))
    cut3 = lambda a: a.reshape(-1, 2 * rows, 3 * half)
    grad_qkv = Scatter(cut3(qkv_send), cut3(qkv_keep), full)
    normed_one, scale_one = norm_parts(inputs.astype(f32))
    input_grad = jnp.stack(d_middle) + norm_back(d_first, normed_one, scale_one, gain_one)

    placed = lambda a, axis: jnp.stack(
        [jnp.where(core == 0, a, 0.0), jnp.where(core == 1, a, 0.0)], axis=axis
    )
    total = lambda a: jnp.sum(a.astype(f32).reshape(-1, a.shape[-1]), axis=0)
    d_mixed_sum = total(d_mixed).reshape(3, half)
    d_pre_sum = jnp.dot(
        unit_perm.astype(f32).T, total(d_pre_cat).reshape(few, units), precision=HIGH
    )
    d_second = jnp.stack(d_second)
    small_grads = (
        total(d_first * normed_one),
        total(d_first),
        placed(d_mixed_sum[::2], 1),
        total(branch),
        total(d_second * jnp.stack(normed_two)),
        total(d_second),
        placed(d_pre_sum, 1),
        total(jnp.stack(up_low)),
    )
    small_grads = jnp.concatenate([g.reshape(n, 2, -1) for g in small_grads], axis=2)
    small_grads = mine_of(small_grads, 1) + core_swap(theirs_of(small_grads, 1))
    small_grads = jnp.dot(chip_perm.astype(f32).T, small_grads, precision=HIGH)
    small_grads = small_grads[:, None]
    small_grads = Scatter(small_grads[few:], small_grads[:few], full)
    small_grads.step()
    grad_qkv.step()
    while grad_qkv.steps:
        small_grads.step(grad_qkv.got)
        grad_qkv.step()
    small_grads = small_grads.keep[0, 0]
    small_grads = [small_grads[a:b] for a, b in zip(ends, ends[1:])]
    grad_fc1, grad_fc2, grad_proj, grad_qkv = (
        g.keep[0] for g in (grad_fc1, grad_fc2, grad_proj, grad_qkv)
    )

    qkv_other = core_swap(grad_qkv[rows:])
    both = lambda own, other, which, axis: jnp.where(
        which == 0, jnp.stack([own, other], axis=axis), jnp.stack([other, own], axis=axis)
    )
    cut3 = lambda a: a.reshape(rows, 3, half)
    grad_qkv = both(cut3(grad_qkv[:rows]), cut3(qkv_other), core, 2).reshape(qkv_weight.shape)

    pair_other = bit_swap(grad_fc1[2 * rows :], pair)
    cut4 = lambda a: a.reshape(2 * rows, few // low, low, units)
    grad_fc1 = both(cut4(grad_fc1[: 2 * rows]), cut4(pair_other), side, 2)
    core_other = core_swap(grad_fc1[rows:])
    grad_fc1 = both(grad_fc1[:rows], core_other, core, 4).reshape(fc1_weight.shape)
    return (
        outputs,
        input_grad,
        small_grads[0],
        small_grads[1],
        grad_qkv,
        small_grads[2],
        grad_proj,
        small_grads[3],
        small_grads[4],
        small_grads[5],
        grad_fc1,
        small_grads[6],
        grad_fc2,
        small_grads[7],
    )


def pack_units_kernel(where_ref, w_ref, mine_ref, theirs_ref):
    wide = mine_ref.shape[2]
    units = 128
    low = 1 << PAIR
    for ref, core in ((mine_ref, where_ref[0]), (theirs_ref, 1 - where_ref[0])):
        for p in range(2):
            side = where_ref[1] ^ p
            for b in range(wide // units):
                chip = (b // low) * 2 * low + side * low + b % low
                at = pl.multiple_of((2 * chip + core) * units, units)
                ref[p, :, b * units : (b + 1) * units] = w_ref[:, pl.ds(at, units)]


def pack_units(weight, units, core, side):
    rows, hidden = weight.shape
    if units == 128:
        out = jax.ShapeDtypeStruct((2, rows, hidden // 4), weight.dtype)
        return pl.pallas_call(
            pack_units_kernel,
            out_shape=(out, out),
            in_specs=[pl.BlockSpec(memory_space=pltpu.SMEM), pl.BlockSpec(memory_space=pltpu.VMEM)],
            out_specs=(pl.BlockSpec(memory_space=pltpu.VMEM),) * 2,
        )(jnp.stack([core, side]), weight)
    low = 1 << PAIR
    cut = weight.reshape(rows, -1, 2, low, 2, units)

    def part(c, p):
        block = lax.dynamic_index_in_dim(cut, c, 4, False)
        return lax.dynamic_index_in_dim(block, p, 2, False).reshape(rows, hidden // 4)

    return tuple(jnp.stack([part(c, side), part(c, 1 - side)]) for c in (core, 1 - core))


LANES = 128
MEASURED_US = {
    "k_pack_heads": 1.6, "k_heads": 7, "k_attend": 6, "k_project": 0.1,
    "k_feed_first": 14, "k_feed": 10, "k_feed_out": 3, "k_pair_send": 0.2, "k_grad_feed": 15,
    "k_middle_back": 30, "k_attend_back": 8, "k_grad_proj": 0.2, "k_grad_heads": 8.7,
    "k_first_back": 6, "k_input_back": 4.3, "k_small": 2, "k_output": 4, "k_columns": 2, "k_rows": 1.8,
}
FLOPS_PER_US = 3e9
VMEM_LIMIT = 56 * 1024 * 1024
SMALL_ROWS = 8
GAIN1, BIAS1, QV, PROJ_B, GAIN2, BIAS2, FC1_B, FC2_B = range(8)


def spread_of(position, orders, core):
    a, b = (spread(position, order) for order in orders)
    return a if a == b else jnp.where(core == 0, a, b)


def position_of(bits, orders, core):
    a, b = (
        sum((((bits >> bit) & 1) << k) for k, bit in enumerate(order)) for order in orders
    )
    return jnp.where(core == 0, a, b)


def call(kernel, out, args, grid=None, in_specs=None, out_specs=None, scratch=(), deps=(), kept=0, us=None, place=None):
    whole = pl.BlockSpec(memory_space=pltpu.VMEM)
    outs = out if isinstance(out, tuple) else (out,)
    specs = [pl.BlockSpec(memory_space=pltpu.SMEM)] + list(in_specs or [whole] * len(args))
    out_specs = out_specs if out_specs is not None else tuple(whole for _ in outs)
    extra = {} if grid is None else {"grid": grid}
    name = getattr(kernel, "func", kernel).__name__
    flops = int((us or MEASURED_US[name]) * FLOPS_PER_US)
    if deps:
        specs += [pl.BlockSpec(memory_space=pl.ANY)] * len(deps)
        inner, count = kernel, 1 + len(args)

        def kernel(*refs):
            return inner(*refs[:count], *refs[count + len(deps) :])

        extra["input_output_aliases"] = {count + k: k for k in range(kept)}
    result = pl.pallas_call(
        kernel,
        out_shape=outs,
        in_specs=specs,
        out_specs=tuple(out_specs),
        scratch_shapes=list(scratch),
        compiler_params=pltpu.CompilerParams(vmem_limit_bytes=VMEM_LIMIT),
        cost_estimate=pl.CostEstimate(flops=flops, bytes_accessed=1000, transcendentals=0),
        **extra,
    )(place, *args, *deps)
    return result if isinstance(out, tuple) else result[0]


class Order:
    def __init__(self, place):
        self.place, self.last = place, ()

    def call(self, *args, wait=(), **named):
        result = call(*args, deps=tuple(wait) + self.last, place=self.place, **named)
        found = result if isinstance(result, tuple) else (result,)
        self.last = (min(found, key=lambda a: a.size),)
        return result

    def now(self, *values):
        values = lax.optimization_barrier((*values, *self.last))
        self.last = tuple(values[len(values) - len(self.last) :])
        values = values[: len(values) - len(self.last)]
        return values if len(values) > 1 else values[0]


def tie(*values):
    return lax.optimization_barrier(values)


def shape(dims, dtype=f32):
    return jax.ShapeDtypeStruct(tuple(dims), dtype)


def aligned(index, step):
    return pl.multiple_of(index * step, step)


def k_pack_heads(place, w, small, theirs, mine):
    three = w.shape[1]
    half = three // 6
    me_core = lax.axis_index("seq")
    for ref, core in ((mine, me_core), (theirs, 1 - me_core)):
        for which in range(3):
            at = pl.multiple_of((which * 2 + core) * half, half)
            ref[:, which * half : (which + 1) * half] = w[:, pl.ds(at, half)]
        ref[:, 3 * half :] = jnp.zeros((w.shape[0], LANES), b16)
        ref[:SMALL_ROWS, 3 * half :] = small[...]


def k_heads(orders, place, sent, got, x_own, x_other, w_qkv, vectors, first, mixed, small):
    me, core, side = place[0], place[1], place[2]
    blocks, two_rows, lanes = sent.shape
    n = 2 * blocks
    rows = two_rows // 2
    three = w_qkv.shape[1]
    half = three // 3
    for p in range(n):
        block = sent if p < blocks else got
        at = p % blocks
        chip = me ^ spread_of(p, orders, core)
        for c in range(2):
            dev = 2 * chip + (core ^ c)
            part = slice(c * rows, (c + 1) * rows)
            w_qkv[pl.ds(aligned(dev, rows), rows), :] = block[at, part, :three]
            small[dev] = block[at, c * rows : c * rows + SMALL_ROWS, three:].astype(f32)

    def lane_block(first_dev, vector, size):
        total = small[first_dev, vector : vector + 1, :]
        for i in range(1, LANES // size):
            total += pltpu.roll(small[first_dev + i, vector : vector + 1, :], i * size, 1)
        return total

    width = w_qkv.shape[0]
    per = width // (2 * n)
    for row, vector in enumerate((GAIN1, BIAS1, PROJ_B, GAIN2, BIAS2, FC2_B)):
        for q in range(width // LANES):
            vectors[row : row + 1, q * LANES : (q + 1) * LANES] = lane_block(
                q * (LANES // per), vector, per
            )
    for which in range(2):
        for q in range(half // LANES):
            dev = (which * 2 + core) * (half // (2 * per)) + q * (LANES // (2 * per))
            at = which * half + q * LANES
            vectors[6:7, at : at + LANES] = lane_block(dev, QV, 2 * per)
    low = 1 << PAIR
    for b in range(n // 2):
        chip = (b // low) * 2 * low + side * low + b % low
        vectors[7:8, b * LANES : (b + 1) * LANES] = small[2 * chip + core, FC1_B : FC1_B + 1, :]

    images, local, _ = x_own.shape
    for i in range(images):
        for c, ref in enumerate((x_own, x_other)):
            normed, _ = norm_parts(ref[i].astype(f32))
            at = (2 * i + c) * local
            first[at : at + local, :] = (
                normed * vectors[0:1, :] + vectors[1:2, :]
            ).astype(b16)
    for which in range(3):
        part = slice(which * half, (which + 1) * half)
        total = dot(first[...], w_qkv[:, part])
        if which != 1:
            total += vectors[6:7, (which // 2) * half : (which // 2 + 1) * half]
        mixed[:, part] = total.astype(b16)


def k_pair_send(place, own0, got0, own1, got1, send0, send1):
    for own, got, send in ((own0, got0, send0), (own1, got1, send1)):
        send[...] = (own[...] + got[...].astype(f32)).astype(b16)


def k_output(place, middle, own, got, pair_got, vectors, out):
    images, local, _ = out.shape
    slot = place[1] * local + lax.broadcasted_iota(jnp.int32, (local, 1), 0)
    for i in range(images):
        part = slice(i * local, (i + 1) * local)
        total = middle[part, :] + vectors[5:6, :] + own[part, :]
        total += got[part, :].astype(f32) + pair_got[part, :].astype(f32)
        out[i] = jnp.where(slot < BUFFER + place[3 + i], total, 0.0).astype(b16)


def k_unpack_units(orders, place, sent, got, w_fc1, w_fc2):
    me, core = place[0], place[1]
    blocks = sent.shape[0]
    units = LANES
    rows = (sent.shape[1] - units) // 4
    low = 1 << PAIR
    for p in range(2 * blocks):
        block = sent if p < blocks else got
        at = p % blocks
        chip = me ^ spread_of(p, orders, core)
        for c2 in range(2):
            for c in range(2):
                dev = 2 * (chip ^ (c2 << PAIR)) + (core ^ c)
                k = 2 * c2 + c
                w_fc1[pl.ds(aligned(dev, rows), rows), :] = block[at, k * rows : (k + 1) * rows, :]
        short = ((chip >> (PAIR + 1)) << PAIR) + (chip & (low - 1))
        w_fc2[pl.ds(aligned(short, units), units), :] = block[at, 4 * rows :, :]


def live_of(place, image, local, axis):
    dims = (2 * local, 1) if axis == 0 else (1, 2 * local)
    at = lax.broadcasted_iota(jnp.int32, dims, axis)
    core = place[1]
    slot = jnp.where(at < local, at + core * local, at - core * local)
    return slot < BUFFER + place[3 + image]


def k_attend(image, place, q, k, v, own, other):
    local = own.shape[0]
    live = live_of(place, image, local, 1)
    outs = []
    for e in range(2):
        part = slice(e * HEAD_DIM, (e + 1) * HEAD_DIM)
        raw = dot_nt(q[:, part] * (HEAD_DIM**-0.5), k[:, part])
        raw = jnp.where(live, raw, -1e30)
        expo = jnp.exp(raw - jnp.max(raw, axis=-1, keepdims=True))
        probs = expo * (1.0 / jnp.sum(expo, axis=-1, keepdims=True))
        outs.append(dot(probs.astype(b16), v[:, part]))
    both = jnp.concatenate(outs, axis=1).astype(b16)
    own[...] = both[:local]
    other[...] = both[local:]


def k_attend_back(image, place, q, k, v, g_own, g_other, d_mixed, sums):
    local = g_own.shape[0]
    pairs = pl.num_programs(0)
    live = live_of(place, image, local, 0)
    scale = HEAD_DIM**-0.5
    g = jnp.concatenate([g_own[...], g_other[...]], axis=0)
    parts = ([], [], [])
    for e in range(2):
        part = slice(e * HEAD_DIM, (e + 1) * HEAD_DIM)
        qe, ke, ve, ge = q[:, part], k[:, part], v[:, part], g[:, part]
        raw = jnp.where(live, dot_nt(ke, qe * scale), -1e30)
        expo = jnp.exp(raw - jnp.max(raw, axis=0, keepdims=True))
        probs = expo * (1.0 / jnp.sum(expo, axis=0, keepdims=True))
        d_probs = dot_nt(ve, ge)
        inner = jnp.sum(probs * d_probs, axis=0, keepdims=True)
        d_scores = (probs * (d_probs - inner)).astype(b16)
        parts[0].append(dot_tn(d_scores, ke) * scale)
        parts[1].append(dot(d_scores, qe) * scale)
        parts[2].append(dot(probs.astype(b16), ge))
    for which in range(3):
        at = pl.multiple_of((which * pairs + pl.program_id(0)) * LANES, LANES)
        value = jnp.concatenate(parts[which], axis=1).astype(b16)
        d_mixed[:, pl.ds(at, LANES)] = value
        total = jnp.sum(value.astype(f32), axis=0, keepdims=True)
        sums[:, pl.ds(at, LANES)] = jnp.broadcast_to(total, (8, LANES))


def k_project(orders, place, sent, got, sent_far, got_far, own0, own1, got0, got1, x, vectors,
              w, middle, second):
    me, core = place[0], place[1]
    blocks, rows, _ = sent.shape
    for c, refs in enumerate(((sent, got), (sent_far, got_far))):
        for p in range(2 * blocks):
            chip = me ^ spread_of(p, orders, core ^ c)
            at = aligned(2 * chip + (core ^ c), rows)
            w[pl.ds(at, rows), :] = refs[p // blocks][p % blocks]
    half = own0.shape[1]
    images, local, _ = x.shape
    both = lambda a, b: jnp.concatenate([a[...], b[...]], axis=0)
    total = dot(both(own0, own1), w[pl.ds(aligned(core, half), half), :])
    total += dot(both(got0, got1), w[pl.ds(aligned(1 - core, half), half), :])
    for i in range(images):
        part = slice(i * local, (i + 1) * local)
        mid = x[i].astype(f32) + total[part] + vectors[2:3, :]
        middle[part, :] = mid
        normed, _ = norm_parts(mid)
        second[part, :] = (normed * vectors[3:4, :] + vectors[4:5, :]).astype(b16)


def k_feed(place, s0, s1, u0, u1, w1, w2, vectors, act, d_pre, ds_own, ds_other, sums, sec, up):
    images, local, _ = u0.shape
    tokens = images * local
    tile = 256
    for k, (s, u) in enumerate(((s0, u0), (s1, u1))):
        sec[k * tokens : (k + 1) * tokens, :] = s[...]
        for i in range(images):
            at = k * tokens + i * local
            up[at : at + local, :] = u[i]
    for at in range(0, w1.shape[1], tile):
        part = slice(at, at + tile)
        pre = dot(sec[...], w1[:, part]) + vectors[7:8, part]
        phi = 0.5 * (1.0 + lax.erf(pre * (0.5**0.5)))
        act[:, part] = (pre * phi).astype(b16)
        slope = phi + pre * jnp.exp(-0.5 * pre * pre) * 0.3989422804014327
        grad = (slope * dot_nt(up[...], w2[part, :])).astype(b16)
        d_pre[:, part] = grad
        total = jnp.sum(grad.astype(f32), axis=0, keepdims=True)
        sums[:, part] = jnp.broadcast_to(total, (8, tile))
    ds_other[...] = dot_nt(d_pre[tokens:, :], w1[...]).astype(b16)
    ds_own[...] = dot_nt(d_pre[:tokens, :], w1[...])


def k_feed_first(orders, place, sent, got, s0, s1, u0, u1, vectors, w1, w2, *outs):
    k_unpack_units(orders, place, sent, got, w1, w2)
    k_feed(place, s0, s1, u0, u1, w1, w2, vectors, *outs)


def k_feed_out(place, act, w2, own, other):
    tokens = own.shape[0]
    other[...] = dot(act[tokens:, :], w2[...]).astype(b16)
    own[...] = dot(act[:tokens, :], w2[...])


def k_middle_back(place, ds_own, ds_got, pair_got, middle, up, w, vectors,
                  d_middle, d_branch, att_own, att_other, sums):
    core = place[1]
    images, local, _ = up.shape
    half = att_own.shape[1]
    total = lambda a: jnp.sum(a, axis=0, keepdims=True)
    rows = [0.0] * 4
    for i in range(images):
        part = slice(i * local, (i + 1) * local)
        d_second = ds_own[part, :] + ds_got[part, :].astype(f32) + pair_got[part, :].astype(f32)
        normed, scale = norm_parts(middle[part, :])
        upstream = up[i].astype(f32)
        d_mid = upstream + norm_back(d_second, normed, scale, vectors[3:4, :])
        d_middle[part, :] = d_mid
        branch = d_mid.astype(b16)
        d_branch[part, :] = branch
        rows[0] += total(d_second * normed)
        rows[1] += total(d_second)
        rows[2] += total(branch.astype(f32))
        rows[3] += total(upstream)
    branch = d_branch[...]
    att_other[...] = dot_nt(branch, w[pl.ds(aligned(1 - core, half), half), :]).astype(b16)
    att_own[...] = dot_nt(branch, w[pl.ds(aligned(core, half), half), :]).astype(b16)
    for r in range(4):
        sums[r : r + 1, :] = rows[r]
    sums[4:, :] = jnp.zeros((4, sums.shape[1]), f32)


def put(held, row, value):
    held[pl.ds(pl.multiple_of(row, value.shape[0]), value.shape[0]), :] = value.astype(b16)


def split(held, send, keep):
    cut = send.shape[0]
    send[...] = held[cut:, :]
    keep[...] = held[:cut, :]


def k_grad_heads(orders, n, place, left, right, send, keep, held):
    me, core = place[0], place[1]
    tile = 256
    rows = held.shape[0] // (2 * n)
    for step in range(left.shape[1] // tile):
        total = dot_tn(left[:, step * tile : (step + 1) * tile], right[...])
        for i in range(tile // rows):
            dev = step * (tile // rows) + i
            at = position_of(me ^ (dev // 2), orders, core)
            value = total[i * rows : (i + 1) * rows, :]
            put(held, at * 2 * rows + (core ^ (dev % 2)) * rows, value)
    split(held, send, keep)


def k_grad_feed(orders, n, place, a0, a1, u0, u1, s0, s1, d0, d1, send, keep, held):
    me, core, side = place[0], place[1], place[2]
    low = 1 << PAIR
    tile = 256
    per = 2 * send.shape[0] // (n // 2)
    rows = (per - LANES) // 4
    for step in range(a0.shape[1] // tile):
        part = slice(step * tile, (step + 1) * tile)
        total = dot_tn(a0[:, part], u0[...]) + dot_tn(a1[:, part], u1[...])
        for i in range(tile // LANES):
            b = step * (tile // LANES) + i
            chip = (b // low) * 2 * low + side * low + b % low
            at = position_of(me ^ chip, orders, core)
            put(held, at * per, total[i * LANES : (i + 1) * LANES, :])
    for step in range(s0.shape[1] // tile):
        part = slice(step * tile, (step + 1) * tile)
        total = dot_tn(s0[:, part], d0[...]) + dot_tn(s1[:, part], d1[...])
        for i in range(tile // rows):
            dev = step * (tile // rows) + i
            bits = me ^ (dev // 2)
            at = position_of(bits, orders, core)
            inner = LANES + (((bits >> PAIR) & 1) * 2 + (core ^ (i % 2))) * rows
            put(held, at * per + inner, total[i * rows : (i + 1) * rows, :])
    split(held, send, keep)


def k_grad_proj(orders, place, *refs):
    lefts, rights, (send, keep, held) = (refs[:4], refs[4:8]), refs[8:10], refs[10:]
    me, core = place[0], place[1]
    rows = 32
    right = jnp.concatenate([a[...] for a in rights], axis=0)
    count = lefts[0][0].shape[1] // (2 * rows)
    for which in range(2):
        left = jnp.concatenate([a[...] for a in lefts[which]], axis=0)
        total = dot_tn(left, right)
        for i in range(count):
            chip = (core ^ which) * count + i
            at = position_of(me ^ chip, orders, core)
            value = jnp.where(
                core == 0,
                total[2 * i * rows : (2 * i + 1) * rows, :],
                total[(2 * i + 1) * rows : (2 * i + 2) * rows, :],
            )
            put(held, at * rows, value)
    split(held, send, keep)


def k_first_back(place, d, w, own, other):
    images, local, width = own.shape
    tile = 256
    for step in range(width // tile):
        part = slice(step * tile, (step + 1) * tile)
        total = dot_nt(d[...], w[part, :])
        for i in range(images):
            at = 2 * i * local
            own[i, :, part] = total[at : at + local]
            other[i, :, part] = total[at + local : at + 2 * local].astype(b16)


def k_input_back(place, x, own, got, mid, vectors, grad, sums):
    total = lambda a: jnp.sum(a, axis=0, keepdims=True)
    images, local, _ = x.shape
    gains = biases = 0.0
    for i in range(images):
        normed, scale = norm_parts(x[i].astype(f32))
        d_first = own[i] + got[i].astype(f32)
        back = norm_back(d_first, normed, scale, vectors[0:1, :])
        grad[i] = mid[i * local : (i + 1) * local, :] + back
        gains += total(d_first * normed)
        biases += total(d_first)
    sums[0:1, :] = gains
    sums[1:2, :] = biases
    sums[2:, :] = jnp.zeros((6, sums.shape[1]), f32)


def k_small(orders, n, place, one, mids, pre0, pre1, mix, mine, theirs, small):
    me, core, side = place[0], place[1], place[2]
    width = one.shape[1]
    per = width // (2 * n)
    half = width // 2
    pres = pre0[...] + pre1[...]
    mixes = mix[:8, :] + mix[8:, :]
    small[...] = jnp.zeros(small.shape, f32)
    rows = (
        (GAIN1, one[0:1, :]),
        (BIAS1, one[1:2, :]),
        (GAIN2, mids[0:1, :]),
        (BIAS2, mids[1:2, :]),
        (PROJ_B, mids[2:3, :]),
        (FC2_B, mids[3:4, :]),
    )
    lane = lambda row, q: row[:, q * LANES : (q + 1) * LANES]
    for vector, row in rows:
        for dev in range(2 * n):
            q, i = divmod(dev * per, LANES)
            part = lane(row, q)
            small[dev, vector : vector + 1, :] = part if i == 0 else pltpu.roll(part, LANES - i, 1)
    for which in range(2):
        row = mixes[0:1, 2 * which * half : (2 * which + 1) * half]
        for dev in range(half // (2 * per)):
            q, i = divmod(dev * 2 * per, LANES)
            part = lane(row, q)
            part = part if i == 0 else pltpu.roll(part, LANES - i, 1)
            small[(2 * which + core) * (half // (2 * per)) + dev, QV : QV + 1, :] = part
    low = 1 << PAIR
    for b in range(n // 2):
        chip = (b // low) * 2 * low + side * low + b % low
        small[2 * chip + core, FC1_B : FC1_B + 1, :] = lane(pres[0:1, :], b)
    for p in range(n):
        mine[p] = small[2 * (me ^ spread_of(p, orders, core)) + core]
        theirs[p] = small[2 * (me ^ spread_of(p, orders, 1 - core)) + 1 - core]


def k_rows(place, own, got, out):
    core = place[1]
    half = out.shape[1] // 6
    for which in range(3):
        part = slice(which * half, (which + 1) * half)
        at = pl.multiple_of((2 * which + core) * half, half)
        out[:, pl.ds(at, half)] = own[: out.shape[0], part]
        at = pl.multiple_of((2 * which + 1 - core) * half, half)
        out[:, pl.ds(at, half)] = got[:, part]


def k_columns(place, own, own_pair, got, got_pair, out):
    core, side = place[1], place[2]
    low = 1 << PAIR
    rows = out.shape[0]
    for ref, c, s in (
        (own, core, side),
        (own_pair, core, 1 - side),
        (got, 1 - core, side),
        (got_pair, 1 - core, 1 - side),
    ):
        for b in range(ref.shape[1] // LANES):
            chip = (b // low) * 2 * low + s * low + b % low
            at = pl.multiple_of((2 * chip + c) * LANES, LANES)
            out[:, pl.ds(at, LANES)] = ref[:rows, b * LANES : (b + 1) * LANES]


class Sums:
    def __init__(self, run, send, keep, orders):
        self.run, self.send, self.keep, self.got = run, send, keep, None
        self.steps = list(zip(*orders))[::-1]
        self.step()

    def settle(self):
        got = self.run.now(self.got)
        cut = got.shape[0] // 2
        if cut:
            total = self.keep[cut:].astype(f32) + got[cut:].astype(f32)
            self.send = total.astype(self.send.dtype)
            self.keep = self.keep[:cut].astype(f32) + got[:cut].astype(f32)
        else:
            self.keep = self.keep.astype(f32) + got.astype(f32)
        self.got = None

    def step(self):
        if self.got is not None:
            self.settle()
        self.got = bit_swap(self.send, self.steps.pop(0))

    def sum(self):
        while self.steps:
            self.step()
        self.settle()
        return self.keep[0]


def fast_body(
    inputs,
    cotangent,
    kept_counts,
    norm1_gain,
    norm1_bias,
    qkv_weight,
    qv_bias,
    proj_weight,
    proj_bias,
    norm2_gain,
    norm2_bias,
    fc1_weight,
    fc1_bias,
    fc2_weight,
    fc2_bias,
):
    images, local, width = inputs.shape
    n = lax.axis_size("img")
    me = lax.axis_index("img")
    core = lax.axis_index("seq")
    levels = n.bit_length() - 1
    half = width // 2
    rows = width // (2 * n)
    units = fc2_weight.shape[0]
    few = n // 2
    hidden = units * few
    side = (me >> PAIR) & 1
    pair = (PAIR, PAIR)
    full = tuple(tuple(range(levels - 1, 1, -1)) + last for last in ((0, 1), (1, 0)))
    most = tuple(tuple(b for b in order if b != PAIR) for order in full)
    last = tuple(order[-2:] + order[:-2] for order in full)
    place = jnp.concatenate([jnp.stack([me, core, side]).astype(jnp.int32), kept_counts])
    run = Order(place)
    on = run.call
    bind = functools.partial
    block = lambda dims, index: pl.BlockSpec(dims, index)
    whole = pl.BlockSpec(memory_space=pltpu.VMEM)

    smalls = (norm1_gain, norm1_bias, qv_bias, proj_bias, norm2_gain, norm2_bias, fc1_bias, fc2_bias)
    small = sum(
        jnp.pad(a[None], ((i, 7 - i), (0, LANES - a.shape[0]))) for i, a in enumerate(smalls)
    )
    packed = shape((rows, 3 * half + LANES), b16)
    theirs, mine = call(k_pack_heads, (packed, packed), (qkv_weight, small), place=kept_counts)
    fc1_mine, fc1_theirs = pack_units(fc1_weight, units, core, side)
    heads = Gather(jnp.concatenate([mine, core_swap(theirs)], axis=0), full)
    fc1_got = core_swap(fc1_theirs)
    x_other = core_swap(inputs)
    slot = core * local + lax.iota(jnp.int32, local)
    row_live = slot[None, :] < BUFFER + kept_counts[:, None]
    up = jnp.where(row_live[:, :, None], cotangent, 0).astype(b16)
    up_other = core_swap(up)
    fc1_send = jnp.concatenate([fc1_mine[1], fc1_got[1]], axis=0)
    proj = Gather(proj_weight, last)

    heads.step()
    fc1_pair = bit_swap(fc1_send, pair)
    heads.held, proj.held, fc1_pair, x_other, up_other = tie(
        heads.held, proj.held, fc1_pair, x_other, up_other
    )
    heads.step()
    proj.step()
    fc2 = Gather(fc2_weight, most)
    heads.held, proj.held, fc2.held = tie(heads.held, proj.held, fc2.held)
    while len(heads.steps) > 1:
        heads.step()
    proj.step()
    fc2.step()
    fc1 = Gather(jnp.concatenate([fc1_mine[0], fc1_got[0], fc1_pair], axis=0), most)
    heads.held, proj.held, fc1.held, fc2.held = tie(heads.held, proj.held, fc1.held, fc2.held)
    heads.step()
    fc1.step()
    heads.got, fc1.held, proj.held = tie(heads.got, fc1.held, proj.held)
    feed = Gather(None, most)
    feed.steps = fc1.steps
    feed.held = jnp.concatenate([fc1.held, fc2.held], axis=1)
    feed.step()
    proj.step()

    tokens = images * 2 * local
    w_qkv, vectors, first, mixed = on(
        bind(k_heads, full),
        (
            shape((width, 3 * half), b16),
            shape((8, width)),
            shape((tokens, width), b16),
            shape((tokens, 3 * half), b16),
        ),
        (heads.sent, heads.got, inputs, x_other),
        scratch=[pltpu.VMEM((2 * n, SMALL_ROWS, LANES), f32)],
    )
    pairs = half // LANES
    slots = 2 * local
    head_specs = lambda i: [
        block((slots, LANES), lambda h, i=i, f=f: (i, f + h)) for f in (0, pairs, 2 * pairs)
    ]
    lane_spec = block((local, LANES), lambda h: (0, h))
    tok = images * local
    flat = lambda cols, dtype=f32: shape((tok, cols), dtype)
    att_own, att_other, att_got = [], [], []
    for i in range(images):
        own, other = on(
            bind(k_attend, i),
            (shape((local, half), b16),) * 2,
            (mixed, mixed, mixed),
            grid=(pairs,),
            in_specs=head_specs(i),
            out_specs=[lane_spec, lane_spec],
        )
        att_own.append(own)
        att_other.append(other)
        att_got.append(core_swap(other))
        if i == 0:
            proj.got, feed.got = run.now(proj.got, feed.got)
            proj.held = jnp.concatenate([proj.sent, proj.got], axis=0)
            feed.held = jnp.concatenate([feed.sent, feed.got], axis=0)
            feed.step()
            proj.step()
            proj_sent_far = core_swap(proj.sent)
    proj.got, up = run.now(proj.got, up)
    up_pair = bit_swap(up, pair)
    proj_far = proj_sent_far, core_swap(proj.got)
    w_proj, middle, second = on(
        bind(k_project, last),
        (shape((width, width), b16), flat(width), flat(width, b16)),
        (proj.sent, proj.got, *proj_far, *att_own, *att_got, inputs, vectors),
    )
    second_other = core_swap(second)
    second_pair = bit_swap(second, pair)
    up_pair = run.now(up_pair)
    up_other_pair = core_swap(up_pair)
    tile = 256
    fixed = lambda dims: block(dims, lambda *_: (0,) * len(dims))
    wide_rows = lambda cols: shape((2 * tok, cols), b16)
    feed_shapes = (
        wide_rows(hidden), wide_rows(hidden), flat(width), flat(width, b16), shape((8, hidden)),
        wide_rows(width), wide_rows(width),
    )
    feeds = []
    w_fc1, w_fc2, *own_feed = on(
        bind(k_feed_first, most),
        (shape((width, hidden), b16), shape((hidden, width), b16)) + feed_shapes,
        (feed.sent, feed.got, second, second_other, up, up_other, vectors),
    )
    feeds.append(own_feed)
    second_pair = run.now(second_pair)
    second_other_pair = core_swap(second_pair)
    feeds.append(
        on(
            k_feed,
            feed_shapes,
            (second_pair, second_other_pair, up_pair, up_other_pair, w_fc1, w_fc2, vectors),
        )
    )
    ds_pair_got = core_swap(feeds[1][3])
    out_shapes = (flat(width), flat(width, b16))
    out_pair_own, out_pair_other = on(k_feed_out, out_shapes, (feeds[1][0], w_fc2))
    out_pair_got = core_swap(out_pair_other)

    acts = [f[0] for f in feeds]
    d_pres = [f[1] for f in feeds]
    ds_send, out_send = on(
        k_pair_send,
        (flat(width, b16),) * 2,
        (feeds[1][2], ds_pair_got, out_pair_own, out_pair_got),
    )
    pair_got = bit_swap(ds_send, pair)
    ds_got = core_swap(run.now(feeds[0][3]))
    halves = lambda count, cols: (shape((count, cols), b16), shape((count, cols), b16))
    held = lambda count, cols: [pltpu.VMEM((2 * count, cols), b16)]
    cut = lambda a, per: a.reshape(-1, per, a.shape[-1])
    feed_send, feed_keep = on(
        bind(k_grad_feed, most, n),
        halves(few // 2 * (4 * rows + units), width),
        (*acts, *[f[6] for f in feeds], *[f[5] for f in feeds], *d_pres),
        scratch=held(few // 2 * (4 * rows + units), width),
    )
    grad_feed = Sums(run, cut(feed_send, 4 * rows + units), cut(feed_keep, 4 * rows + units), most)

    out_pair = bit_swap(run.now(out_send), pair)
    d_middle, d_branch, d_att, d_att_other, mid_sums = on(
        k_middle_back,
        (flat(width), flat(width, b16), flat(half, b16), flat(half, b16), shape((8, width))),
        (feeds[0][2], ds_got, pair_got, middle, up, w_proj, vectors),
    )
    d_att_got = core_swap(d_att_other)
    att_far, d_branch_far = [core_swap(a) for a in att_own], core_swap(d_branch)
    d_mixed, mix_sums = (), ()
    for i in range(images):
        part = block((local, LANES), lambda h, i=i: (i, h))
        d_mixed, mix_sums = on(
            bind(k_attend_back, i),
            (shape((tokens, 3 * half), b16), shape((8 * images, 3 * half))),
            (mixed, mixed, mixed, d_att, d_att_got),
            grid=(pairs,),
            in_specs=head_specs(i) + [part, part],
            out_specs=[
                block((slots, 3 * half), lambda h, i=i: (i, 0)),
                block((8, 3 * half), lambda h, i=i: (i, 0)),
            ],
            wait=(d_mixed, mix_sums) if i > 0 else (),
            kept=2 if i > 0 else 0,
            us=8 if i > 0 else 0.2,
        )
        if i == 0:
            proj_send, proj_keep = on(
                bind(k_grad_proj, full),
                halves(half // 2, width),
                (*att_own, *att_other, *att_got, *att_far, d_branch, d_branch_far),
                scratch=held(half // 2, width),
            )
            grad_proj = Sums(run, cut(proj_send, rows), cut(proj_keep, rows), full)
            grad_feed.step()
    qkv_send, qkv_keep = on(
        bind(k_grad_heads, full, n),
        halves(half, 3 * half),
        (first, d_mixed),
        scratch=held(half, 3 * half),
    )
    grad_qkv = Sums(run, cut(qkv_send, 2 * rows), cut(qkv_keep, 2 * rows), full)
    grad_feed.step()
    grad_proj.step()
    df_own, df_other = on(
        k_first_back,
        (shape(inputs.shape), shape(inputs.shape, b16)),
        (d_mixed, w_qkv),
    )
    df_got = core_swap(df_other)
    out_own, out_other = on(k_feed_out, out_shapes, (acts[0], w_fc2))
    out_got = core_swap(run.now(out_other))
    grad_qkv.step()
    grad_proj.step()
    input_grad, one_sums = on(
        k_input_back,
        (shape(inputs.shape), shape((8, width))),
        (inputs, df_own, df_got, d_middle, vectors),
    )
    small_shape = shape((n, SMALL_ROWS, LANES))
    small_mine, small_theirs = on(
        bind(k_small, full, n),
        (small_shape, small_shape),
        (one_sums, mid_sums, feeds[0][4], feeds[1][4], mix_sums),
        scratch=[pltpu.VMEM((2 * n, SMALL_ROWS, LANES), f32)],
    )
    small_got = core_swap(small_theirs)
    grad_feed = grad_feed.sum()
    grad_fc2, fc1_own = grad_feed[:units], grad_feed[units:]
    small_sum = small_mine + run.now(small_got)
    small_sums = Sums(run, small_sum[few:], small_sum[:few], full)
    grad_qkv.step()
    small_sums.step()
    grad_qkv.step()
    grad_proj.step()
    fc1_from = bit_swap(fc1_own[2 * rows :], pair)
    fc1_core = core_swap(fc1_own[rows : 2 * rows])
    small_sums.step()
    outputs = on(k_output, shape(inputs.shape, b16), (middle, out_own, out_got, out_pair, vectors))
    small_sums.step()
    fc1_from = run.now(fc1_from)
    fc1_from_core = core_swap(fc1_from[rows:])
    grad_proj = grad_proj.sum()
    fc1_rows = on(
        k_columns, shape(fc1_weight.shape), (fc1_own, fc1_from, fc1_core, fc1_from_core)
    )
    small_sums.settle()

    final = small_sums.keep[0]
    vector_grads = [final[v, : a.shape[0]] for v, a in enumerate(smalls)]
    qkv_own = grad_qkv.sum()
    qkv_rows = on(
        k_rows, shape((rows, 6 * half)), (qkv_own, core_swap(qkv_own[rows:]))
    )
    return (
        outputs,
        input_grad,
        vector_grads[GAIN1],
        vector_grads[BIAS1],
        qkv_rows,
        vector_grads[QV],
        grad_proj,
        vector_grads[PROJ_B],
        vector_grads[GAIN2],
        vector_grads[BIAS2],
        fc1_rows,
        vector_grads[FC1_B],
        grad_fc2,
        vector_grads[FC2_B],
    )


def body(*args):
    whole_tiles = args[3].shape[0] % 32 == 0 and args[12].shape[0] == LANES
    return (fast_body if whole_tiles else plain_body)(*args)


def solution(mesh):
    row = P(("img", "seq"))
    mat = P(("img", "seq"), None)
    act = P("img", "seq", None)
    return jax.shard_map(
        body,
        mesh=mesh,
        in_specs=(act, act, P("img"), row, row, mat, row, mat, row, row, row, mat, row, mat, row),
        out_specs=(act, act, row, row, mat, row, mat, row, row, row, mat, row, mat, row),
        check_vma=False,
    )
```

```python
import functools

import jax
import jax.numpy as jnp
import numpy as np
from jax import lax
from jax.experimental import pallas as pl
from jax.experimental.pallas import tpu as pltpu
from jax.sharding import PartitionSpec as P

HEAD_DIM = 64
BUFFER = 64
PAIR = 2
f32 = jnp.float32
b16 = jnp.bfloat16
HIGH = lax.Precision.HIGHEST


def dot(left, right):
    return jnp.dot(left, right, preferred_element_type=f32)


def dot_tn(left, right):
    return lax.dot_general(left, right, (((0,), (0,)), ((), ())), preferred_element_type=f32)


def dot_nt(left, right):
    return lax.dot_general(left, right, (((1,), (1,)), ((), ())), preferred_element_type=f32)


def norm_parts(values):
    centre = values - jnp.mean(values, axis=-1, keepdims=True)
    scale = lax.rsqrt(jnp.mean(centre * centre, axis=-1, keepdims=True) + 1e-06)
    return centre * scale, scale


def norm_back(grad, normed, scale, gain):
    e = grad * gain
    return scale * (
        e
        - jnp.mean(e, axis=-1, keepdims=True)
        - normed * jnp.mean(e * normed, axis=-1, keepdims=True)
    )


def core_swap(value):
    return lax.ppermute(value, "seq", [(0, 1), (1, 0)])


def bit_swap(value, bits):
    n = lax.axis_size("img")
    pairs = [
        (2 * j + c, 2 * (j ^ (1 << bits[c])) + c) for j in range(n) for c in range(2)
    ]
    return lax.ppermute(value, ("img", "seq"), pairs)


def after(value, *others):
    return lax.optimization_barrier((value, *others))[0]


class Gather:
    def __init__(self, block, orders):
        self.held = None if block is None else block[None]
        self.steps = list(zip(*orders))

    def step(self, *others):
        self.sent = after(self.held, *others) if others else self.held
        self.got = bit_swap(self.sent, self.steps.pop(0))
        self.held = jnp.concatenate([self.sent, self.got], axis=0)
        return self.got


class Scatter:
    def __init__(self, send, keep, orders):
        self.send, self.keep = send, keep
        self.steps = list(zip(*orders))[::-1]

    def step(self, *others):
        send = after(self.send, *others) if others else self.send
        self.got = bit_swap(send, self.steps.pop(0))
        total = self.keep + self.got.astype(f32)
        cut = total.shape[0] // 2
        if cut:
            self.send = total[cut:].astype(send.dtype)
        self.keep = total[: max(cut, 1)]


def spread(position, order):
    return sum((((position >> k) & 1) << bit) for k, bit in enumerate(order))


def onehot(left, right):
    return (left[:, None] == right[None, :]).astype(b16)


class Places:
    def __init__(self, n, width, units, full, most):
        rows, half, few = width // (2 * n), width // 2, n // 2
        place, chips = np.arange(width), np.arange(few)
        col = np.arange(few * units)
        names = ("qkv", "fc1", "proj", "heads", "units", "chips", "owners")
        found = {name: [] for name in names}
        for me in range(n):
            for core in range(2):
                chip = me ^ spread(place // (2 * rows), full[core])
                found["qkv"].append((2 * chip + (core ^ (place // rows % 2))) * rows + place % rows)
                chip = me ^ spread(place // (4 * rows), most[core])
                chip = chip ^ ((place // (2 * rows) % 2) << PAIR)
                found["fc1"].append((2 * chip + (core ^ (place // rows % 2))) * rows + place % rows)
                source = core ^ (place // half)
                chip = me ^ np.where(
                    source == 0,
                    spread(place // rows % n, full[0]),
                    spread(place // rows % n, full[1]),
                )
                found["proj"].append((2 * chip + source) * rows + place % rows)
                found["heads"].append(source * half + place % half)
                short = lambda chip: (chip >> (PAIR + 1) << PAIR) + chip % (1 << PAIR)
                owner = me ^ spread(chips, most[core])
                found["units"].append(short(owner)[col // units] * units + col % units)
                side = (me >> PAIR) & 1
                low = 1 << PAIR
                found["owners"].append(chips // low * 2 * low + side * low + chips % low)
                found["chips"].append(me ^ spread(np.arange(n), full[core]))
        for name in names:
            setattr(self, name, np.stack(found[name]).astype(np.int32))


def live_slots(meta_ref, local, axis):
    shape = (2 * local, 1) if axis == 0 else (1, 2 * local)
    place = lax.broadcasted_iota(jnp.int32, shape, axis)
    core = meta_ref[0]
    slot = jnp.where(place < local, place + core * local, place - core * local)
    return slot < BUFFER + meta_ref[1]


def attend_kernel(meta_ref, q_ref, k_ref, v_ref, o_ref):
    live = live_slots(meta_ref, q_ref.shape[0] // 2, 1)
    outs = []
    for e in range(2):
        part = slice(e * HEAD_DIM, (e + 1) * HEAD_DIM)
        raw = dot_nt(q_ref[:, part], k_ref[:, part]) * (HEAD_DIM**-0.5)
        raw = jnp.where(live, raw, -1e30)
        expo = jnp.exp(raw - jnp.max(raw, axis=-1, keepdims=True))
        probs = expo * (1.0 / jnp.sum(expo, axis=-1, keepdims=True))
        outs.append(dot(probs.astype(b16), v_ref[:, part]))
    o_ref[...] = jnp.concatenate(outs, axis=1).astype(b16)


def attend_back_kernel(meta_ref, q_ref, k_ref, v_ref, g_ref, o_ref):
    pairs = o_ref.shape[1] // (3 * 2 * HEAD_DIM)
    live = live_slots(meta_ref, q_ref.shape[0] // 2, 0)
    scale = HEAD_DIM**-0.5
    parts = ([], [], [])
    for e in range(2):
        part = slice(e * HEAD_DIM, (e + 1) * HEAD_DIM)
        qe, ke, ve, ge = (r[:, part] for r in (q_ref, k_ref, v_ref, g_ref))
        raw = jnp.where(live, dot_nt(ke, qe) * scale, -1e30)
        expo = jnp.exp(raw - jnp.max(raw, axis=0, keepdims=True))
        probs = expo * (1.0 / jnp.sum(expo, axis=0, keepdims=True))
        d_probs = dot_nt(ve, ge)
        inner = jnp.sum(probs * d_probs, axis=0, keepdims=True)
        d_scores = (probs * (d_probs - inner)).astype(b16)
        parts[0].append(dot_tn(d_scores, ke) * scale)
        parts[1].append(dot(d_scores, qe) * scale)
        parts[2].append(dot(probs.astype(b16), ge))
    for which in range(3):
        at = pl.multiple_of((which * pairs + pl.program_id(0)) * 2 * HEAD_DIM, 2 * HEAD_DIM)
        o_ref[:, pl.ds(at, 2 * HEAD_DIM)] = jnp.concatenate(parts[which], axis=1).astype(b16)


def attention(mixed, meta, grad=None):
    slots, wide = mixed.shape
    pairs = wide // (3 * 2 * HEAD_DIM)
    block = (slots, 2 * HEAD_DIM)
    spec = lambda first: pl.BlockSpec(block, lambda h, m, f=first: (0, f + h))
    specs = [spec(0), spec(pairs), spec(2 * pairs)]
    dots = 2 * pairs * 2 * slots * slots * HEAD_DIM
    if grad is None:
        kernel, extra, out_wide, out_spec, count = attend_kernel, (), wide // 3, spec(0), 2
    else:
        kernel, extra, out_wide, count = attend_back_kernel, (grad,), wide, 5
        specs.append(spec(0))
        out_spec = pl.BlockSpec((slots, wide), lambda h, m: (0, 0))
    return pl.pallas_call(
        kernel,
        out_shape=jax.ShapeDtypeStruct((slots, out_wide), b16),
        grid_spec=pltpu.PrefetchScalarGridSpec(
            num_scalar_prefetch=1, grid=(pairs,), in_specs=specs, out_specs=out_spec
        ),
        cost_estimate=pl.CostEstimate(
            flops=4 * count * dots, bytes_accessed=4 * mixed.size, transcendentals=0
        ),
    )(meta, mixed, mixed, mixed, *extra)


def plain_body(
    inputs,
    cotangent,
    kept_counts,
    norm1_gain,
    norm1_bias,
    qkv_weight,
    qv_bias,
    proj_weight,
    proj_bias,
    norm2_gain,
    norm2_bias,
    fc1_weight,
    fc1_bias,
    fc2_weight,
    fc2_bias,
):
    images, local, width = inputs.shape
    n = lax.axis_size("img")
    me = lax.axis_index("img")
    core = lax.axis_index("seq")
    levels = n.bit_length() - 1
    half = width // 2
    rows = width // (2 * n)
    units = fc2_weight.shape[0]
    few = n // 2
    hidden = units * few
    low = 1 << PAIR
    side = (me >> PAIR) & 1

    full = tuple(tuple(range(levels - 1, 1, -1)) + last for last in ((0, 1), (1, 0)))
    most = tuple(
        (first,) + tuple(b for b in range(levels - 1, 1, -1) if b != PAIR) + (1 - first,)
        for first in (0, 1)
    )

    table = Places(n, width, units, full, most)
    dev = 2 * me + core
    pick = lambda rows_of: lax.dynamic_index_in_dim(jnp.asarray(rows_of), dev, 0, False)

    mine_of = lambda a, axis: lax.dynamic_index_in_dim(a, core, axis, False)
    theirs_of = lambda a, axis: lax.dynamic_index_in_dim(a, 1 - core, axis, False)
    smalls = (norm1_gain, norm1_bias, qv_bias, proj_bias, norm2_gain, norm2_bias, fc1_bias, fc2_bias)
    ends = [0]
    for item in smalls:
        ends.append(ends[-1] + item.shape[0])
    pair = (PAIR, PAIR)
    qkv_cut = qkv_weight.reshape(rows, 3, 2, half)
    qkv_got = core_swap(theirs_of(qkv_cut, 2))
    qkv_block = jnp.concatenate([mine_of(qkv_cut, 2), qkv_got], axis=0)
    qkv = Gather(qkv_block.reshape(2 * rows, 3 * half), full)
    x_other = core_swap(inputs)
    q_got = [qkv.step()]

    small_own = jnp.concatenate(smalls)
    small_other = core_swap(small_own)
    small = jnp.where(
        core == 0, jnp.stack([small_own, small_other]), jnp.stack([small_other, small_own])
    )
    small = Gather(small, full)
    small.step(qkv_got)

    fc1_cut = after(fc1_weight, qkv_got).reshape(rows, few // low, 2, low, 2, units)
    fc1_got = core_swap(theirs_of(fc1_cut, 4))
    fc1_block = jnp.stack([mine_of(fc1_cut, 4), fc1_got])
    side_of = lambda which: lax.dynamic_index_in_dim(fc1_block, which, 3, False)
    fc1_block = jnp.stack([side_of(side), bit_swap(side_of(1 - side), pair)])
    fc1 = Gather(fc1_block.reshape(4 * rows, hidden), most)
    fc2 = Gather(fc2_weight, most)

    q_got.append(qkv.step())
    small.step(q_got[0])
    fc2_got = fc2.step(q_got[0])
    while len(qkv.steps) > 2:
        q_got.append(qkv.step())
        small.step(q_got[-2])
    qkv.step()
    q_got.append(qkv.got)
    small.step(q_got[-2])
    proj = Gather(proj_weight, full)
    proj_got = proj.step(q_got[-2])
    fc1_first = fc1.step(fc2_got)
    qkv.step()
    q_got.append(qkv.got)
    small.step(q_got[-2])
    while len(proj.steps) > 2:
        proj_got = proj.step(q_got[-2])
    slot = core * local + lax.iota(jnp.int32, local)
    row_live = [(slot < BUFFER + kept_counts[i])[:, None] for i in range(images)]

    def to_four(own, *others):
        two = jnp.concatenate([own, bit_swap(after(own, *others), pair)], axis=0)
        return jnp.concatenate([two, core_swap(two)], axis=0)

    cotangent = after(cotangent, q_got[-3])
    up_low = [jnp.where(live, c, 0).astype(b16) for live, c in zip(row_live, cotangent)]
    up_all = [to_four(u) for u in up_low]

    dev = after(dev, q_got[0])
    abs_rows = lax.iota(jnp.int32, width)
    qkv_perm = onehot(abs_rows, pick(table.qkv))
    fc1_perm = onehot(abs_rows, pick(table.fc1))
    proj_perm = onehot(pick(table.heads), pick(table.proj))
    col_perm = onehot(lax.iota(jnp.int32, hidden), pick(table.units))
    chip_perm = onehot(lax.iota(jnp.int32, n), pick(table.chips))
    unit_perm = onehot(pick(table.owners), lax.iota(jnp.int32, n))
    x_all = jnp.stack([inputs, x_other], axis=1).reshape(images * 2 * local, width)
    normed_all, _ = norm_parts(x_all.astype(f32))
    small = dot(chip_perm, small.held.reshape(n, -1)).reshape(n, 2, -1)
    gain_one, shift_one, b_qv, b_proj, gain_two, shift_two, b_fc1, b_fc2 = (
        small[:, :, a:b].reshape(-1) for a, b in zip(ends, ends[1:])
    )
    bias_fc1 = jnp.dot(
        unit_perm.astype(f32), mine_of(b_fc1.reshape(n, 2, units), 1), precision=HIGH
    ).reshape(-1)
    qv_cut = mine_of(b_qv.reshape(2, 2, half), 1)
    bias_qkv = jnp.concatenate([qv_cut[0], jnp.zeros((half,), f32), qv_cut[1]])
    first = (normed_all * gain_one + shift_one).astype(b16)
    first = dot(first, qkv_perm).astype(b16)

    w_qkv = qkv.held.reshape(width, 3 * half)
    mixed = (dot(first, w_qkv) + bias_qkv).astype(b16).reshape(images, 2 * local, 3 * half)
    metas = [jnp.stack([core.astype(jnp.int32), kept_counts[i]]) for i in range(images)]
    proj.step(q_got[-1])
    proj.step()
    w_proj = proj.held.reshape(half, width)
    w_proj = jnp.concatenate([w_proj, core_swap(w_proj)], axis=0)
    w_proj = dot(proj_perm, w_proj).astype(b16)
    fc2_got = fc2.step(q_got[-1])
    fc1_got = fc1.step(fc2_got)
    while fc2.steps:
        fc2.step()
    w_fc2 = dot(col_perm, fc2.held.reshape(hidden, width)).astype(b16)
    while fc1.steps:
        fc1.step()
    w_fc1 = dot(fc1_perm, fc1.held.reshape(width, hidden)).astype(b16)

    attended, middle, second, normed_two, scale_two = [], [], [], [], []
    for i in range(images):
        heads = attention(mixed[i], metas[i])
        heads = jnp.concatenate([heads[:local], core_swap(heads[local:])], axis=1)
        attended.append(heads)
        middle.append(inputs[i].astype(f32) + dot(heads, w_proj) + b_proj)
        normed, scale = norm_parts(middle[i])
        normed_two.append(normed)
        scale_two.append(scale)
        second.append(to_four((normed * gain_two + shift_two).astype(b16)))

    activated, slope = [], []
    for i in range(images):
        pre = dot(second[i], w_fc1) + bias_fc1
        phi = 0.5 * (1.0 + lax.erf(pre * (0.5**0.5)))
        activated.append((pre * phi).astype(b16))
        slope.append((phi + pre * jnp.exp(-0.5 * pre * pre) * 0.3989422804014327).astype(b16))

    def core_sum(part):
        return part[: 2 * local] + core_swap(part[2 * local :].astype(b16)).astype(f32)

    def pair_sum(two):
        return two[:local] + bit_swap(two[local:].astype(b16), pair).astype(f32)

    d_pre, d_two = [], []
    for i in range(images):
        d_pre.append((slope[i].astype(f32) * dot_nt(up_all[i], w_fc2)).astype(b16))
        d_two.append(core_sum(dot_nt(d_pre[i], w_fc1)))
    out_two = [core_sum(dot(activated[i], w_fc2)) for i in range(images)]
    d_second = [pair_sum(d) for d in d_two]

    cat = lambda parts: jnp.concatenate(parts, axis=0)
    cut = hidden // 2
    up_cat = cat(up_all)
    activated = after(cat(activated), *d_two)
    activated_rel = dot(activated, col_perm).astype(b16)
    grad_fc2 = Scatter(
        dot_tn(activated_rel[:, cut:], up_cat).astype(b16).reshape(-1, units, width),
        dot_tn(activated_rel[:, :cut], up_cat).reshape(-1, units, width),
        most,
    )
    second_rel = dot(cat(second), fc1_perm).astype(b16)
    d_pre_cat = cat(d_pre)
    grad_fc1 = Scatter(
        dot_tn(second_rel[:, half:], d_pre_cat).astype(b16).reshape(-1, 4 * rows, hidden),
        dot_tn(second_rel[:, :half], d_pre_cat).reshape(-1, 4 * rows, hidden),
        most,
    )
    grad_fc2.step()
    grad_fc1.step(grad_fc2.got)
    while grad_fc2.steps:
        grad_fc2.step()
    while grad_fc1.steps:
        grad_fc1.step()

    outputs = [
        jnp.where(row_live[i], middle[i] + pair_sum(after(out_two[i], *d_second)) + b_fc2, 0.0)
        for i in range(images)
    ]
    outputs = jnp.stack(outputs).astype(b16)

    d_middle, d_branch, d_mixed = [], [], []
    for i in range(images):
        back = norm_back(d_second[i], normed_two[i], scale_two[i], gain_two)
        d_middle.append(up_low[i].astype(f32) + back)
        d_branch.append(d_middle[i].astype(b16))
        d_att = dot_nt(d_branch[i], w_proj).astype(b16)
        d_att = jnp.concatenate([d_att[:, :half], core_swap(d_att[:, half:])], axis=0)
        d_mixed.append(attention(mixed[i], metas[i], d_att))

    attended_rel = dot(cat(attended), proj_perm).astype(b16)
    attended_rel = jnp.concatenate(
        [attended_rel[:, :half], core_swap(attended_rel[:, half:])], axis=0
    )
    branch = cat(d_branch)
    branch_all = jnp.concatenate([branch, core_swap(branch)], axis=0)
    parts = lambda a: a.reshape(-1, rows, a.shape[-1])
    proj_send = dot_tn(attended_rel[:, half // 2 :], branch_all).astype(b16)
    proj_keep = dot_tn(attended_rel[:, : half // 2], branch_all)
    grad_proj = Scatter(parts(proj_send), parts(proj_keep), full)
    while grad_proj.steps:
        grad_proj.step()

    d_mixed = cat(d_mixed)
    qkv_send = dot_tn(first[:, half:], d_mixed).astype(b16)
    d_first = dot_nt(dot_nt(after(d_mixed, qkv_send), w_qkv).astype(b16), qkv_perm).astype(b16)
    d_first = d_first.reshape(images, 2, local, width)
    d_first = d_first[:, 0].astype(f32) + core_swap(d_first[:, 1]).astype(f32)
    qkv_keep = dot_tn(first[:, :half], after(d_mixed, d_first))
    cut3 = lambda a: a.reshape(-1, 2 * rows, 3 * half)
    grad_qkv = Scatter(cut3(qkv_send), cut3(qkv_keep), full)
    normed_one, scale_one = norm_parts(inputs.astype(f32))
    input_grad = jnp.stack(d_middle) + norm_back(d_first, normed_one, scale_one, gain_one)

    placed = lambda a, axis: jnp.stack(
        [jnp.where(core == 0, a, 0.0), jnp.where(core == 1, a, 0.0)], axis=axis
    )
    total = lambda a: jnp.sum(a.astype(f32).reshape(-1, a.shape[-1]), axis=0)
    d_mixed_sum = total(d_mixed).reshape(3, half)
    d_pre_sum = jnp.dot(
        unit_perm.astype(f32).T, total(d_pre_cat).reshape(few, units), precision=HIGH
    )
    d_second = jnp.stack(d_second)
    small_grads = (
        total(d_first * normed_one),
        total(d_first),
        placed(d_mixed_sum[::2], 1),
        total(branch),
        total(d_second * jnp.stack(normed_two)),
        total(d_second),
        placed(d_pre_sum, 1),
        total(jnp.stack(up_low)),
    )
    small_grads = jnp.concatenate([g.reshape(n, 2, -1) for g in small_grads], axis=2)
    small_grads = mine_of(small_grads, 1) + core_swap(theirs_of(small_grads, 1))
    small_grads = jnp.dot(chip_perm.astype(f32).T, small_grads, precision=HIGH)
    small_grads = small_grads[:, None]
    small_grads = Scatter(small_grads[few:], small_grads[:few], full)
    small_grads.step()
    grad_qkv.step()
    while grad_qkv.steps:
        small_grads.step(grad_qkv.got)
        grad_qkv.step()
    small_grads = small_grads.keep[0, 0]
    small_grads = [small_grads[a:b] for a, b in zip(ends, ends[1:])]
    grad_fc1, grad_fc2, grad_proj, grad_qkv = (
        g.keep[0] for g in (grad_fc1, grad_fc2, grad_proj, grad_qkv)
    )

    qkv_other = core_swap(grad_qkv[rows:])
    both = lambda own, other, which, axis: jnp.where(
        which == 0, jnp.stack([own, other], axis=axis), jnp.stack([other, own], axis=axis)
    )
    cut3 = lambda a: a.reshape(rows, 3, half)
    grad_qkv = both(cut3(grad_qkv[:rows]), cut3(qkv_other), core, 2).reshape(qkv_weight.shape)

    pair_other = bit_swap(grad_fc1[2 * rows :], pair)
    cut4 = lambda a: a.reshape(2 * rows, few // low, low, units)
    grad_fc1 = both(cut4(grad_fc1[: 2 * rows]), cut4(pair_other), side, 2)
    core_other = core_swap(grad_fc1[rows:])
    grad_fc1 = both(grad_fc1[:rows], core_other, core, 4).reshape(fc1_weight.shape)
    return (
        outputs,
        input_grad,
        small_grads[0],
        small_grads[1],
        grad_qkv,
        small_grads[2],
        grad_proj,
        small_grads[3],
        small_grads[4],
        small_grads[5],
        grad_fc1,
        small_grads[6],
        grad_fc2,
        small_grads[7],
    )


def pack_units_kernel(where_ref, w_ref, mine_ref, theirs_ref):
    wide = mine_ref.shape[2]
    units = 128
    low = 1 << PAIR
    for ref, core in ((mine_ref, where_ref[0]), (theirs_ref, 1 - where_ref[0])):
        for p in range(2):
            side = where_ref[1] ^ p
            for b in range(wide // units):
                chip = (b // low) * 2 * low + side * low + b % low
                at = pl.multiple_of((2 * chip + core) * units, units)
                ref[p, :, b * units : (b + 1) * units] = w_ref[:, pl.ds(at, units)]


def pack_units(weight, units, core, side):
    rows, hidden = weight.shape
    if units == 128:
        out = jax.ShapeDtypeStruct((2, rows, hidden // 4), weight.dtype)
        return pl.pallas_call(
            pack_units_kernel,
            out_shape=(out, out),
            in_specs=[pl.BlockSpec(memory_space=pltpu.SMEM), pl.BlockSpec(memory_space=pltpu.VMEM)],
            out_specs=(pl.BlockSpec(memory_space=pltpu.VMEM),) * 2,
        )(jnp.stack([core, side]), weight)
    low = 1 << PAIR
    cut = weight.reshape(rows, -1, 2, low, 2, units)

    def part(c, p):
        block = lax.dynamic_index_in_dim(cut, c, 4, False)
        return lax.dynamic_index_in_dim(block, p, 2, False).reshape(rows, hidden // 4)

    return tuple(jnp.stack([part(c, side), part(c, 1 - side)]) for c in (core, 1 - core))


LANES = 128
MEASURED_US = {
    "k_pack_heads": 1.6, "k_heads": 7, "k_attend": 6, "k_project": 0.1,
    "k_feed_first": 14, "k_feed": 10, "k_feed_out": 3, "k_pair_send": 0.2, "k_grad_feed": 15,
    "k_middle_back": 30, "k_attend_back": 8, "k_grad_proj": 0.2, "k_grad_heads": 8.7,
    "k_first_back": 6, "k_input_back": 4.3, "k_small": 2, "k_output": 4, "k_columns": 2, "k_rows": 1.8,
}
FLOPS_PER_US = 3e9
VMEM_LIMIT = 56 * 1024 * 1024
SMALL_ROWS = 8
GAIN1, BIAS1, QV, PROJ_B, GAIN2, BIAS2, FC1_B, FC2_B = range(8)


def spread_of(position, orders, core):
    a, b = (spread(position, order) for order in orders)
    return a if a == b else jnp.where(core == 0, a, b)


def position_of(bits, orders, core):
    a, b = (
        sum((((bits >> bit) & 1) << k) for k, bit in enumerate(order)) for order in orders
    )
    return jnp.where(core == 0, a, b)


def call(kernel, out, args, grid=None, in_specs=None, out_specs=None, scratch=(), deps=(), kept=0, us=None, place=None):
    whole = pl.BlockSpec(memory_space=pltpu.VMEM)
    outs = out if isinstance(out, tuple) else (out,)
    specs = [pl.BlockSpec(memory_space=pltpu.SMEM)] + list(in_specs or [whole] * len(args))
    out_specs = out_specs if out_specs is not None else tuple(whole for _ in outs)
    extra = {} if grid is None else {"grid": grid}
    name = getattr(kernel, "func", kernel).__name__
    flops = int((us or MEASURED_US[name]) * FLOPS_PER_US)
    if deps:
        specs += [pl.BlockSpec(memory_space=pl.ANY)] * len(deps)
        inner, count = kernel, 1 + len(args)

        def kernel(*refs):
            return inner(*refs[:count], *refs[count + len(deps) :])

        extra["input_output_aliases"] = {count + k: k for k in range(kept)}
    result = pl.pallas_call(
        kernel,
        out_shape=outs,
        in_specs=specs,
        out_specs=tuple(out_specs),
        scratch_shapes=list(scratch),
        compiler_params=pltpu.CompilerParams(vmem_limit_bytes=VMEM_LIMIT),
        cost_estimate=pl.CostEstimate(flops=flops, bytes_accessed=1000, transcendentals=0),
        **extra,
    )(place, *args, *deps)
    return result if isinstance(out, tuple) else result[0]


class Order:
    def __init__(self, place):
        self.place, self.last = place, ()

    def call(self, *args, wait=(), **named):
        result = call(*args, deps=tuple(wait) + self.last, place=self.place, **named)
        found = result if isinstance(result, tuple) else (result,)
        self.last = (min(found, key=lambda a: a.size),)
        return result

    def now(self, *values):
        values = lax.optimization_barrier((*values, *self.last))
        self.last = tuple(values[len(values) - len(self.last) :])
        values = values[: len(values) - len(self.last)]
        return values if len(values) > 1 else values[0]


def tie(*values):
    return lax.optimization_barrier(values)


def shape(dims, dtype=f32):
    return jax.ShapeDtypeStruct(tuple(dims), dtype)


def aligned(index, step):
    return pl.multiple_of(index * step, step)


def k_pack_heads(place, w, small, theirs, mine):
    three = w.shape[1]
    half = three // 6
    me_core = lax.axis_index("seq")
    for ref, core in ((mine, me_core), (theirs, 1 - me_core)):
        for which in range(3):
            at = pl.multiple_of((which * 2 + core) * half, half)
            ref[:, which * half : (which + 1) * half] = w[:, pl.ds(at, half)]
        ref[:, 3 * half :] = jnp.zeros((w.shape[0], LANES), b16)
        ref[:SMALL_ROWS, 3 * half :] = small[...]


def k_heads(orders, place, sent, got, x_own, x_other, w_qkv, vectors, first, mixed, small):
    me, core, side = place[0], place[1], place[2]
    blocks, two_rows, lanes = sent.shape
    n = 2 * blocks
    rows = two_rows // 2
    three = w_qkv.shape[1]
    half = three // 3
    for p in range(n):
        block = sent if p < blocks else got
        at = p % blocks
        chip = me ^ spread_of(p, orders, core)
        for c in range(2):
            dev = 2 * chip + (core ^ c)
            part = slice(c * rows, (c + 1) * rows)
            w_qkv[pl.ds(aligned(dev, rows), rows), :] = block[at, part, :three]
            small[dev] = block[at, c * rows : c * rows + SMALL_ROWS, three:].astype(f32)

    def lane_block(first_dev, vector, size):
        total = small[first_dev, vector : vector + 1, :]
        for i in range(1, LANES // size):
            total += pltpu.roll(small[first_dev + i, vector : vector + 1, :], i * size, 1)
        return total

    width = w_qkv.shape[0]
    per = width // (2 * n)
    for row, vector in enumerate((GAIN1, BIAS1, PROJ_B, GAIN2, BIAS2, FC2_B)):
        for q in range(width // LANES):
            vectors[row : row + 1, q * LANES : (q + 1) * LANES] = lane_block(
                q * (LANES // per), vector, per
            )
    for which in range(2):
        for q in range(half // LANES):
            dev = (which * 2 + core) * (half // (2 * per)) + q * (LANES // (2 * per))
            at = which * half + q * LANES
            vectors[6:7, at : at + LANES] = lane_block(dev, QV, 2 * per)
    low = 1 << PAIR
    for b in range(n // 2):
        chip = (b // low) * 2 * low + side * low + b % low
        vectors[7:8, b * LANES : (b + 1) * LANES] = small[2 * chip + core, FC1_B : FC1_B + 1, :]

    images, local, _ = x_own.shape
    for i in range(images):
        for c, ref in enumerate((x_own, x_other)):
            normed, _ = norm_parts(ref[i].astype(f32))
            at = (2 * i + c) * local
            first[at : at + local, :] = (
                normed * vectors[0:1, :] + vectors[1:2, :]
            ).astype(b16)
    for which in range(3):
        part = slice(which * half, (which + 1) * half)
        total = dot(first[...], w_qkv[:, part])
        if which != 1:
            total += vectors[6:7, (which // 2) * half : (which // 2 + 1) * half]
        mixed[:, part] = total.astype(b16)


def k_pair_send(place, own0, got0, own1, got1, send0, send1):
    for own, got, send in ((own0, got0, send0), (own1, got1, send1)):
        send[...] = (own[...] + got[...].astype(f32)).astype(b16)


def k_output(place, middle, own, got, pair_got, vectors, out):
    images, local, _ = out.shape
    slot = place[1] * local + lax.broadcasted_iota(jnp.int32, (local, 1), 0)
    for i in range(images):
        part = slice(i * local, (i + 1) * local)
        total = middle[part, :] + vectors[5:6, :] + own[part, :]
        total += got[part, :].astype(f32) + pair_got[part, :].astype(f32)
        out[i] = jnp.where(slot < BUFFER + place[3 + i], total, 0.0).astype(b16)


def k_unpack_units(orders, place, sent, got, w_fc1, w_fc2):
    me, core = place[0], place[1]
    blocks = sent.shape[0]
    units = LANES
    rows = (sent.shape[1] - units) // 4
    low = 1 << PAIR
    for p in range(2 * blocks):
        block = sent if p < blocks else got
        at = p % blocks
        chip = me ^ spread_of(p, orders, core)
        for c2 in range(2):
            for c in range(2):
                dev = 2 * (chip ^ (c2 << PAIR)) + (core ^ c)
                k = 2 * c2 + c
                w_fc1[pl.ds(aligned(dev, rows), rows), :] = block[at, k * rows : (k + 1) * rows, :]
        short = ((chip >> (PAIR + 1)) << PAIR) + (chip & (low - 1))
        w_fc2[pl.ds(aligned(short, units), units), :] = block[at, 4 * rows :, :]


def live_of(place, image, local, axis):
    dims = (2 * local, 1) if axis == 0 else (1, 2 * local)
    at = lax.broadcasted_iota(jnp.int32, dims, axis)
    core = place[1]
    slot = jnp.where(at < local, at + core * local, at - core * local)
    return slot < BUFFER + place[3 + image]


def k_attend(image, place, q, k, v, own, other):
    local = own.shape[0]
    live = live_of(place, image, local, 1)
    outs = []
    for e in range(2):
        part = slice(e * HEAD_DIM, (e + 1) * HEAD_DIM)
        raw = dot_nt(q[:, part] * (HEAD_DIM**-0.5), k[:, part])
        raw = jnp.where(live, raw, -1e30)
        expo = jnp.exp(raw - jnp.max(raw, axis=-1, keepdims=True))
        probs = expo * (1.0 / jnp.sum(expo, axis=-1, keepdims=True))
        outs.append(dot(probs.astype(b16), v[:, part]))
    both = jnp.concatenate(outs, axis=1).astype(b16)
    own[...] = both[:local]
    other[...] = both[local:]


def k_attend_back(image, place, q, k, v, g_own, g_other, d_mixed, sums):
    local = g_own.shape[0]
    pairs = pl.num_programs(0)
    live = live_of(place, image, local, 0)
    scale = HEAD_DIM**-0.5
    g = jnp.concatenate([g_own[...], g_other[...]], axis=0)
    parts = ([], [], [])
    for e in range(2):
        part = slice(e * HEAD_DIM, (e + 1) * HEAD_DIM)
        qe, ke, ve, ge = q[:, part], k[:, part], v[:, part], g[:, part]
        raw = jnp.where(live, dot_nt(ke, qe * scale), -1e30)
        expo = jnp.exp(raw - jnp.max(raw, axis=0, keepdims=True))
        probs = expo * (1.0 / jnp.sum(expo, axis=0, keepdims=True))
        d_probs = dot_nt(ve, ge)
        inner = jnp.sum(probs * d_probs, axis=0, keepdims=True)
        d_scores = (probs * (d_probs - inner)).astype(b16)
        parts[0].append(dot_tn(d_scores, ke) * scale)
        parts[1].append(dot(d_scores, qe) * scale)
        parts[2].append(dot(probs.astype(b16), ge))
    for which in range(3):
        at = pl.multiple_of((which * pairs + pl.program_id(0)) * LANES, LANES)
        value = jnp.concatenate(parts[which], axis=1).astype(b16)
        d_mixed[:, pl.ds(at, LANES)] = value
        total = jnp.sum(value.astype(f32), axis=0, keepdims=True)
        sums[:, pl.ds(at, LANES)] = jnp.broadcast_to(total, (8, LANES))


def k_project(orders, place, sent, got, sent_far, got_far, own0, own1, got0, got1, x, vectors,
              w, middle, second):
    me, core = place[0], place[1]
    blocks, rows, _ = sent.shape
    for c, refs in enumerate(((sent, got), (sent_far, got_far))):
        for p in range(2 * blocks):
            chip = me ^ spread_of(p, orders, core ^ c)
            at = aligned(2 * chip + (core ^ c), rows)
            w[pl.ds(at, rows), :] = refs[p // blocks][p % blocks]
    half = own0.shape[1]
    images, local, _ = x.shape
    both = lambda a, b: jnp.concatenate([a[...], b[...]], axis=0)
    total = dot(both(own0, own1), w[pl.ds(aligned(core, half), half), :])
    total += dot(both(got0, got1), w[pl.ds(aligned(1 - core, half), half), :])
    for i in range(images):
        part = slice(i * local, (i + 1) * local)
        mid = x[i].astype(f32) + total[part] + vectors[2:3, :]
        middle[part, :] = mid
        normed, _ = norm_parts(mid)
        second[part, :] = (normed * vectors[3:4, :] + vectors[4:5, :]).astype(b16)


def k_feed(place, s0, s1, u0, u1, w1, w2, vectors, act, d_pre, ds_own, ds_other, sums, sec, up):
    images, local, _ = u0.shape
    tokens = images * local
    tile = 256
    for k, (s, u) in enumerate(((s0, u0), (s1, u1))):
        sec[k * tokens : (k + 1) * tokens, :] = s[...]
        for i in range(images):
            at = k * tokens + i * local
            up[at : at + local, :] = u[i]
    for at in range(0, w1.shape[1], tile):
        part = slice(at, at + tile)
        pre = dot(sec[...], w1[:, part]) + vectors[7:8, part]
        phi = 0.5 * (1.0 + lax.erf(pre * (0.5**0.5)))
        act[:, part] = (pre * phi).astype(b16)
        slope = phi + pre * jnp.exp(-0.5 * pre * pre) * 0.3989422804014327
        grad = (slope * dot_nt(up[...], w2[part, :])).astype(b16)
        d_pre[:, part] = grad
        total = jnp.sum(grad.astype(f32), axis=0, keepdims=True)
        sums[:, part] = jnp.broadcast_to(total, (8, tile))
    ds_other[...] = dot_nt(d_pre[tokens:, :], w1[...]).astype(b16)
    ds_own[...] = dot_nt(d_pre[:tokens, :], w1[...])


def k_feed_first(orders, place, sent, got, s0, s1, u0, u1, vectors, w1, w2, *outs):
    k_unpack_units(orders, place, sent, got, w1, w2)
    k_feed(place, s0, s1, u0, u1, w1, w2, vectors, *outs)


def k_feed_out(place, act, w2, own, other):
    tokens = own.shape[0]
    other[...] = dot(act[tokens:, :], w2[...]).astype(b16)
    own[...] = dot(act[:tokens, :], w2[...])


def k_middle_back(place, ds_own, ds_got, pair_got, middle, up, w, vectors,
                  d_middle, d_branch, att_own, att_other, sums):
    core = place[1]
    images, local, _ = up.shape
    half = att_own.shape[1]
    total = lambda a: jnp.sum(a, axis=0, keepdims=True)
    rows = [0.0] * 4
    for i in range(images):
        part = slice(i * local, (i + 1) * local)
        d_second = ds_own[part, :] + ds_got[part, :].astype(f32) + pair_got[part, :].astype(f32)
        normed, scale = norm_parts(middle[part, :])
        upstream = up[i].astype(f32)
        d_mid = upstream + norm_back(d_second, normed, scale, vectors[3:4, :])
        d_middle[part, :] = d_mid
        branch = d_mid.astype(b16)
        d_branch[part, :] = branch
        rows[0] += total(d_second * normed)
        rows[1] += total(d_second)
        rows[2] += total(branch.astype(f32))
        rows[3] += total(upstream)
    branch = d_branch[...]
    att_other[...] = dot_nt(branch, w[pl.ds(aligned(1 - core, half), half), :]).astype(b16)
    att_own[...] = dot_nt(branch, w[pl.ds(aligned(core, half), half), :]).astype(b16)
    for r in range(4):
        sums[r : r + 1, :] = rows[r]
    sums[4:, :] = jnp.zeros((4, sums.shape[1]), f32)


def put(held, row, value):
    held[pl.ds(pl.multiple_of(row, value.shape[0]), value.shape[0]), :] = value.astype(b16)


def split(held, send, keep):
    cut = send.shape[0]
    send[...] = held[cut:, :]
    keep[...] = held[:cut, :]


def k_grad_heads(orders, n, place, left, right, send, keep, held):
    me, core = place[0], place[1]
    tile = 256
    rows = held.shape[0] // (2 * n)
    for step in range(left.shape[1] // tile):
        total = dot_tn(left[:, step * tile : (step + 1) * tile], right[...])
        for i in range(tile // rows):
            dev = step * (tile // rows) + i
            at = position_of(me ^ (dev // 2), orders, core)
            value = total[i * rows : (i + 1) * rows, :]
            put(held, at * 2 * rows + (core ^ (dev % 2)) * rows, value)
    split(held, send, keep)


def k_grad_feed(orders, n, place, a0, a1, u0, u1, s0, s1, d0, d1, send, keep, held):
    me, core, side = place[0], place[1], place[2]
    low = 1 << PAIR
    tile = 256
    per = 2 * send.shape[0] // (n // 2)
    rows = (per - LANES) // 4
    for step in range(a0.shape[1] // tile):
        part = slice(step * tile, (step + 1) * tile)
        total = dot_tn(a0[:, part], u0[...]) + dot_tn(a1[:, part], u1[...])
        for i in range(tile // LANES):
            b = step * (tile // LANES) + i
            chip = (b // low) * 2 * low + side * low + b % low
            at = position_of(me ^ chip, orders, core)
            put(held, at * per, total[i * LANES : (i + 1) * LANES, :])
    for step in range(s0.shape[1] // tile):
        part = slice(step * tile, (step + 1) * tile)
        total = dot_tn(s0[:, part], d0[...]) + dot_tn(s1[:, part], d1[...])
        for i in range(tile // rows):
            dev = step * (tile // rows) + i
            bits = me ^ (dev // 2)
            at = position_of(bits, orders, core)
            inner = LANES + (((bits >> PAIR) & 1) * 2 + (core ^ (i % 2))) * rows
            put(held, at * per + inner, total[i * rows : (i + 1) * rows, :])
    split(held, send, keep)


def k_grad_proj(orders, place, *refs):
    lefts, rights, (send, keep, held) = (refs[:4], refs[4:8]), refs[8:10], refs[10:]
    me, core = place[0], place[1]
    rows = 32
    right = jnp.concatenate([a[...] for a in rights], axis=0)
    count = lefts[0][0].shape[1] // (2 * rows)
    for which in range(2):
        left = jnp.concatenate([a[...] for a in lefts[which]], axis=0)
        total = dot_tn(left, right)
        for i in range(count):
            chip = (core ^ which) * count + i
            at = position_of(me ^ chip, orders, core)
            value = jnp.where(
                core == 0,
                total[2 * i * rows : (2 * i + 1) * rows, :],
                total[(2 * i + 1) * rows : (2 * i + 2) * rows, :],
            )
            put(held, at * rows, value)
    split(held, send, keep)


def k_first_back(place, d, w, own, other):
    images, local, width = own.shape
    tile = 256
    for step in range(width // tile):
        part = slice(step * tile, (step + 1) * tile)
        total = dot_nt(d[...], w[part, :])
        for i in range(images):
            at = 2 * i * local
            own[i, :, part] = total[at : at + local]
            other[i, :, part] = total[at + local : at + 2 * local].astype(b16)


def k_input_back(place, x, own, got, mid, vectors, grad, sums):
    total = lambda a: jnp.sum(a, axis=0, keepdims=True)
    images, local, _ = x.shape
    gains = biases = 0.0
    for i in range(images):
        normed, scale = norm_parts(x[i].astype(f32))
        d_first = own[i] + got[i].astype(f32)
        back = norm_back(d_first, normed, scale, vectors[0:1, :])
        grad[i] = mid[i * local : (i + 1) * local, :] + back
        gains += total(d_first * normed)
        biases += total(d_first)
    sums[0:1, :] = gains
    sums[1:2, :] = biases
    sums[2:, :] = jnp.zeros((6, sums.shape[1]), f32)


def k_small(orders, n, place, one, mids, pre0, pre1, mix, mine, theirs, small):
    me, core, side = place[0], place[1], place[2]
    width = one.shape[1]
    per = width // (2 * n)
    half = width // 2
    pres = pre0[...] + pre1[...]
    mixes = mix[:8, :] + mix[8:, :]
    small[...] = jnp.zeros(small.shape, f32)
    rows = (
        (GAIN1, one[0:1, :]),
        (BIAS1, one[1:2, :]),
        (GAIN2, mids[0:1, :]),
        (BIAS2, mids[1:2, :]),
        (PROJ_B, mids[2:3, :]),
        (FC2_B, mids[3:4, :]),
    )
    lane = lambda row, q: row[:, q * LANES : (q + 1) * LANES]
    for vector, row in rows:
        for dev in range(2 * n):
            q, i = divmod(dev * per, LANES)
            part = lane(row, q)
            small[dev, vector : vector + 1, :] = part if i == 0 else pltpu.roll(part, LANES - i, 1)
    for which in range(2):
        row = mixes[0:1, 2 * which * half : (2 * which + 1) * half]
        for dev in range(half // (2 * per)):
            q, i = divmod(dev * 2 * per, LANES)
            part = lane(row, q)
            part = part if i == 0 else pltpu.roll(part, LANES - i, 1)
            small[(2 * which + core) * (half // (2 * per)) + dev, QV : QV + 1, :] = part
    low = 1 << PAIR
    for b in range(n // 2):
        chip = (b // low) * 2 * low + side * low + b % low
        small[2 * chip + core, FC1_B : FC1_B + 1, :] = lane(pres[0:1, :], b)
    for p in range(n):
        mine[p] = small[2 * (me ^ spread_of(p, orders, core)) + core]
        theirs[p] = small[2 * (me ^ spread_of(p, orders, 1 - core)) + 1 - core]


def k_rows(place, own, got, out):
    core = place[1]
    half = out.shape[1] // 6
    for which in range(3):
        part = slice(which * half, (which + 1) * half)
        at = pl.multiple_of((2 * which + core) * half, half)
        out[:, pl.ds(at, half)] = own[: out.shape[0], part]
        at = pl.multiple_of((2 * which + 1 - core) * half, half)
        out[:, pl.ds(at, half)] = got[:, part]


def k_columns(place, own, own_pair, got, got_pair, out):
    core, side = place[1], place[2]
    low = 1 << PAIR
    rows = out.shape[0]
    for ref, c, s in (
        (own, core, side),
        (own_pair, core, 1 - side),
        (got, 1 - core, side),
        (got_pair, 1 - core, 1 - side),
    ):
        for b in range(ref.shape[1] // LANES):
            chip = (b // low) * 2 * low + s * low + b % low
            at = pl.multiple_of((2 * chip + c) * LANES, LANES)
            out[:, pl.ds(at, LANES)] = ref[:rows, b * LANES : (b + 1) * LANES]


class Sums:
    def __init__(self, run, send, keep, orders):
        self.run, self.send, self.keep, self.got = run, send, keep, None
        self.steps = list(zip(*orders))[::-1]
        self.step()

    def settle(self):
        got = self.run.now(self.got)
        cut = got.shape[0] // 2
        if cut:
            total = self.keep[cut:].astype(f32) + got[cut:].astype(f32)
            self.send = total.astype(self.send.dtype)
            self.keep = self.keep[:cut].astype(f32) + got[:cut].astype(f32)
        else:
            self.keep = self.keep.astype(f32) + got.astype(f32)
        self.got = None

    def step(self):
        if self.got is not None:
            self.settle()
        self.got = bit_swap(self.send, self.steps.pop(0))

    def sum(self):
        while self.steps:
            self.step()
        self.settle()
        return self.keep[0]


def fast_body(
    inputs,
    cotangent,
    kept_counts,
    norm1_gain,
    norm1_bias,
    qkv_weight,
    qv_bias,
    proj_weight,
    proj_bias,
    norm2_gain,
    norm2_bias,
    fc1_weight,
    fc1_bias,
    fc2_weight,
    fc2_bias,
):
    images, local, width = inputs.shape
    n = lax.axis_size("img")
    me = lax.axis_index("img")
    core = lax.axis_index("seq")
    levels = n.bit_length() - 1
    half = width // 2
    rows = width // (2 * n)
    units = fc2_weight.shape[0]
    few = n // 2
    hidden = units * few
    side = (me >> PAIR) & 1
    pair = (PAIR, PAIR)
    full = tuple(tuple(range(levels - 1, 1, -1)) + last for last in ((0, 1), (1, 0)))
    most = tuple(tuple(b for b in order if b != PAIR) for order in full)
    last = tuple(order[-2:] + order[:-2] for order in full)
    place = jnp.concatenate([jnp.stack([me, core, side]).astype(jnp.int32), kept_counts])
    run = Order(place)
    on = run.call
    bind = functools.partial
    block = lambda dims, index: pl.BlockSpec(dims, index)
    whole = pl.BlockSpec(memory_space=pltpu.VMEM)

    smalls = (norm1_gain, norm1_bias, qv_bias, proj_bias, norm2_gain, norm2_bias, fc1_bias, fc2_bias)
    small = sum(
        jnp.pad(a[None], ((i, 7 - i), (0, LANES - a.shape[0]))) for i, a in enumerate(smalls)
    )
    packed = shape((rows, 3 * half + LANES), b16)
    theirs, mine = call(k_pack_heads, (packed, packed), (qkv_weight, small), place=kept_counts)
    fc1_mine, fc1_theirs = pack_units(fc1_weight, units, core, side)
    heads = Gather(jnp.concatenate([mine, core_swap(theirs)], axis=0), full)
    fc1_got = core_swap(fc1_theirs)
    x_other = core_swap(inputs)
    slot = core * local + lax.iota(jnp.int32, local)
    row_live = slot[None, :] < BUFFER + kept_counts[:, None]
    up = jnp.where(row_live[:, :, None], cotangent, 0).astype(b16)
    up_other = core_swap(up)
    fc1_send = jnp.concatenate([fc1_mine[1], fc1_got[1]], axis=0)
    proj = Gather(proj_weight, last)

    heads.step()
    fc1_pair = bit_swap(fc1_send, pair)
    heads.held, proj.held, fc1_pair, x_other, up_other = tie(
        heads.held, proj.held, fc1_pair, x_other, up_other
    )
    heads.step()
    proj.step()
    fc2 = Gather(fc2_weight, most)
    heads.held, proj.held, fc2.held = tie(heads.held, proj.held, fc2.held)
    while len(heads.steps) > 1:
        heads.step()
    proj.step()
    fc2.step()
    fc1 = Gather(jnp.concatenate([fc1_mine[0], fc1_got[0], fc1_pair], axis=0), most)
    heads.held, proj.held, fc1.held, fc2.held, up = tie(
        heads.held, proj.held, fc1.held, fc2.held, up
    )
    heads.step()
    fc1.step()
    up_pair = bit_swap(up, pair)
    heads.got, fc1.held, proj.held, up_pair = tie(heads.got, fc1.held, proj.held, up_pair)
    up_other_pair = core_swap(up_pair)
    feed = Gather(None, most)
    feed.steps = fc1.steps
    feed.held = jnp.concatenate([fc1.held, fc2.held], axis=1)
    feed.step()
    proj.step()

    tokens = images * 2 * local
    w_qkv, vectors, first, mixed = on(
        bind(k_heads, full),
        (
            shape((width, 3 * half), b16),
            shape((8, width)),
            shape((tokens, width), b16),
            shape((tokens, 3 * half), b16),
        ),
        (heads.sent, heads.got, inputs, x_other),
        scratch=[pltpu.VMEM((2 * n, SMALL_ROWS, LANES), f32)],
    )
    pairs = half // LANES
    slots = 2 * local
    head_specs = lambda i: [
        block((slots, LANES), lambda h, i=i, f=f: (i, f + h)) for f in (0, pairs, 2 * pairs)
    ]
    lane_spec = block((local, LANES), lambda h: (0, h))
    tok = images * local
    flat = lambda cols, dtype=f32: shape((tok, cols), dtype)
    att_own, att_other, att_got = [], [], []
    for i in range(images):
        own, other = on(
            bind(k_attend, i),
            (shape((local, half), b16),) * 2,
            (mixed, mixed, mixed),
            grid=(pairs,),
            in_specs=head_specs(i),
            out_specs=[lane_spec, lane_spec],
        )
        att_own.append(own)
        att_other.append(other)
        att_got.append(core_swap(other))
        if i == 0:
            proj.got, feed.got = run.now(proj.got, feed.got)
            proj.held = jnp.concatenate([proj.sent, proj.got], axis=0)
            feed.held = jnp.concatenate([feed.sent, feed.got], axis=0)
            feed.step()
            proj.step()
            proj_sent_far = core_swap(proj.sent)
    proj.got = run.now(proj.got)
    proj_far = proj_sent_far, core_swap(proj.got)
    w_proj, middle, second = on(
        bind(k_project, last),
        (shape((width, width), b16), flat(width), flat(width, b16)),
        (proj.sent, proj.got, *proj_far, *att_own, *att_got, inputs, vectors),
    )
    second_other = core_swap(second)
    second_pair = bit_swap(second, pair)
    tile = 256
    fixed = lambda dims: block(dims, lambda *_: (0,) * len(dims))
    wide_rows = lambda cols: shape((2 * tok, cols), b16)
    feed_shapes = (
        wide_rows(hidden), wide_rows(hidden), flat(width), flat(width, b16), shape((8, hidden)),
        wide_rows(width), wide_rows(width),
    )
    feeds = []
    w_fc1, w_fc2, *own_feed = on(
        bind(k_feed_first, most),
        (shape((width, hidden), b16), shape((hidden, width), b16)) + feed_shapes,
        (feed.sent, feed.got, second, second_other, up, up_other, vectors),
    )
    feeds.append(own_feed)
    second_pair = run.now(second_pair)
    second_other_pair = core_swap(second_pair)
    feeds.append(
        on(
            k_feed,
            feed_shapes,
            (second_pair, second_other_pair, up_pair, up_other_pair, w_fc1, w_fc2, vectors),
        )
    )
    ds_pair_got = core_swap(feeds[1][3])
    out_shapes = (flat(width), flat(width, b16))
    out_pair_own, out_pair_other = on(k_feed_out, out_shapes, (feeds[1][0], w_fc2))
    out_pair_got = core_swap(out_pair_other)

    acts = [f[0] for f in feeds]
    d_pres = [f[1] for f in feeds]
    ds_send, out_send = on(
        k_pair_send,
        (flat(width, b16),) * 2,
        (feeds[1][2], ds_pair_got, out_pair_own, out_pair_got),
    )
    pair_got = bit_swap(ds_send, pair)
    ds_got = core_swap(run.now(feeds[0][3]))
    halves = lambda count, cols: (shape((count, cols), b16), shape((count, cols), b16))
    held = lambda count, cols: [pltpu.VMEM((2 * count, cols), b16)]
    cut = lambda a, per: a.reshape(-1, per, a.shape[-1])
    feed_send, feed_keep = on(
        bind(k_grad_feed, most, n),
        halves(few // 2 * (4 * rows + units), width),
        (*acts, *[f[6] for f in feeds], *[f[5] for f in feeds], *d_pres),
        scratch=held(few // 2 * (4 * rows + units), width),
    )
    grad_feed = Sums(run, cut(feed_send, 4 * rows + units), cut(feed_keep, 4 * rows + units), most)

    out_pair = bit_swap(run.now(out_send), pair)
    d_middle, d_branch, d_att, d_att_other, mid_sums = on(
        k_middle_back,
        (flat(width), flat(width, b16), flat(half, b16), flat(half, b16), shape((8, width))),
        (feeds[0][2], ds_got, pair_got, middle, up, w_proj, vectors),
    )
    d_att_got = core_swap(d_att_other)
    att_far, d_branch_far = [core_swap(a) for a in att_own], core_swap(d_branch)
    d_mixed, mix_sums = (), ()
    for i in range(images):
        part = block((local, LANES), lambda h, i=i: (i, h))
        d_mixed, mix_sums = on(
            bind(k_attend_back, i),
            (shape((tokens, 3 * half), b16), shape((8 * images, 3 * half))),
            (mixed, mixed, mixed, d_att, d_att_got),
            grid=(pairs,),
            in_specs=head_specs(i) + [part, part],
            out_specs=[
                block((slots, 3 * half), lambda h, i=i: (i, 0)),
                block((8, 3 * half), lambda h, i=i: (i, 0)),
            ],
            wait=(d_mixed, mix_sums) if i > 0 else (),
            kept=2 if i > 0 else 0,
            us=8 if i > 0 else 0.2,
        )
        if i == 0:
            proj_send, proj_keep = on(
                bind(k_grad_proj, full),
                halves(half // 2, width),
                (*att_own, *att_other, *att_got, *att_far, d_branch, d_branch_far),
                scratch=held(half // 2, width),
            )
            grad_proj = Sums(run, cut(proj_send, rows), cut(proj_keep, rows), full)
            grad_feed.step()
    qkv_send, qkv_keep = on(
        bind(k_grad_heads, full, n),
        halves(half, 3 * half),
        (first, d_mixed),
        scratch=held(half, 3 * half),
    )
    grad_qkv = Sums(run, cut(qkv_send, 2 * rows), cut(qkv_keep, 2 * rows), full)
    grad_feed.step()
    grad_proj.step()
    df_own, df_other = on(
        k_first_back,
        (shape(inputs.shape), shape(inputs.shape, b16)),
        (d_mixed, w_qkv),
    )
    df_got = core_swap(df_other)
    out_own, out_other = on(k_feed_out, out_shapes, (acts[0], w_fc2))
    out_got = core_swap(run.now(out_other))
    grad_qkv.step()
    grad_proj.step()
    input_grad, one_sums = on(
        k_input_back,
        (shape(inputs.shape), shape((8, width))),
        (inputs, df_own, df_got, d_middle, vectors),
    )
    small_shape = shape((n, SMALL_ROWS, LANES))
    small_mine, small_theirs = on(
        bind(k_small, full, n),
        (small_shape, small_shape),
        (one_sums, mid_sums, feeds[0][4], feeds[1][4], mix_sums),
        scratch=[pltpu.VMEM((2 * n, SMALL_ROWS, LANES), f32)],
    )
    small_got = core_swap(small_theirs)
    grad_feed = grad_feed.sum()
    grad_fc2, fc1_own = grad_feed[:units], grad_feed[units:]
    small_sum = small_mine + run.now(small_got)
    small_sums = Sums(run, small_sum[few:], small_sum[:few], full)
    grad_qkv.step()
    small_sums.step()
    grad_qkv.step()
    grad_proj.step()
    fc1_from = bit_swap(fc1_own[2 * rows :], pair)
    fc1_core = core_swap(fc1_own[rows : 2 * rows])
    small_sums.step()
    outputs = on(k_output, shape(inputs.shape, b16), (middle, out_own, out_got, out_pair, vectors))
    small_sums.step()
    fc1_from = run.now(fc1_from)
    fc1_from_core = core_swap(fc1_from[rows:])
    grad_proj = grad_proj.sum()
    fc1_rows = on(
        k_columns, shape(fc1_weight.shape), (fc1_own, fc1_from, fc1_core, fc1_from_core)
    )
    small_sums.settle()

    final = small_sums.keep[0]
    vector_grads = [final[v, : a.shape[0]] for v, a in enumerate(smalls)]
    qkv_own = grad_qkv.sum()
    qkv_rows = on(
        k_rows, shape((rows, 6 * half)), (qkv_own, core_swap(qkv_own[rows:]))
    )
    return (
        outputs,
        input_grad,
        vector_grads[GAIN1],
        vector_grads[BIAS1],
        qkv_rows,
        vector_grads[QV],
        grad_proj,
        vector_grads[PROJ_B],
        vector_grads[GAIN2],
        vector_grads[BIAS2],
        fc1_rows,
        vector_grads[FC1_B],
        grad_fc2,
        vector_grads[FC2_B],
    )


def body(*args):
    whole_tiles = args[3].shape[0] % 32 == 0 and args[12].shape[0] == LANES
    return (fast_body if whole_tiles else plain_body)(*args)


def solution(mesh):
    row = P(("img", "seq"))
    mat = P(("img", "seq"), None)
    act = P("img", "seq", None)
    return jax.shard_map(
        body,
        mesh=mesh,
        in_specs=(act, act, P("img"), row, row, mat, row, mat, row, row, row, mat, row, mat, row),
        out_specs=(act, act, row, row, mat, row, mat, row, row, row, mat, row, mat, row),
        check_vma=False,
    )
```
